32 devices in a mesh: strip: 8 (over z, y), bucket: 4 (over x, core).
Axes of the slice: x: 2, y: 2, z: 4, core: 2. Of those that a mesh axis runs over, the one named last changes fastest.
Arguments:
- block_input: float32 [32, 56, 56, 384], P('bucket', 'strip'), may hold values from -6 to 6
- cotangent: float32 [32, 56, 56, 384], P('bucket', 'strip'), may hold values from -6 to 6
- window_cols: int32 [4], P('bucket'), may hold values from 1 to 8, as said below
- keep_mask: int32 [32, 2], P('bucket'), may hold values 0 or 1
- owner_list: int32 [13879], replicated, may hold values from 0 to 31, as said below
- master: float32 [20832, 128], P(('strip', 'bucket')), as said below
- first_moment: float32 [20832, 128], P(('strip', 'bucket')), as said below
- second_moment: float32 [20832, 128], P(('strip', 'bucket')), as said below
Outputs:
- block_output: float32 [32, 56, 56, 384], P('bucket', 'strip')
- grad_input: float32 [32, 56, 56, 384], P('bucket', 'strip')
- new_first: float32 [20832, 128], P(('strip', 'bucket'))
- new_second: float32 [20832, 128], P(('strip', 'bucket'))
- new_master: float32 [20832, 128], P(('strip', 'bucket'))
The draws below stay inside these ranges and needn't reach their ends.
Inputs may be any that keep to these rules, and one draw needn't show every extreme that they name: `window_cols`: some bucket is 8 windows wide. `owner_list`: the owner of each packed row, as an index in strip-then-bucket order. No device owns more than 651 rows and some device owns exactly 651. `master`: slot d * 651 + t holds the packed row of device d's t-th owned row in increasing row order; unused slots hold zeros. `first_moment`: same slot layout as master; unused slots are zero. `second_moment`: same slot layout as master; positive in used slots, zero in unused ones.
All inputs are finite; a program needn't handle non-finite values. No bound on the sum of `keep_mask` on one device may be relied on, other than what follows from the above.
Results may differ from the reference program's by a relative error of at most 0.011.
Values may be sent and summed in bfloat16 or wider, within the bound.
A program may use at most 256 MiB of HBM per device.

```python
import math
import jax
import jax.numpy as jnp
from jax import lax

C = 384
HEADS = 12
HD = 32
FF = 1536
WIN = 7
SHIFT = 3
STEP = 10
S_DEV = 8
WCOL = 8
SAMPLES = 32
H = 56
WM = 56
SMALL_ROWS = 39
NROWS = 13879
CAP = 651
N_STRIP = 8
N_BUCKET = 4


def row_edges_drawn():
    first = 3 * C * C // 128
    second = first + C * C // 128
    third = second + C * FF // 128
    fourth = third + FF * C // 128
    fifth = fourth + SMALL_ROWS
    return [first, second, third, fourth, fifth]


def row_kind_drawn(row_ids):
    kind = jnp.zeros(row_ids.shape, jnp.int32)
    for boundary in row_edges_drawn():
        kind = kind + (row_ids >= boundary).astype(jnp.int32)
    return jnp.where(row_ids < 0, 6, kind)


def assign_rows(key):
    device_count = N_STRIP * N_BUCKET
    slot_total = device_count * CAP
    shuffled = jax.random.permutation(jax.random.fold_in(key, 101), slot_total).astype(jnp.int32)
    crowded = jax.random.randint(jax.random.fold_in(key, 102), (), 0, device_count)
    ranking = jnp.where(shuffled // CAP == crowded, 0, slot_total) + jnp.arange(slot_total, dtype=jnp.int32)
    ordered = shuffled[jnp.argsort(ranking)]
    return (ordered[:NROWS] // CAP).astype(jnp.int32)


def slot_sources(owners):
    device_count = N_STRIP * N_BUCKET
    hits = (owners[:, None] == jnp.arange(device_count, dtype=jnp.int32)[None, :]).astype(jnp.int32)
    rank = jnp.sum(jnp.cumsum(hits, axis=0) * hits, axis=1).astype(jnp.int32) - 1
    slots = owners * CAP + rank
    return jnp.full((device_count * CAP,), -1, jnp.int32).at[slots].set(jnp.arange(NROWS, dtype=jnp.int32))


def per_kind(row_ids, amounts):
    kind = row_kind_drawn(row_ids)
    result = jnp.zeros(row_ids.shape, jnp.float32)
    for index, amount in enumerate(amounts):
        result = result + jnp.where(kind == index, amount, 0.0)
    return result


def grad_size(row_ids):
    base = math.sqrt(SAMPLES * H * WM / 2.0)
    return per_kind(row_ids, [0.6 * base, 0.35 * base, 0.3 * base, 0.65 * base, base, 0.25 * base, 0.0])


def draw_window_cols(key, part):
    key = jax.random.fold_in(key, 3)
    widths = jax.random.randint(jax.random.fold_in(key, 1), (N_BUCKET,), 1, WCOL + 1)
    widest = jax.random.randint(jax.random.fold_in(key, 2), (), 0, N_BUCKET)
    return jnp.where(jnp.arange(N_BUCKET) == widest, WCOL, widths).astype(jnp.int32)


def draw_owner_list(key, part):
    return assign_rows(key)


def draw_master(key, part):
    sources = slot_sources(assign_rows(key))
    key = jax.random.fold_in(key, 7)
    noise = jax.random.normal(key, (sources.shape[0], 128), jnp.float32)
    spread = per_kind(sources, [C ** (-0.5), (C // 8) ** (-0.5), C ** (-0.5), FF ** (-0.5), 0.3, 0.5, 0.0])
    offset = (sources - row_edges_drawn()[3])[:, None] * 128 + jnp.arange(128)[None, :]
    base = 5 * C + FF
    gains = (offset >= base) & (offset < base + C) | (offset >= base + 2 * C) & (offset < base + 3 * C)
    gains = gains & (row_kind_drawn(sources) == 4)[:, None]
    return jnp.where(gains, 1.0 + 0.2 * noise, spread[:, None] * noise).astype(jnp.float32)


def draw_first_moment(key, part):
    sources = slot_sources(assign_rows(key))
    key = jax.random.fold_in(key, 8)
    noise = jax.random.normal(key, (sources.shape[0], 128), jnp.float32)
    return (grad_size(sources)[:, None] * noise).astype(jnp.float32)


def draw_second_moment(key, part):
    sources = slot_sources(assign_rows(key))
    key = jax.random.fold_in(key, 9)
    factor = jnp.exp(jax.random.uniform(key, (sources.shape[0], 128), jnp.float32) * math.log(4.0))
    size = grad_size(sources)[:, None]
    return (size * size * factor).astype(jnp.float32)


def set_ends(entries, key, smallest, high):
    longest = entries.shape.index(max(entries.shape))
    spots = []
    for shift in (0, 1):
        where = [jax.random.randint(jax.random.fold_in(key, axis), (), 0, length) for axis, length in enumerate(entries.shape)]
        where[longest] = (where[longest] + shift) % entries.shape[longest]
        spots.append(tuple(where))
    return entries.at[spots[0]].set(smallest).at[spots[1]].set(high)


def shard_levels(stream_key, extent, cuts, low, high):
    def one(dim, blocks):
        draws = jax.random.uniform(jax.random.fold_in(jax.random.fold_in(stream_key, 6), dim), (blocks,), jnp.float32, low / len(cuts), high / len(cuts))
        return jnp.repeat(jnp.exp(draws), extent[dim] // blocks).reshape((-1,) + (1,) * (len(extent) - dim - 1))

    level = one(*cuts[0])
    for cut in cuts[1:]:
        level = level * one(*cut)
    return level


def normal_values(rng, extent, scale, bound, shards=(), held_as=jnp.bfloat16):
    values = scale * jax.random.normal(rng, extent, jnp.float32)
    if shards:
        values = values * shard_levels(rng, extent, shards, -0.22, 0.18)
    return jnp.clip(values, -bound, bound).astype(held_as)


def setup_inputs(seed: int = 0) -> dict:
    arg_keys = jax.random.split(jax.random.key(seed), 9)
    block_input = normal_values(arg_keys[0], (SAMPLES, H, WM, C), 1.0, 6.0, ((0, 4), (1, 8)), jnp.float32)
    cotangent = normal_values(arg_keys[1], (SAMPLES, H, WM, C), 1.0, 6.0, ((0, 4), (1, 8)), jnp.float32)
    window_cols = draw_window_cols(jax.random.fold_in(arg_keys[8], 71), 0)
    keep_mask = set_ends((jax.random.randint(arg_keys[3], (SAMPLES, 2), 0, 5) < 4).astype(jnp.int32), jax.random.fold_in(arg_keys[3], 1), 0, 1)
    owner_list = draw_owner_list(jax.random.fold_in(arg_keys[8], 71), 0)
    master = draw_master(jax.random.fold_in(arg_keys[8], 71), 0)
    first_moment = draw_first_moment(jax.random.fold_in(arg_keys[8], 71), 0)
    second_moment = draw_second_moment(jax.random.fold_in(arg_keys[8], 71), 0)
    return dict(block_input=block_input, cotangent=cotangent, window_cols=window_cols, keep_mask=keep_mask, owner_list=owner_list, master=master, first_moment=first_moment, second_moment=second_moment)


@jax.custom_vjp
def low(v):
    return lax.optimization_barrier(v.astype(jnp.bfloat16)).astype(jnp.float32)

@jax.custom_vjp
def low_back(v):
    return v

def low_keep(v):
    return (low(v), None)

def low_pass(kept, grad):
    return (grad,)

def back_keep(v):
    return (v, None)

def back_low(kept, grad):
    return (low(grad),)
low.defvjp(low_keep, low_pass)
low_back.defvjp(back_keep, back_low)
PRECISE = lax.Precision.HIGHEST
NORM_EPS = 1e-05
KEEP_PROB = 0.8
MASK_FILL = -100.0
BETA_ONE = 0.5
BETA_TWO = 0.5
ADAM_EPS = 1e-08
DECAY = 0.05

def row_edges():
    first = 3 * C * C // 128
    second = first + C * C // 128
    third = second + C * FF // 128
    fourth = third + FF * C // 128
    fifth = fourth + SMALL_ROWS
    return [first, second, third, fourth, fifth]

def row_kind(row_ids):
    kind = jnp.zeros(row_ids.shape, jnp.int32)
    for boundary in row_edges():
        kind = kind + (row_ids >= boundary).astype(jnp.int32)
    return jnp.where(row_ids < 0, 6, kind)

def row_rates(row_ids):
    kind = row_kind(row_ids)
    rates = [2.0 / math.sqrt(C), 2.0 / math.sqrt(C // 8), 2.0 / math.sqrt(C), 2.0 / math.sqrt(FF), 1.0, 1.0, 0.0]
    decays = [DECAY, DECAY, DECAY, DECAY, 0.0, 0.0, 0.0]
    rate_rows = jnp.zeros(row_ids.shape, jnp.float32)
    decay_rows = jnp.zeros(row_ids.shape, jnp.float32)
    for index, amount in enumerate(rates):
        rate_rows = rate_rows + jnp.where(kind == index, amount, 0.0).astype(jnp.float32)
        decay_rows = decay_rows + jnp.where(kind == index, decays[index], 0.0).astype(jnp.float32)
    return (rate_rows, decay_rows)

def slot_rows(owner_list, device_count, capacity):
    hits = (owner_list[:, None] == jnp.arange(device_count, dtype=jnp.int32)[None, :]).astype(jnp.int32)
    rank = lax.optimization_barrier(jnp.sum(jnp.cumsum(hits, axis=0) * hits, axis=1)).astype(jnp.int32) - 1
    return (owner_list * capacity + rank).astype(jnp.int32)

def slot_owner_rows(slots, slot_total):
    return jnp.full((slot_total,), -1, jnp.int32).at[slots].set(jnp.arange(slots.shape[0], dtype=jnp.int32))

def unpack(packed):
    flat = packed.reshape(-1)
    lengths = [C * 3 * C, C * C, C * FF, FF * C, 3 * C, C, FF, C, C, C, C, C]
    pieces = []
    start = 0
    for length in lengths:
        pieces.append(flat[start:start + length])
        start = start + length
    table_start = row_edges()[4] * 128
    table = flat[table_start:table_start + (2 * WIN - 1) ** 2 * HEADS].reshape((2 * WIN - 1) ** 2, HEADS)
    matrices = (pieces[0].reshape(C, 3 * C), pieces[1].reshape(C, C), pieces[2].reshape(C, FF), pieces[3].reshape(FF, C))
    return (matrices, pieces[4:12], table)

def column_map(image_width, offset, columns):
    column_ids = jnp.arange(columns, dtype=jnp.int32)
    return jnp.where(column_ids < image_width, (column_ids + offset) % image_width, column_ids)

def relative_index():
    position = jnp.arange(WIN * WIN, dtype=jnp.int32)
    row_pos = position // WIN
    col_pos = position % WIN
    return ((row_pos[:, None] - row_pos[None, :] + WIN - 1) * (2 * WIN - 1) + col_pos[:, None] - col_pos[None, :] + WIN - 1).reshape(-1)

def shift_labels(global_rows, image_width, height, columns):
    row_part = (global_rows >= height - WIN).astype(jnp.int32) + (global_rows >= height - SHIFT).astype(jnp.int32)
    column_ids = jnp.arange(columns, dtype=jnp.int32)
    col_part = (column_ids >= image_width - WIN).astype(jnp.int32) + (column_ids >= image_width - SHIFT).astype(jnp.int32) + (column_ids >= image_width).astype(jnp.int32)
    return row_part[:, None] * 4 + col_part[None, :]

def layer_norm(values, gain, offset):
    center = values - lax.optimization_barrier(jnp.mean(values, axis=-1, keepdims=True))
    spread = lax.optimization_barrier(jnp.mean(center * center, axis=-1, keepdims=True))
    return center * lax.rsqrt(spread + NORM_EPS) * gain + offset

def matmul(left, right):
    return jnp.dot(left, right, precision=PRECISE, preferred_element_type=jnp.float32)

def windows_of(values):
    row_count, columns, channels = values.shape
    values = values.reshape(row_count // WIN, WIN, columns // WIN, WIN, channels).transpose(0, 2, 1, 3, 4)
    return values.reshape(-1, WIN * WIN, channels)

def image_of(values, row_count, columns):
    channels = values.shape[-1]
    values = values.reshape(row_count // WIN, columns // WIN, WIN, WIN, channels).transpose(0, 2, 1, 3, 4)
    return values.reshape(row_count, columns, channels)

def one_image(params, image, image_width, keep):
    matrices, smalls, table = params
    triple_weight, proj_weight, up_weight, down_weight = matrices
    triple_bias, proj_bias, up_bias, down_bias, gain_one, shift_one, gain_two, shift_two = smalls
    score_scale = HD ** (-0.5)
    column_ids = jnp.arange(WM, dtype=jnp.int32)
    valid = (column_ids < image_width).astype(jnp.float32)
    keep_scale = keep.astype(jnp.float32) / KEEP_PROB
    normed = low_back(low(layer_norm(image, gain_one, shift_one)))
    moved = jnp.take(jnp.roll(normed, -SHIFT, axis=0), column_map(image_width, SHIFT, WM), axis=1)
    windows = windows_of(moved)
    window_count = windows.shape[0]
    triple = low_back(low(matmul(windows.reshape(-1, C), low(triple_weight)) + triple_bias))
    triple = triple.reshape(window_count, WIN * WIN, 3, HEADS, HD)
    query = triple[:, :, 0]
    keys = triple[:, :, 1]
    values = triple[:, :, 2]
    rel_bias = table[relative_index()].reshape(WIN * WIN, WIN * WIN, HEADS).transpose(2, 0, 1)
    labels = shift_labels(jnp.arange(H, dtype=jnp.int32), image_width, H, WM)
    label_windows = windows_of(labels[:, :, None]).reshape(window_count, WIN * WIN)
    masking = jnp.where(label_windows[:, :, None] != label_windows[:, None, :], MASK_FILL, 0.0)
    scores = jnp.einsum('wqhd,wkhd->whqk', query, keys, precision=PRECISE) * score_scale + rel_bias[None] + masking[:, None]
    scores = low_back(scores)
    attention = low(jax.nn.softmax(scores, axis=-1))
    context = jnp.einsum('whqk,wkhd->wqhd', attention, values, precision=PRECISE).reshape(window_count, WIN * WIN, C)
    context = low_back(low(context))
    context = jnp.roll(jnp.take(image_of(context, H, WM), column_map(image_width, -SHIFT, WM), axis=1), SHIFT, axis=0)
    branch = low_back(matmul(context.reshape(-1, C), low(proj_weight)) + proj_bias).reshape(H, WM, C)
    mixed = image + keep_scale[0] * branch
    second = low(layer_norm(mixed, gain_two, shift_two))
    hidden = low_back(matmul(second.reshape(-1, C), low(up_weight)) + up_bias)
    active = low(jax.nn.gelu(hidden, approximate=False))
    branch_two = low_back(matmul(active, low(down_weight)) + down_bias).reshape(H, WM, C)
    return (mixed + keep_scale[1] * branch_two) * valid[None, :, None]

def adamw(weights, first, second, grads, row_ids):
    rate_rows, decay_rows = row_rates(row_ids)
    first = BETA_ONE * first + (1.0 - BETA_ONE) * grads
    second = BETA_TWO * second + (1.0 - BETA_TWO) * grads * grads
    first_hat = first / (1.0 - BETA_ONE ** STEP)
    second_hat = second / (1.0 - BETA_TWO ** STEP)
    weights = weights - rate_rows[:, None] * (first_hat / (jnp.sqrt(second_hat) + ADAM_EPS) + decay_rows[:, None] * weights)
    return (first, second, weights)

def reference(block_input, cotangent, window_cols, keep_mask, owner_list, master, first_moment, second_moment):
    device_count = N_STRIP * N_BUCKET
    slots = slot_rows(owner_list, device_count, CAP)
    sources = slot_owner_rows(slots, device_count * CAP)
    packed = master[slots]
    widths = (jnp.repeat(window_cols, S_DEV) * WIN).astype(jnp.int32)

    def forward(images, packed_rows):
        params = unpack(packed_rows)
        step_fn = jax.checkpoint(lambda item: one_image(params, item[0], item[1], item[2]))
        return lax.map(step_fn, (images, widths, keep_mask))
    output, pull = jax.vjp(forward, block_input, packed)
    grad_images, grad_packed = pull(cotangent)
    filled = sources >= 0
    grads = jnp.where(filled[:, None], grad_packed[jnp.maximum(sources, 0)], 0.0)
    first, second, weights = adamw(master, first_moment, second_moment, grads, sources)
    return (output, grad_images, first, second, weights)
```

```python
import math

import jax
import jax.numpy as jnp
import numpy as np
from jax import lax
from jax.experimental import pallas as pl
from jax.experimental.pallas import tpu as pltpu
from jax.sharding import PartitionSpec as P

C = 384
HEADS = 12
HD = 32
FF = 1536
WIN = 7
SHIFT = 3
STEP = 10
SMALL_ROWS = 39
TABLE_ROWS = 16


PRECISE = lax.Precision.HIGHEST
NORM_EPS = 1e-05
KEEP_PROB = 0.8
MASK_FILL = -100.0
BETA_ONE = 0.5
BETA_TWO = 0.5
ADAM_EPS = 1e-08
DECAY = 0.05


def from_behind(value, axis, by):
    peers = lax.axis_size(axis)
    return lax.ppermute(value, axis, [(i, (i + by) % peers) for i in range(peers)])


def row_edges():
    first = 3 * C * C // 128
    second = first + C * C // 128
    third = second + C * FF // 128
    fourth = third + FF * C // 128
    fifth = fourth + SMALL_ROWS
    return [first, second, third, fourth, fifth]


def row_kind(row_ids):
    kind = jnp.zeros(row_ids.shape, jnp.int32)
    for boundary in row_edges():
        kind = kind + (row_ids >= boundary).astype(jnp.int32)
    return jnp.where(row_ids < 0, 6, kind)


def row_rates(row_ids):
    kind = row_kind(row_ids)
    rates = [
        2.0 / math.sqrt(C),
        2.0 / math.sqrt(C // 8),
        2.0 / math.sqrt(C),
        2.0 / math.sqrt(FF),
        1.0,
        1.0,
        0.0,
    ]
    decays = [DECAY, DECAY, DECAY, DECAY, 0.0, 0.0, 0.0]
    rate_rows = jnp.zeros(row_ids.shape, jnp.float32)
    decay_rows = jnp.zeros(row_ids.shape, jnp.float32)
    for index, amount in enumerate(rates):
        rate_rows = rate_rows + jnp.where(kind == index, amount, 0.0).astype(jnp.float32)
        decay_rows = decay_rows + jnp.where(kind == index, decays[index], 0.0).astype(jnp.float32)
    return (rate_rows, decay_rows)


def slot_rows(owner_list, device_count, capacity):
    hits = (owner_list[:, None] == jnp.arange(device_count, dtype=jnp.int32)[None, :]).astype(
        jnp.int32
    )
    rank = jnp.sum(jnp.cumsum(hits, axis=0) * hits, axis=1) - 1
    return owner_list * capacity + rank


def slot_owner_rows(slots, slot_total):
    return (
        jnp.full((slot_total,), -1, jnp.int32)
        .at[slots]
        .set(jnp.arange(slots.shape[0], dtype=jnp.int32))
    )


def unpack(packed):
    flat = packed.reshape(-1)
    lengths = [C * 3 * C, C * C, C * FF, FF * C, 3 * C, C, FF, C, C, C, C, C]
    pieces = []
    start = 0
    for length in lengths:
        pieces.append(flat[start : start + length])
        start = start + length
    table_start = row_edges()[4] * 128
    table = flat[table_start : table_start + (2 * WIN - 1) ** 2 * HEADS].reshape(
        (2 * WIN - 1) ** 2, HEADS
    )
    matrices = (
        pieces[0].reshape(C, 3 * C),
        pieces[1].reshape(C, C),
        pieces[2].reshape(C, FF),
        pieces[3].reshape(FF, C),
    )
    return (matrices, pieces[4:12], table)


def pack(matrices, smalls, table):
    parts = [piece.reshape(-1) for piece in matrices] + [piece for piece in smalls]
    small_pad = SMALL_ROWS * 128 - (9 * C + FF)
    table_pad = TABLE_ROWS * 128 - (2 * WIN - 1) ** 2 * HEADS
    parts = parts + [
        jnp.zeros((small_pad,), jnp.float32),
        table.reshape(-1),
        jnp.zeros((table_pad,), jnp.float32),
    ]
    return jnp.concatenate(parts).reshape(-1, 128)


GROUPS = 3
GROUP_HEADS = HEADS // GROUPS
CELLS = WIN * 8
LANES = 64
LOG2E = math.log2(math.e)
F32 = jnp.float32
BF16 = jnp.bfloat16


def relative_pairs():
    key = np.arange(CELLS)
    query = np.arange(LANES)
    key_row, key_col = key // 8, key % 8
    query_row, query_col = query // 8, query % 8
    index = (query_row[None, :] - key_row[:, None] + WIN - 1) * (2 * WIN - 1)
    index = index + query_col[None, :] - key_col[:, None] + WIN - 1
    real = (key_col < WIN)[:, None] & ((query_col < WIN) & (query_row < WIN))[None, :]
    return np.where(real, index, -1).astype(np.int32)


def pair_onehot():
    pairs = jnp.asarray(relative_pairs().reshape(-1))
    return (pairs[:, None] == jnp.arange((2 * WIN - 1) ** 2, dtype=jnp.int32)[None, :]).astype(F32)


def attention_bias(table, last_strip):
    spread = lax.dot_general(
        table, pair_onehot(), (((0,), (1,)), ((), ())), precision=PRECISE, preferred_element_type=F32
    ).reshape(HEADS, CELLS, LANES)
    key, query = np.arange(CELLS), np.arange(LANES)
    key_low, query_low = key // 8 >= WIN - SHIFT, query // 8 >= WIN - SHIFT
    key_side, query_side = key % 8 >= WIN - SHIFT, query % 8 >= WIN - SHIFT
    by_row = key_low[:, None] != query_low[None, :]
    by_col = key_side[:, None] != query_side[None, :]
    by_row = jnp.asarray(by_row) & last_strip
    both = jnp.stack([by_row, by_row | jnp.asarray(by_col)])
    masking = jnp.where(both, MASK_FILL, 0.0).astype(F32)
    total = spread[None] + masking[:, None]
    total = jnp.where(jnp.asarray(key % 8 < WIN)[None, None, :, None], total * LOG2E, -1e30)
    total = total.reshape(2, GROUPS, GROUP_HEADS, CELLS, LANES).transpose(0, 1, 3, 2, 4)
    return total.reshape(2, GROUPS, CELLS, GROUP_HEADS * LANES)


def nn(left, right):
    return lax.dot_general(left, right, (((1,), (0,)), ((), ())), preferred_element_type=F32)


def nt(left, right):
    return lax.dot_general(left, right, (((1,), (1,)), ((), ())), preferred_element_type=F32)


def tn(left, right):
    return lax.dot_general(left, right, (((0,), (0,)), ((), ())), preferred_element_type=F32)


def gelu_pair(u):
    x = jnp.abs(u) * (0.3275911 / math.sqrt(2.0)) + 1.0
    t = pl.reciprocal(x)
    gauss = jnp.exp2(u * u * (-0.5 * LOG2E))
    poly = t * (0.5 * 1.061405429) - 0.5 * 1.453152027
    poly = poly * t + 0.5 * 1.421413741
    poly = poly * t - 0.5 * 0.284496736
    poly = poly * t + 0.5 * 0.254829592
    tail = poly * t * gauss
    normal = jnp.where(u >= 0, 1.0 - tail, tail)
    return u * normal, normal + u * gauss * (1.0 / math.sqrt(2.0 * math.pi))


def row_norm(values):
    center = values - jnp.mean(values, axis=-1, keepdims=True)
    scale = lax.rsqrt(jnp.mean(center * center, axis=-1, keepdims=True) + NORM_EPS)
    return center * scale, scale


def norm_pull(grad, normal, scale):
    first = jnp.mean(grad, axis=-1, keepdims=True)
    second = jnp.mean(grad * normal, axis=-1, keepdims=True)
    return scale * (grad - first - normal * second)


def column_sum(values):
    return jnp.sum(values, axis=0, keepdims=True)


def block_kernel(
    cols_ref, keep_ref, x_ref, xh_ref, dy_ref, dyh_ref, bias_ref,
    wq_ref, wp_ref, wu_ref, wd_ref, bq_ref, bp_ref, bu_ref, bd_ref, g1_ref, b1_ref, g2_ref, b2_ref,
    out_ref, outh_ref, gx_ref, gxh_ref,
    gwq_ref, gwp_ref, gwu_ref, gwdt_ref,
    gbq_ref, gbp_ref, gbu_ref, gbd_ref, gg1_ref, gb1_ref, gg2_ref, gb2_ref, gs_ref,
    line, xw, dyw, n1s, zs, qkv, prob, ctx, x1s, n2s, h2s, gfs, ys, gh2s, gctx, gqkv, resw, htr, gtr,
):
    step = pl.program_id(0)
    width = cols_ref[0] * WIN
    keep_one = keep_ref[step, 0]
    keep_two = keep_ref[step, 1]
    wide = xw.shape[0] // CELLS
    columns = x_ref.shape[2]
    slabs = C // 128
    own = WIN - SHIFT

    @pl.when(step == 0)
    def _():
        line[...] = jnp.zeros_like(line)
        qkv[...] = jnp.zeros_like(qkv)
        gctx[...] = jnp.zeros_like(gctx)
        for ref in (gwq_ref, gwp_ref, gwu_ref, gwdt_ref, gbq_ref, gbp_ref, gbu_ref, gbd_ref,
                    gg1_ref, gb1_ref, gg2_ref, gb2_ref, gs_ref):
            ref[...] = jnp.zeros_like(ref)

    def to_windows(main, halo, target):
        for a in range(WIN):
            row = main[0, SHIFT + a] if a < own else halo[0, a - own].astype(F32)
            for s in range(slabs):
                part = row[:, s * 128 : s * 128 + 128]
                line[s, a, 0:columns, :] = part
                line[s, a, pl.ds(width, 8), :] = part[0:8]
        for w in range(wide):
            for a in range(WIN):
                for s in range(slabs):
                    target[w * CELLS + a * 8 : w * CELLS + a * 8 + 8, s * 128 : s * 128 + 128] = line[
                        s, a, w * WIN + SHIFT : w * WIN + SHIFT + 8, :
                    ]

    def from_windows(source, main, halo):
        for w in range(wide):
            for a in range(WIN):
                for s in range(slabs):
                    line[s, a, w * WIN + SHIFT : w * WIN + SHIFT + 8, :] = source[
                        w * CELLS + a * 8 : w * CELLS + a * 8 + 8, s * 128 : s * 128 + 128
                    ]
        kept = lax.broadcasted_iota(jnp.int32, (columns, 128), 0) < width
        front = lax.broadcasted_iota(jnp.int32, (8, 128), 0) < SHIFT
        for a in range(WIN):
            for s in range(slabs):
                wrapped = line[s, a, pl.ds(width, 8), :]
                line[s, a, 0:8, :] = jnp.where(front, wrapped, line[s, a, 0:8, :])
                row = jnp.where(kept, line[s, a, 0:columns, :], 0.0)
                if a < own:
                    main[0, SHIFT + a, :, s * 128 : s * 128 + 128] = row
                else:
                    halo[0, a - own, :, s * 128 : s * 128 + 128] = row.astype(BF16)

    to_windows(x_ref, xh_ref, xw)
    to_windows(dy_ref, dyh_ref, dyw)

    normal, scale_one = row_norm(xw[...])
    n1s[...] = normal
    z = normal * g1_ref[...] + b1_ref[...]
    zs[...] = z.astype(BF16)
    triple = nn(zs[...], wq_ref[...]) + bq_ref[...]
    for w in range(wide):
        qkv[w, 0:CELLS, :] = triple[w * CELLS : w * CELLS + CELLS].astype(BF16)

    lane_head = lax.broadcasted_iota(jnp.int32, (1, 128), 1) // HD
    head_bits = [(lane_head == h).astype(F32).astype(BF16) for h in range(GROUP_HEADS)]

    def stack_of(part):
        return jnp.concatenate([part * head_bits[h] for h in range(GROUP_HEADS)], axis=0)

    def unstack(part):
        total = None
        for h in range(GROUP_HEADS):
            piece = jnp.where(lane_head == h, part[h * LANES : h * LANES + CELLS], 0.0)
            total = piece if total is None else total + piece
        return total

    score_scale = HD ** (-0.5)

    def attend(w, _):
        variant = (w == cols_ref[0] - 1).astype(jnp.int32)
        rows = pl.ds(pl.multiple_of(w * CELLS, 8), CELLS)
        for g in range(GROUPS):
            q = qkv[w, :, g * 128 : g * 128 + 128]
            k = qkv[w, 0:CELLS, C + g * 128 : C + g * 128 + 128]
            v = qkv[w, 0:CELLS, 2 * C + g * 128 : 2 * C + g * 128 + 128]
            s = nt(k, stack_of(q)) * (score_scale * LOG2E) + bias_ref[variant, g]
            e = jnp.exp2(s - jnp.max(s, axis=0, keepdims=True))
            a = e * (1.0 / jnp.sum(e, axis=0, keepdims=True))
            prob[w, g] = a
            ctx[rows, g * 128 : g * 128 + 128] = unstack(tn(a.astype(BF16), v))
        return 0

    lax.fori_loop(0, wide, attend, 0)

    ctx_low = ctx[...].astype(BF16)
    x1 = xw[...] + keep_one * (nn(ctx_low, wp_ref[...]) + bp_ref[...])
    x1s[...] = x1
    normal, scale_two = row_norm(x1)
    n2s[...] = normal
    h2 = (normal * g2_ref[...] + b2_ref[...]).astype(BF16)
    h2s[...] = h2
    htr[...] = h2.astype(F32).T.astype(BF16)

    token = lax.broadcasted_iota(jnp.int32, (wide * CELLS, 1), 0)
    valid = ((token % 8 < WIN) & (token < cols_ref[0] * CELLS)).astype(F32)
    gy = dyw[...] * valid
    gf = (gy * keep_two).astype(BF16)
    gfs[...] = gf
    gbd_ref[...] += column_sum(gf.astype(F32))
    gtr[...] = gf.astype(F32).T.astype(BF16)
    ys[...] = jnp.zeros_like(ys)
    gh2s[...] = jnp.zeros_like(gh2s)

    chunk = 512

    def feed(j, _):
        part = pl.ds(pl.multiple_of(j * chunk, chunk), chunk)
        u = nn(h2s[...], wu_ref[:, part]) + bu_ref[:, part]
        gm = nt(gfs[...], wd_ref[part, :])
        m, slope = gelu_pair(u)
        m = m.astype(BF16)
        gu = (gm * slope).astype(BF16)
        ys[...] += nn(m, wd_ref[part, :])
        gwdt_ref[:, part] += nn(gtr[...], m)
        gwu_ref[:, part] += nn(htr[...], gu)
        gbu_ref[:, part] += column_sum(gu.astype(F32))
        gh2s[...] += nt(gu, wu_ref[:, part])
        return 0

    lax.fori_loop(0, FF // chunk, feed, 0)

    resw[...] = (x1s[...] + keep_two * (ys[...] + bd_ref[...])) * valid
    from_windows(resw, out_ref, outh_ref)

    gh2 = gh2s[...]
    gg2_ref[...] += column_sum(gh2 * n2s[...])
    gb2_ref[...] += column_sum(gh2)
    gx1 = dyw[...] * valid + norm_pull(gh2 * g2_ref[...], n2s[...], scale_two)
    x1s[...] = gx1
    ga = (keep_one * gx1).astype(BF16)
    gbp_ref[...] += column_sum(ga.astype(F32))
    gwp_ref[...] += nn(ctx[...].T.astype(BF16), ga)
    gc = nt(ga, wp_ref[...])
    for w in range(wide):
        gctx[w, 0:CELLS, :] = gc[w * CELLS : w * CELLS + CELLS].astype(BF16)

    def pull(w, _):
        rows = pl.ds(pl.multiple_of(w * CELLS, 8), CELLS)
        for g in range(GROUPS):
            q = qkv[w, :, g * 128 : g * 128 + 128]
            k = qkv[w, 0:CELLS, C + g * 128 : C + g * 128 + 128]
            v = qkv[w, 0:CELLS, 2 * C + g * 128 : 2 * C + g * 128 + 128]
            gstack = stack_of(gctx[w, :, g * 128 : g * 128 + 128])
            a = prob[w, g]
            grad = nt(v, gstack)
            inner = jnp.sum(grad * a, axis=0, keepdims=True)
            gs = (a * (grad - inner)).astype(BF16)
            gs_ref[g] += gs.astype(F32)
            gqkv[rows, g * 128 : g * 128 + 128] = unstack(tn(gs, k)) * score_scale
            gqkv[rows, C + g * 128 : C + g * 128 + 128] = nn(gs, stack_of(q)) * score_scale
            gqkv[rows, 2 * C + g * 128 : 2 * C + g * 128 + 128] = nn(a.astype(BF16), gstack)
        return 0

    lax.fori_loop(0, wide, pull, 0)

    gtriple = gqkv[...].astype(BF16)
    gbq_ref[...] += column_sum(gtriple.astype(F32))
    gwq_ref[...] += nn(zs[...].astype(F32).T.astype(BF16), gtriple)
    gz = nt(gtriple, wq_ref[...]).astype(BF16).astype(F32)
    gg1_ref[...] += column_sum(gz * n1s[...])
    gb1_ref[...] += column_sum(gz)
    resw[...] = x1s[...] + norm_pull(gz * g1_ref[...], n1s[...], scale_one)
    from_windows(resw, gx_ref, gxh_ref)


def run_block(cols, keep, x, xh, dy, dyh, bias, weights, vectors):
    samples, rows, columns, _ = x.shape
    wide = columns // WIN
    tokens = wide * CELLS

    def per_image(array):
        return pl.BlockSpec((1,) + array.shape[1:], lambda i: (i, 0, 0, 0))

    def whole(shape):
        return pl.BlockSpec(shape, lambda i: (0,) * len(shape))

    smem = pl.BlockSpec(memory_space=pltpu.SMEM)
    full = jax.ShapeDtypeStruct(x.shape, F32)
    part = jax.ShapeDtypeStruct(xh.shape, BF16)
    grads = [(C, 3 * C), (C, C), (C, FF), (C, FF), (1, 3 * C), (1, C), (1, FF), (1, C),
             (1, C), (1, C), (1, C), (1, C), (GROUPS, CELLS, GROUP_HEADS * LANES)]
    return pl.pallas_call(
        block_kernel,
        grid=(samples,),
        in_specs=[smem, smem, per_image(x), per_image(xh), per_image(dy), per_image(dyh), whole(bias.shape)]
        + [whole(w.shape) for w in weights] + [whole(v.shape) for v in vectors],
        out_specs=[per_image(x), per_image(xh), per_image(x), per_image(xh)] + [whole(s) for s in grads],
        out_shape=[full, part, full, part] + [jax.ShapeDtypeStruct(s, F32) for s in grads],
        scratch_shapes=[
            pltpu.VMEM((C // 128, WIN, columns + 8, 128), F32),
            pltpu.VMEM((tokens, C), F32),
            pltpu.VMEM((tokens, C), F32),
            pltpu.VMEM((tokens, C), F32),
            pltpu.VMEM((tokens, C), BF16),
            pltpu.VMEM((wide, LANES, 3 * C), BF16),
            pltpu.VMEM((wide, GROUPS, CELLS, GROUP_HEADS * LANES), F32),
            pltpu.VMEM((tokens, C), F32),
            pltpu.VMEM((tokens, C), F32),
            pltpu.VMEM((tokens, C), F32),
            pltpu.VMEM((tokens, C), BF16),
            pltpu.VMEM((tokens, C), BF16),
            pltpu.VMEM((tokens, C), F32),
            pltpu.VMEM((tokens, C), F32),
            pltpu.VMEM((wide, LANES, C), BF16),
            pltpu.VMEM((tokens, 3 * C), F32),
            pltpu.VMEM((tokens, C), F32),
            pltpu.VMEM((C, tokens), BF16),
            pltpu.VMEM((C, tokens), BF16),
        ],
        compiler_params=pltpu.CompilerParams(vmem_limit_bytes=58 * 1024 * 1024),
        name="block",
    )(cols, keep, x, xh, dy, dyh, bias, *weights, *vectors)


def adamw(weights, first, second, grads, row_ids):
    rate_rows, decay_rows = row_rates(row_ids)
    first = BETA_ONE * first + (1.0 - BETA_ONE) * grads
    second = BETA_TWO * second + (1.0 - BETA_TWO) * grads * grads
    first_hat = first / (1.0 - BETA_ONE**STEP)
    second_hat = second / (1.0 - BETA_TWO**STEP)
    weights = weights - rate_rows[:, None] * (
        first_hat / (jnp.sqrt(second_hat) + ADAM_EPS) + decay_rows[:, None] * weights
    )
    return (first, second, weights)


def shards(
    block_input, cotangent, window_cols, keep_mask, owner_list, master, first_moment, second_moment
):
    strips = lax.axis_size("strip")
    device_count = strips * lax.axis_size("bucket")
    capacity = master.shape[0]
    x_halo = from_behind(block_input[:, :SHIFT].astype(BF16), "strip", -1)
    dy_halo = from_behind(cotangent[:, :SHIFT].astype(BF16), "strip", -1)
    slots = slot_rows(owner_list, device_count, capacity)
    sources = slot_owner_rows(slots, device_count * capacity)
    gathered = lax.all_gather(master, ("strip", "bucket"), axis=0, tiled=True)
    matrices, smalls, table = unpack(gathered[slots])
    weights = [matrix.astype(BF16) for matrix in matrices]
    vectors = [small.reshape(1, -1) for small in smalls]
    bias = attention_bias(table, lax.axis_index("strip") == strips - 1)
    keep = keep_mask.astype(F32) / KEEP_PROB
    results = run_block(
        window_cols, keep, block_input, x_halo, cotangent, dy_halo, bias, weights, vectors
    )
    output, output_halo, grad_input, grad_halo = results[:4]
    gwq, gwp, gwu, gwdt = results[4:8]
    smalls_grad = [small.reshape(-1) for small in results[8:16]]
    pair_sums = results[16].reshape(GROUPS, CELLS, GROUP_HEADS, LANES).transpose(0, 2, 1, 3)
    grad_table = lax.dot_general(
        pair_onehot(), pair_sums.reshape(HEADS, -1), (((0,), (1,)), ((), ())),
        precision=PRECISE, preferred_element_type=F32,
    )
    output = output.at[:, :SHIFT].set(from_behind(output_halo, "strip", 1).astype(F32))
    grad_input = grad_input.at[:, :SHIFT].set(from_behind(grad_halo, "strip", 1).astype(F32))
    packed_grad = pack([gwq, gwp, gwu, gwdt.T], smalls_grad, grad_table)
    my_index = lax.axis_index(("strip", "bucket"))
    my_sources = lax.dynamic_slice_in_dim(sources, my_index * capacity, capacity)
    spread_out = jnp.where((sources >= 0)[:, None], packed_grad[jnp.maximum(sources, 0)], 0.0)
    grads = lax.psum_scatter(spread_out, ("strip", "bucket"), scatter_dimension=0, tiled=True)
    first, second_new, new_weights = adamw(master, first_moment, second_moment, grads, my_sources)
    return (output, grad_input, first, second_new, new_weights)


def solution(mesh):
    in_specs = (
        P("bucket", "strip", None, None),
        P("bucket", "strip", None, None),
        P("bucket"),
        P("bucket", None),
        P(),
        P(("strip", "bucket"), None),
        P(("strip", "bucket"), None),
        P(("strip", "bucket"), None),
    )
    out_specs = (
        P("bucket", "strip", None, None),
        P("bucket", "strip", None, None),
        P(("strip", "bucket"), None),
        P(("strip", "bucket"), None),
        P(("strip", "bucket"), None),
    )
    return jax.shard_map(shards, mesh=mesh, in_specs=in_specs, out_specs=out_specs, check_vma=False)
```

```python
import math

import jax
import jax.numpy as jnp
import numpy as np
from jax import lax
from jax.experimental import pallas as pl
from jax.experimental.pallas import tpu as pltpu
from jax.sharding import PartitionSpec as P

C = 384
HEADS = 12
HD = 32
FF = 1536
WIN = 7
SHIFT = 3
STEP = 10
SMALL_ROWS = 39
TABLE_ROWS = 16


PRECISE = lax.Precision.HIGHEST
NORM_EPS = 1e-05
KEEP_PROB = 0.8
MASK_FILL = -100.0
BETA_ONE = 0.5
BETA_TWO = 0.5
ADAM_EPS = 1e-08
DECAY = 0.05


def from_behind(value, axis, by):
    peers = lax.axis_size(axis)
    return lax.ppermute(value, axis, [(i, (i + by) % peers) for i in range(peers)])


def row_edges():
    first = 3 * C * C // 128
    second = first + C * C // 128
    third = second + C * FF // 128
    fourth = third + FF * C // 128
    fifth = fourth + SMALL_ROWS
    return [first, second, third, fourth, fifth]


GROUPS = 3
GROUP_HEADS = HEADS // GROUPS
CELLS = WIN * 8
LANES = 64
LOG2E = math.log2(math.e)
F32 = jnp.float32
BF16 = jnp.bfloat16


def relative_pairs():
    key = np.arange(CELLS)
    query = np.arange(LANES)
    key_row, key_col = key // 8, key % 8
    query_row, query_col = query // 8, query % 8
    index = (query_row[None, :] - key_row[:, None] + WIN - 1) * (2 * WIN - 1)
    index = index + query_col[None, :] - key_col[:, None] + WIN - 1
    real = (key_col < WIN)[:, None] & ((query_col < WIN) & (query_row < WIN))[None, :]
    return np.where(real, index, -1).astype(np.int32)


def pair_onehot():
    pairs = jnp.asarray(relative_pairs().reshape(-1))
    return (pairs[:, None] == jnp.arange((2 * WIN - 1) ** 2, dtype=jnp.int32)[None, :]).astype(F32)


def attention_bias(table, last_strip):
    spread = lax.dot_general(
        table, pair_onehot(), (((0,), (1,)), ((), ())), precision=PRECISE, preferred_element_type=F32
    ).reshape(HEADS, CELLS, LANES)
    key, query = np.arange(CELLS), np.arange(LANES)
    key_low, query_low = key // 8 >= WIN - SHIFT, query // 8 >= WIN - SHIFT
    key_side, query_side = key % 8 >= WIN - SHIFT, query % 8 >= WIN - SHIFT
    by_row = key_low[:, None] != query_low[None, :]
    by_col = key_side[:, None] != query_side[None, :]
    by_row = jnp.asarray(by_row) & last_strip
    both = jnp.stack([by_row, by_row | jnp.asarray(by_col)])
    masking = jnp.where(both, MASK_FILL, 0.0).astype(F32)
    total = spread[None] + masking[:, None]
    total = jnp.where(jnp.asarray(key % 8 < WIN)[None, None, :, None], total * LOG2E, -1e30)
    total = total.reshape(2, GROUPS, GROUP_HEADS, CELLS, LANES).transpose(0, 1, 3, 2, 4)
    return total.reshape(2, GROUPS, CELLS, GROUP_HEADS * LANES)


def nn(left, right):
    return lax.dot_general(left, right, (((1,), (0,)), ((), ())), preferred_element_type=F32)


def nt(left, right):
    return lax.dot_general(left, right, (((1,), (1,)), ((), ())), preferred_element_type=F32)


def tn(left, right):
    return lax.dot_general(left, right, (((0,), (0,)), ((), ())), preferred_element_type=F32)


def gelu_pair(u):
    x = jnp.abs(u) * (0.3275911 / math.sqrt(2.0)) + 1.0
    t = pl.reciprocal(x)
    gauss = jnp.exp2(u * u * (-0.5 * LOG2E))
    poly = t * (0.5 * 1.061405429) - 0.5 * 1.453152027
    poly = poly * t + 0.5 * 1.421413741
    poly = poly * t - 0.5 * 0.284496736
    poly = poly * t + 0.5 * 0.254829592
    tail = poly * t * gauss
    normal = jnp.where(u >= 0, 1.0 - tail, tail)
    return u * normal, normal + u * gauss * (1.0 / math.sqrt(2.0 * math.pi))


def row_norm(values):
    center = values - jnp.mean(values, axis=-1, keepdims=True)
    scale = lax.rsqrt(jnp.mean(center * center, axis=-1, keepdims=True) + NORM_EPS)
    return center * scale, scale


def norm_pull(grad, normal, scale):
    first = jnp.mean(grad, axis=-1, keepdims=True)
    second = jnp.mean(grad * normal, axis=-1, keepdims=True)
    return scale * (grad - first - normal * second)


def column_sum(values):
    return jnp.sum(values, axis=0, keepdims=True)


def block_kernel(
    cols_ref, keep_ref, x_ref, xh_ref, dy_ref, dyh_ref, bias_ref,
    wire_ref,
    out_ref, outh_ref, gx_ref, gxh_ref, gwire_ref, gs_ref,
    wq_ref, wp_ref, wu_ref, wd_ref, bq_ref, bp_ref, bu_ref, bd_ref, g1_ref, b1_ref, g2_ref, b2_ref,
    gwq_ref, gwp_ref, gwu_ref, gwdt_ref,
    gbq_ref, gbp_ref, gbu_ref, gbd_ref, gg1_ref, gb1_ref, gg2_ref, gb2_ref,
    line, xw, dyw, n1s, zs, qkv, prob, ctx, x1s, n2s, h2s, gfs, ys, gh2s, gctx, gqkv, resw, htr, gtr,
):
    step = pl.program_id(0)
    width = cols_ref[0] * WIN
    keep_one = keep_ref[step, 0]
    keep_two = keep_ref[step, 1]
    wide = xw.shape[0] // CELLS
    columns = x_ref.shape[2]
    slabs = C // 128
    own = WIN - SHIFT

    matrices = (wq_ref, wp_ref, wu_ref, wd_ref)
    vectors = (bq_ref, bp_ref, bu_ref, bd_ref, g1_ref, b1_ref, g2_ref, b2_ref)
    vector_grads = (gbq_ref, gbp_ref, gbu_ref, gbd_ref, gg1_ref, gb1_ref, gg2_ref, gb2_ref)

    @pl.when(step == 0)
    def _():
        for ref, (first, slabs, rows) in zip(matrices, slab_plan()):
            for j in range(slabs):
                ref[:, j * 128 : j * 128 + 128] = wire_ref[first + j * rows : first + (j + 1) * rows, :]
        small = jnp.zeros((SMALL_SPAN, 128), F32)
        for i in range(3):
            first = SMALL_START + i * SMALL_SPAN
            small = small + wire_ref[first : first + SMALL_SPAN, :].astype(F32)
        row = 0
        for ref in vectors:
            for j in range(ref.shape[1] // 128):
                ref[:, j * 128 : j * 128 + 128] = small[row : row + 1]
                row += 1
        line[...] = jnp.zeros_like(line)
        qkv[...] = jnp.zeros_like(qkv)
        gctx[...] = jnp.zeros_like(gctx)
        for ref in (gwq_ref, gwp_ref, gwu_ref, gwdt_ref, gs_ref) + vector_grads:
            ref[...] = jnp.zeros_like(ref)

    def to_windows(main, halo, target):
        for a in range(WIN):
            row = main[0, SHIFT + a] if a < own else halo[0, a - own].astype(F32)
            for s in range(slabs):
                part = row[:, s * 128 : s * 128 + 128]
                line[s, a, 0:columns, :] = part
                line[s, a, pl.ds(width, 8), :] = part[0:8]
        for w in range(wide):
            for a in range(WIN):
                for s in range(slabs):
                    target[w * CELLS + a * 8 : w * CELLS + a * 8 + 8, s * 128 : s * 128 + 128] = line[
                        s, a, w * WIN + SHIFT : w * WIN + SHIFT + 8, :
                    ]

    def from_windows(source, main, halo):
        for w in range(wide):
            for a in range(WIN):
                for s in range(slabs):
                    line[s, a, w * WIN + SHIFT : w * WIN + SHIFT + 8, :] = source[
                        w * CELLS + a * 8 : w * CELLS + a * 8 + 8, s * 128 : s * 128 + 128
                    ]
        kept = lax.broadcasted_iota(jnp.int32, (columns, 128), 0) < width
        front = lax.broadcasted_iota(jnp.int32, (8, 128), 0) < SHIFT
        for a in range(WIN):
            for s in range(slabs):
                wrapped = line[s, a, pl.ds(width, 8), :]
                line[s, a, 0:8, :] = jnp.where(front, wrapped, line[s, a, 0:8, :])
                row = jnp.where(kept, line[s, a, 0:columns, :], 0.0)
                if a < own:
                    main[0, SHIFT + a, :, s * 128 : s * 128 + 128] = row
                else:
                    halo[0, a - own, :, s * 128 : s * 128 + 128] = row.astype(BF16)

    to_windows(x_ref, xh_ref, xw)
    to_windows(dy_ref, dyh_ref, dyw)

    normal, scale_one = row_norm(xw[...])
    n1s[...] = normal
    z = normal * g1_ref[...] + b1_ref[...]
    zs[...] = z.astype(BF16)
    triple = nn(zs[...], wq_ref[...]) + bq_ref[...]
    for w in range(wide):
        qkv[w, 0:CELLS, :] = triple[w * CELLS : w * CELLS + CELLS].astype(BF16)

    lane_head = lax.broadcasted_iota(jnp.int32, (1, 128), 1) // HD
    head_bits = [(lane_head == h).astype(F32).astype(BF16) for h in range(GROUP_HEADS)]

    def stack_of(part):
        return jnp.concatenate([part * head_bits[h] for h in range(GROUP_HEADS)], axis=0)

    def unstack(part):
        total = None
        for h in range(GROUP_HEADS):
            piece = jnp.where(lane_head == h, part[h * LANES : h * LANES + CELLS], 0.0)
            total = piece if total is None else total + piece
        return total

    score_scale = HD ** (-0.5)

    def attend(w, _):
        variant = (w == cols_ref[0] - 1).astype(jnp.int32)
        rows = pl.ds(pl.multiple_of(w * CELLS, 8), CELLS)
        for g in range(GROUPS):
            q = qkv[w, :, g * 128 : g * 128 + 128]
            k = qkv[w, 0:CELLS, C + g * 128 : C + g * 128 + 128]
            v = qkv[w, 0:CELLS, 2 * C + g * 128 : 2 * C + g * 128 + 128]
            s = nt(k, stack_of(q)) * (score_scale * LOG2E) + bias_ref[variant, g]
            e = jnp.exp2(s - jnp.max(s, axis=0, keepdims=True))
            a = e * (1.0 / jnp.sum(e, axis=0, keepdims=True))
            prob[w, g] = a
            ctx[rows, g * 128 : g * 128 + 128] = unstack(tn(a.astype(BF16), v))
        return 0

    lax.fori_loop(0, wide, attend, 0)

    ctx_low = ctx[...].astype(BF16)
    x1 = xw[...] + keep_one * (nn(ctx_low, wp_ref[...]) + bp_ref[...])
    x1s[...] = x1
    normal, scale_two = row_norm(x1)
    n2s[...] = normal
    h2 = (normal * g2_ref[...] + b2_ref[...]).astype(BF16)
    h2s[...] = h2
    htr[...] = h2.astype(F32).T.astype(BF16)

    token = lax.broadcasted_iota(jnp.int32, (wide * CELLS, 1), 0)
    valid = ((token % 8 < WIN) & (token < cols_ref[0] * CELLS)).astype(F32)
    gy = dyw[...] * valid
    gf = (gy * keep_two).astype(BF16)
    gfs[...] = gf
    gbd_ref[...] += column_sum(gf.astype(F32))
    gtr[...] = gf.astype(F32).T.astype(BF16)
    ys[...] = jnp.zeros_like(ys)
    gh2s[...] = jnp.zeros_like(gh2s)

    chunk = 512

    def feed(j, _):
        part = pl.ds(pl.multiple_of(j * chunk, chunk), chunk)
        u = nn(h2s[...], wu_ref[:, part]) + bu_ref[:, part]
        gm = nt(gfs[...], wd_ref[part, :])
        m, slope = gelu_pair(u)
        m = m.astype(BF16)
        gu = (gm * slope).astype(BF16)
        ys[...] += nn(m, wd_ref[part, :])
        gwdt_ref[:, part] += nn(gtr[...], m)
        gwu_ref[:, part] += nn(htr[...], gu)
        gbu_ref[:, part] += column_sum(gu.astype(F32))
        gh2s[...] += nt(gu, wu_ref[:, part])
        return 0

    lax.fori_loop(0, FF // chunk, feed, 0)

    resw[...] = (x1s[...] + keep_two * (ys[...] + bd_ref[...])) * valid
    from_windows(resw, out_ref, outh_ref)

    gh2 = gh2s[...]
    gg2_ref[...] += column_sum(gh2 * n2s[...])
    gb2_ref[...] += column_sum(gh2)
    gx1 = dyw[...] * valid + norm_pull(gh2 * g2_ref[...], n2s[...], scale_two)
    x1s[...] = gx1
    ga = (keep_one * gx1).astype(BF16)
    gbp_ref[...] += column_sum(ga.astype(F32))
    gwp_ref[...] += nn(ctx[...].T.astype(BF16), ga)
    gc = nt(ga, wp_ref[...])
    for w in range(wide):
        gctx[w, 0:CELLS, :] = gc[w * CELLS : w * CELLS + CELLS].astype(BF16)

    def pull(w, _):
        rows = pl.ds(pl.multiple_of(w * CELLS, 8), CELLS)
        for g in range(GROUPS):
            q = qkv[w, :, g * 128 : g * 128 + 128]
            k = qkv[w, 0:CELLS, C + g * 128 : C + g * 128 + 128]
            v = qkv[w, 0:CELLS, 2 * C + g * 128 : 2 * C + g * 128 + 128]
            gstack = stack_of(gctx[w, :, g * 128 : g * 128 + 128])
            a = prob[w, g]
            grad = nt(v, gstack)
            inner = jnp.sum(grad * a, axis=0, keepdims=True)
            gs = (a * (grad - inner)).astype(BF16)
            gs_ref[g] += gs.astype(F32)
            gqkv[rows, g * 128 : g * 128 + 128] = unstack(tn(gs, k)) * score_scale
            gqkv[rows, C + g * 128 : C + g * 128 + 128] = nn(gs, stack_of(q)) * score_scale
            gqkv[rows, 2 * C + g * 128 : 2 * C + g * 128 + 128] = nn(a.astype(BF16), gstack)
        return 0

    lax.fori_loop(0, wide, pull, 0)

    gtriple = gqkv[...].astype(BF16)
    gbq_ref[...] += column_sum(gtriple.astype(F32))
    gwq_ref[...] += nn(zs[...].astype(F32).T.astype(BF16), gtriple)
    gz = nt(gtriple, wq_ref[...]).astype(BF16).astype(F32)
    gg1_ref[...] += column_sum(gz * n1s[...])
    gb1_ref[...] += column_sum(gz)
    resw[...] = x1s[...] + norm_pull(gz * g1_ref[...], n1s[...], scale_one)
    from_windows(resw, gx_ref, gxh_ref)

    @pl.when(step == pl.num_programs(0) - 1)
    def _():
        for grad, (first, slabs, rows) in zip((gwq_ref, gwp_ref, gwu_ref), slab_plan()):
            for j in range(slabs):
                gwire_ref[first + j * rows : first + (j + 1) * rows, :] = grad[:, j * 128 : j * 128 + 128].astype(BF16)
        first, slabs, rows = slab_plan()[3]
        for j in range(slabs):
            gwire_ref[first + j * rows : first + (j + 1) * rows, :] = gwdt_ref[j * 128 : j * 128 + 128, :].T.astype(BF16)
        pieces = [ref[:, j * 128 : j * 128 + 128] for ref in vector_grads for j in range(ref.shape[1] // 128)]
        spare = gwire_ref.shape[0] - SMALL_START - len(pieces)
        pieces.append(jnp.zeros((spare, 128), F32))
        gwire_ref[SMALL_START:, :] = jnp.concatenate(pieces, axis=0).astype(BF16)


def run_block(cols, keep, x, xh, dy, dyh, bias, wire):
    samples, rows, columns, _ = x.shape
    wide = columns // WIN
    tokens = wide * CELLS

    def per_image(array):
        return pl.BlockSpec((1,) + array.shape[1:], lambda i: (i, 0, 0, 0))

    def whole(shape):
        return pl.BlockSpec(shape, lambda i: (0,) * len(shape))

    smem = pl.BlockSpec(memory_space=pltpu.SMEM)
    full = jax.ShapeDtypeStruct(x.shape, F32)
    part = jax.ShapeDtypeStruct(xh.shape, BF16)
    sums = (GROUPS, CELLS, GROUP_HEADS * LANES)
    vectors = [3 * C, C, FF, C, C, C, C, C]
    return pl.pallas_call(
        block_kernel,
        grid=(samples,),
        in_specs=[smem, smem, per_image(x), per_image(xh), per_image(dy), per_image(dyh), whole(bias.shape)]
        + [whole(wire.shape)],
        out_specs=[per_image(x), per_image(xh), per_image(x), per_image(xh), whole(wire.shape), whole(sums)],
        out_shape=[full, part, full, part, jax.ShapeDtypeStruct(wire.shape, BF16), jax.ShapeDtypeStruct(sums, F32)],
        scratch_shapes=[pltpu.VMEM(s, BF16) for s in ((C, 3 * C), (C, C), (C, FF), (FF, C))]
        + [pltpu.VMEM((1, size), F32) for size in vectors]
        + [pltpu.VMEM(s, F32) for s in ((C, 3 * C), (C, C), (C, FF), (C, FF))]
        + [pltpu.VMEM((1, size), F32) for size in vectors]
        + [
            pltpu.VMEM((C // 128, WIN, columns + 8, 128), F32),
            pltpu.VMEM((tokens, C), F32),
            pltpu.VMEM((tokens, C), F32),
            pltpu.VMEM((tokens, C), F32),
            pltpu.VMEM((tokens, C), BF16),
            pltpu.VMEM((wide, LANES, 3 * C), BF16),
            pltpu.VMEM((wide, GROUPS, CELLS, GROUP_HEADS * LANES), F32),
            pltpu.VMEM((tokens, C), F32),
            pltpu.VMEM((tokens, C), F32),
            pltpu.VMEM((tokens, C), F32),
            pltpu.VMEM((tokens, C), BF16),
            pltpu.VMEM((tokens, C), BF16),
            pltpu.VMEM((tokens, C), F32),
            pltpu.VMEM((tokens, C), F32),
            pltpu.VMEM((wide, LANES, C), BF16),
            pltpu.VMEM((tokens, 3 * C), F32),
            pltpu.VMEM((tokens, C), F32),
            pltpu.VMEM((C, tokens), BF16),
            pltpu.VMEM((C, tokens), BF16),
        ],
        compiler_params=pltpu.CompilerParams(vmem_limit_bytes=58 * 1024 * 1024),
        name="block",
    )(cols, keep, x, xh, dy, dyh, bias, wire)


SMALL_START = 3 * C * C // 128 + C * C // 128 + 2 * C * FF // 128
SMALL_SPAN = 64
WIRE_ROWS = SMALL_START + 3 * SMALL_SPAN


def slab_plan():
    return [
        (0, 3 * C // 128, C),
        (3 * C * C // 128, C // 128, C),
        (4 * C * C // 128, FF // 128, C),
        (4 * C * C // 128 + C * FF // 128, C // 128, FF),
    ]


def wire_rows(device_count):
    unit = 2 * device_count * 16
    return -(-WIRE_ROWS // unit) * unit


def split_three(values):
    high = values.astype(BF16)
    rest = values - high.astype(F32)
    middle = rest.astype(BF16)
    return high, middle, (rest - middle.astype(F32)).astype(BF16)


def dispatch_kernel(me_ref, owner_ref, master_ref, out_ref, rank_ref, start_ref, padded, packed, start_s, sem):
    blocks = owner_ref.shape[0]
    capacity = master_ref.shape[0]
    mine = (owner_ref[...] == me_ref[0]).astype(F32)
    low = mine.astype(BF16)
    row = lax.broadcasted_iota(jnp.int32, (128, 128), 0)
    col = lax.broadcasted_iota(jnp.int32, (128, 128), 1)
    within = nn(low, (row <= col).astype(F32).astype(BF16))
    sums = nn(low, jnp.ones((128, 128), BF16))
    below = lax.broadcasted_iota(jnp.int32, (blocks, blocks), 1) < lax.broadcasted_iota(jnp.int32, (blocks, blocks), 0)
    start = nn(below.astype(F32).astype(BF16), sums.astype(BF16))
    rank_ref[...] = jnp.where(mine > 0, within - 1.0, -1.0)
    start_ref[...] = start.astype(jnp.int32)
    copy = pltpu.make_async_copy(start_ref, start_s, sem)
    copy.start()
    padded[...] = jnp.zeros_like(padded)
    padded[0:capacity, :] = master_ref[...]
    out_ref[...] = jnp.zeros_like(out_ref)
    copy.wait()
    slot = row.astype(F32)

    def block(b, _):
        hot = (slot == rank_ref[pl.ds(b, 1), :]).astype(F32).astype(BF16)
        rows = padded[pl.ds(start_s[b, 0], 128), :].astype(BF16)
        packed[pl.ds(pl.multiple_of(b * 128, 128), 128), :] = tn(hot, rows)
        return 0

    small = SMALL_START // 128
    lax.fori_loop(0, small, block, 0, unroll=4)
    hot = (slot == rank_ref[small : small + 1, :]).astype(F32).astype(BF16)
    for i, piece in enumerate(split_three(padded[pl.ds(start_s[small, 0], 128), :])):
        first = SMALL_START + i * SMALL_SPAN
        out_ref[first : first + SMALL_SPAN, :] = tn(hot, piece)[0:SMALL_SPAN].astype(BF16)
    for first, slabs, rows in slab_plan():
        for j in range(slabs):
            out_ref[first + j * rows : first + (j + 1) * rows, :] = packed[
                pl.ds(first + j, rows, stride=slabs), :
            ].astype(BF16)


def run_dispatch(me, owners, master, wire):
    blocks = owners.shape[0]
    vmem = pl.BlockSpec(memory_space=pltpu.VMEM)
    return pl.pallas_call(
        dispatch_kernel,
        in_specs=[pl.BlockSpec(memory_space=pltpu.SMEM), vmem, vmem],
        out_specs=[vmem] * 3,
        out_shape=[
            jax.ShapeDtypeStruct((wire, 128), BF16),
            jax.ShapeDtypeStruct((blocks, 128), F32),
            jax.ShapeDtypeStruct((blocks, 128), jnp.int32),
        ],
        scratch_shapes=[
            pltpu.VMEM((-(-(master.shape[0] + 128) // 8) * 8, 128), F32),
            pltpu.VMEM((SMALL_START, 128), F32),
            pltpu.SMEM((blocks, 128), jnp.int32),
            pltpu.SemaphoreType.DMA,
        ],
        compiler_params=pltpu.CompilerParams(vmem_limit_bytes=40 * 1024 * 1024),
        name="dispatch",
    )(me, owners, master)


def collect_kernel(start_ref, rank_ref, grad_ref, master_ref, first_ref, second_ref,
                   first_out, second_out, master_out, packed, total):
    capacity = master_ref.shape[0]
    total[...] = jnp.zeros_like(total)
    for first, slabs, rows in slab_plan():
        for j in range(slabs):
            packed[pl.ds(first + j, rows, stride=slabs), :] = grad_ref[
                first + j * rows : first + (j + 1) * rows, :
            ].astype(F32)
    packed[SMALL_START : SMALL_START + SMALL_SPAN, :] = grad_ref[SMALL_START : SMALL_START + SMALL_SPAN, :].astype(F32)
    packed[SMALL_START + SMALL_SPAN : SMALL_START + 128, :] = jnp.zeros((128 - SMALL_SPAN, 128), F32)
    slot = lax.broadcasted_iota(jnp.int32, (128, 128), 0).astype(F32)

    def block(b, _):
        hot = (slot == rank_ref[pl.ds(b, 1), :]).astype(F32).astype(BF16)
        part = nn(hot, packed[pl.ds(pl.multiple_of(b * 128, 128), 128), :].astype(BF16))
        where = pl.ds(start_ref[b, 0], 128)
        total[where, :] = total[where, :] + part
        return 0

    lax.fori_loop(0, SMALL_START // 128 + 1, block, 0)
    slots = lax.broadcasted_iota(jnp.int32, (capacity, 1), 0)
    edges = [edge // 128 for edge in row_edges()[:4]] + [SMALL_START // 128 + 1]
    rates = [2.0 / math.sqrt(C), 2.0 / math.sqrt(C // 8), 2.0 / math.sqrt(C), 2.0 / math.sqrt(FF), 1.0, 0.0]
    rate = jnp.full((capacity, 1), rates[0], F32)
    for edge, amount in zip(edges, rates[1:]):
        rate = jnp.where(slots >= start_ref[edge, 0], amount, rate)
    decay = jnp.where(slots < start_ref[edges[3], 0], DECAY, 0.0)
    grads = total[0:capacity, :]
    weights = master_ref[...]
    first = BETA_ONE * first_ref[...] + (1.0 - BETA_ONE) * grads
    second = BETA_TWO * second_ref[...] + (1.0 - BETA_TWO) * grads * grads
    first_out[...] = first
    second_out[...] = second
    first_hat = first / (1.0 - BETA_ONE**STEP)
    second_hat = second / (1.0 - BETA_TWO**STEP)
    master_out[...] = weights - rate * (first_hat / (jnp.sqrt(second_hat) + ADAM_EPS) + decay * weights)


def run_collect(starts, ranks, grads, master, first, second):
    vmem = pl.BlockSpec(memory_space=pltpu.VMEM)
    return pl.pallas_call(
        collect_kernel,
        in_specs=[pl.BlockSpec(memory_space=pltpu.SMEM)] + [vmem] * 5,
        out_specs=[vmem] * 3,
        out_shape=[jax.ShapeDtypeStruct(master.shape, F32)] * 3,
        scratch_shapes=[
            pltpu.VMEM((SMALL_START + 128, 128), F32),
            pltpu.VMEM((-(-(master.shape[0] + 128) // 8) * 8, 128), F32),
        ],
        compiler_params=pltpu.CompilerParams(vmem_limit_bytes=40 * 1024 * 1024),
        name="collect",
    )(starts, ranks, grads, master, first, second)


def all_reduce_kernel(strips, buckets, in_ref, out_ref, core_in, core_sum, in_one, sum_one, in_two, sum_two,
                      in_three, send_sems, recv_sems):
    strip, bucket = lax.axis_index("strip"), lax.axis_index("bucket")
    sizes = {"z": strips // 2, "y": 2, "x": buckets // 2, "core": 2}
    mine = {"z": strip // 2, "y": strip % 2, "x": bucket // 2, "core": bucket % 2}

    def device(axis, index):
        place = dict(mine)
        place[axis] = index
        return (place["z"] * 2 + place["y"], place["x"] * 2 + place["core"])

    def peer(axis, offset):
        return lax.rem(mine[axis] + offset, sizes[axis])

    barrier = pltpu.get_barrier_semaphore()
    greeted = 0
    for axis, size in sizes.items():
        for offset in range(1, size):
            pl.semaphore_signal(barrier, inc=1, device_id=device(axis, peer(axis, offset)),
                                device_id_type=pl.DeviceIdType.MESH)
            greeted += 1
    pl.semaphore_wait(barrier, greeted)

    used = [0]

    def send(source, target, axis, offset):
        at = used[0]
        used[0] += 1
        copy = pltpu.make_async_remote_copy(
            src_ref=source, dst_ref=target, send_sem=send_sems.at[at], recv_sem=recv_sems.at[at],
            device_id=device(axis, peer(axis, offset)), device_id_type=pl.DeviceIdType.MESH,
        )
        copy.start()
        return copy

    rows = in_ref.shape[0]
    quarter = rows // 4
    orders = [("x", "y"), ("y", "x")]
    started = []

    def at(start, length):
        return pl.ds(pl.multiple_of(start, 16), length)

    flight = []
    for p in range(2):
        other = (1 - mine["core"]) * 2 * quarter + p * quarter
        flight.append(send(in_ref.at[at(other, quarter)], core_in.at[p], "core", 1))
    stage = []
    for p in range(2):
        flight[p].wait()
        own = mine["core"] * 2 * quarter + p * quarter
        core_sum[p] = in_ref[at(own, quarter), :] + core_in[p]
        stage.append(core_sum.at[p])

    def scatter(level, length, axis_of, inboxes, sums):
        flights = []
        for p in range(2):
            axis = axis_of(p)
            piece = length // sizes[axis]
            group = []
            for offset in range(1, sizes[axis]):
                source = stage[p].at[at(peer(axis, offset) * piece, piece)]
                group.append(send(source, inboxes.at[p, pl.ds((offset - 1) * piece, piece)], axis, offset))
            flights.append(group)
        for p in range(2):
            axis = axis_of(p)
            piece = length // sizes[axis]
            for copy in flights[p]:
                copy.wait()
            value = stage[p][at(mine[axis] * piece, piece), :].astype(F32)
            for offset in range(1, sizes[axis]):
                value = value + inboxes[p, (offset - 1) * piece : offset * piece, :].astype(F32)
            if sums is None:
                base = mine["core"] * 2 * quarter + p * quarter + spans(p)[-1][0]
                out_ref[at(base, piece), :] = value.astype(BF16)
            else:
                sums[p, 0:piece, :] = value.astype(BF16)
                stage[p] = sums.at[p]

    def spans(p):
        result = []
        start, length = 0, quarter
        for axis in orders[p] + ("z",):
            length = length // sizes[axis]
            start = start + mine[axis] * length
            result.append((start, length))
        return result

    scatter(1, quarter, lambda p: orders[p][0], in_one, sum_one)
    lengths = [quarter // sizes[orders[p][0]] for p in range(2)]

    def scatter_two():
        flights = []
        for p in range(2):
            axis = orders[p][1]
            piece = lengths[p] // sizes[axis]
            group = []
            for offset in range(1, sizes[axis]):
                source = stage[p].at[at(peer(axis, offset) * piece, piece)]
                group.append(send(source, in_two.at[p, pl.ds((offset - 1) * piece, piece)], axis, offset))
            flights.append(group)
        for p in range(2):
            axis = orders[p][1]
            piece = lengths[p] // sizes[axis]
            for copy in flights[p]:
                copy.wait()
            value = stage[p][at(mine[axis] * piece, piece), :].astype(F32)
            for offset in range(1, sizes[axis]):
                value = value + in_two[p, (offset - 1) * piece : offset * piece, :].astype(F32)
            sum_two[p, 0:piece, :] = value.astype(BF16)
            stage[p] = sum_two.at[p]

    scatter_two()
    eighth = quarter // (sizes["x"] * sizes["y"])
    scatter(3, eighth, lambda p: "z", in_three, None)

    for level in (2, 1, 0):
        flights = []
        for p in range(2):
            axis = (orders[p] + ("z",))[level]
            start, length = spans(p)[level]
            region = out_ref.at[at(mine["core"] * 2 * quarter + p * quarter + start, length)]
            flights.append([send(region, region, axis, offset) for offset in range(1, sizes[axis])])
        for group in flights:
            for copy in group:
                copy.wait()
    flights = []
    for p in range(2):
        region = out_ref.at[at(mine["core"] * 2 * quarter + p * quarter, quarter)]
        flights.append(send(region, region, "core", 1))
    for copy in flights:
        copy.wait()


def all_reduce(values, strips, buckets):
    rows = values.shape[0]
    quarter = rows // 4
    x, y, z = buckets // 2, 2, strips // 2
    vmem = pl.BlockSpec(memory_space=pltpu.VMEM)
    copies = 2 * (2 * 1 + 2 * (x - 1 + y - 1 + z - 1))
    small = min(x, y)
    return pl.pallas_call(
        lambda *refs: all_reduce_kernel(strips, buckets, *refs),
        in_specs=[vmem],
        out_specs=vmem,
        out_shape=jax.ShapeDtypeStruct(values.shape, BF16),
        scratch_shapes=[
            pltpu.VMEM((2, quarter, 128), BF16),
            pltpu.VMEM((2, quarter, 128), BF16),
            pltpu.VMEM((2, quarter, 128), BF16),
            pltpu.VMEM((2, quarter // small, 128), BF16),
            pltpu.VMEM((2, quarter // small, 128), BF16),
            pltpu.VMEM((2, quarter // (x * y), 128), BF16),
            pltpu.VMEM((2, quarter // (x * y), 128), BF16),
            pltpu.SemaphoreType.DMA((copies,)),
            pltpu.SemaphoreType.DMA((copies,)),
        ],
        compiler_params=pltpu.CompilerParams(
            vmem_limit_bytes=40 * 1024 * 1024, collective_id=0, has_side_effects=True
        ),
        name="all_reduce",
    )(values)


def shards(
    block_input, cotangent, window_cols, keep_mask, owner_list, master, first_moment, second_moment
):
    strips = lax.axis_size("strip")
    buckets = lax.axis_size("bucket")
    wire_total = wire_rows(strips * buckets)
    x_halo = from_behind(block_input[:, :SHIFT].astype(BF16), "strip", -1)
    dy_halo = from_behind(cotangent[:, :SHIFT].astype(BF16), "strip", -1)
    my_index = lax.axis_index(("strip", "bucket")).astype(jnp.int32).reshape(1)
    blocks = -(-(SMALL_START // 128 + 2) // 8) * 8
    owners = jnp.pad(owner_list, (0, blocks * 128 - owner_list.shape[0]), constant_values=-1).reshape(blocks, 128)
    sparse, ranks, starts = run_dispatch(my_index, owners, master, wire_total)
    wire = all_reduce(sparse, strips, buckets)
    small = [wire[SMALL_START + i * SMALL_SPAN : SMALL_START + (i + 1) * SMALL_SPAN].astype(F32) for i in range(3)]
    pairs = (2 * WIN - 1) ** 2
    table = (small[0] + small[1] + small[2])[SMALL_ROWS : SMALL_ROWS + TABLE_ROWS].reshape(-1)
    table = table[: pairs * HEADS].reshape(pairs, HEADS)
    bias = attention_bias(table, lax.axis_index("strip") == strips - 1)
    keep = keep_mask.astype(F32) / KEEP_PROB
    output, output_halo, grad_input, grad_halo, grad_wire, pair_sums = run_block(
        window_cols, keep, block_input, x_halo, cotangent, dy_halo, bias, wire
    )
    pair_sums = pair_sums.reshape(GROUPS, CELLS, GROUP_HEADS, LANES).transpose(0, 2, 1, 3)
    grad_table = lax.dot_general(
        pair_onehot(), pair_sums.reshape(HEADS, -1), (((0,), (1,)), ((), ())),
        precision=PRECISE, preferred_element_type=F32,
    ).reshape(-1)
    grad_table = jnp.pad(grad_table, (0, TABLE_ROWS * 128 - pairs * HEADS)).reshape(TABLE_ROWS, 128)
    grad_wire = lax.dynamic_update_slice(grad_wire, grad_table.astype(BF16), (SMALL_START + SMALL_ROWS, 0))
    output = output.at[:, :SHIFT].set(from_behind(output_halo, "strip", 1).astype(F32))
    grad_input = grad_input.at[:, :SHIFT].set(from_behind(grad_halo, "strip", 1).astype(F32))
    grads = all_reduce(grad_wire, strips, buckets)
    first, second_new, new_weights = run_collect(starts, ranks, grads, master, first_moment, second_moment)
    return (output, grad_input, first, second_new, new_weights)


def solution(mesh):
    in_specs = (
        P("bucket", "strip", None, None),
        P("bucket", "strip", None, None),
        P("bucket"),
        P("bucket", None),
        P(),
        P(("strip", "bucket"), None),
        P(("strip", "bucket"), None),
        P(("strip", "bucket"), None),
    )
    out_specs = (
        P("bucket", "strip", None, None),
        P("bucket", "strip", None, None),
        P(("strip", "bucket"), None),
        P(("strip", "bucket"), None),
        P(("strip", "bucket"), None),
    )
    return jax.shard_map(shards, mesh=mesh, in_specs=in_specs, out_specs=out_specs, check_vma=False)
```

```python
import math

import jax
import jax.numpy as jnp
import numpy as np
from jax import lax
from jax.experimental import pallas as pl
from jax.experimental.pallas import tpu as pltpu
from jax.sharding import PartitionSpec as P

C = 384
HEADS = 12
HD = 32
FF = 1536
WIN = 7
SHIFT = 3
STEP = 10
SMALL_ROWS = 39
TABLE_ROWS = 16


PRECISE = lax.Precision.HIGHEST
NORM_EPS = 1e-05
KEEP_PROB = 0.8
MASK_FILL = -100.0
BETA_ONE = 0.5
BETA_TWO = 0.5
ADAM_EPS = 1e-08
DECAY = 0.05


def from_behind(value, axis, by):
    peers = lax.axis_size(axis)
    return lax.ppermute(value, axis, [(i, (i + by) % peers) for i in range(peers)])


def row_edges():
    first = 3 * C * C // 128
    second = first + C * C // 128
    third = second + C * FF // 128
    fourth = third + FF * C // 128
    fifth = fourth + SMALL_ROWS
    return [first, second, third, fourth, fifth]


GROUPS = 3
GROUP_HEADS = HEADS // GROUPS
CELLS = WIN * 8
LANES = 64
LOG2E = math.log2(math.e)
F32 = jnp.float32
BF16 = jnp.bfloat16


def relative_pairs():
    key = np.arange(CELLS)
    query = np.arange(LANES)
    key_row, key_col = key // 8, key % 8
    query_row, query_col = query // 8, query % 8
    index = (query_row[None, :] - key_row[:, None] + WIN - 1) * (2 * WIN - 1)
    index = index + query_col[None, :] - key_col[:, None] + WIN - 1
    real = (key_col < WIN)[:, None] & ((query_col < WIN) & (query_row < WIN))[None, :]
    return np.where(real, index, -1).astype(np.int32)


def pair_onehot():
    pairs = jnp.asarray(relative_pairs().reshape(-1))
    return (pairs[:, None] == jnp.arange((2 * WIN - 1) ** 2, dtype=jnp.int32)[None, :]).astype(F32)


def attention_bias(table, last_strip):
    spread = lax.dot_general(
        table, pair_onehot(), (((0,), (1,)), ((), ())), precision=PRECISE, preferred_element_type=F32
    ).reshape(HEADS, CELLS, LANES)
    key, query = np.arange(CELLS), np.arange(LANES)
    key_low, query_low = key // 8 >= WIN - SHIFT, query // 8 >= WIN - SHIFT
    key_side, query_side = key % 8 >= WIN - SHIFT, query % 8 >= WIN - SHIFT
    by_row = key_low[:, None] != query_low[None, :]
    by_col = key_side[:, None] != query_side[None, :]
    by_row = jnp.asarray(by_row) & last_strip
    both = jnp.stack([by_row, by_row | jnp.asarray(by_col)])
    masking = jnp.where(both, MASK_FILL, 0.0).astype(F32)
    total = spread[None] + masking[:, None]
    total = jnp.where(jnp.asarray(key % 8 < WIN)[None, None, :, None], total * LOG2E, -1e30)
    total = total.reshape(2, GROUPS, GROUP_HEADS, CELLS, LANES).transpose(0, 1, 3, 2, 4)
    return total.reshape(2, GROUPS, CELLS, GROUP_HEADS * LANES)


def nn(left, right):
    return lax.dot_general(left, right, (((1,), (0,)), ((), ())), preferred_element_type=F32)


def nt(left, right):
    return lax.dot_general(left, right, (((1,), (1,)), ((), ())), preferred_element_type=F32)


def tn(left, right):
    return lax.dot_general(left, right, (((0,), (0,)), ((), ())), preferred_element_type=F32)


def gelu_pair(u):
    normal = 0.5 + 0.5 * lax.erf(u * math.sqrt(0.5))
    gauss = jnp.exp2(u * u * (-0.5 * LOG2E))
    return u * normal, normal + u * gauss * (1.0 / math.sqrt(2.0 * math.pi))


def row_norm(values):
    center = values - jnp.mean(values, axis=-1, keepdims=True)
    scale = lax.rsqrt(jnp.mean(center * center, axis=-1, keepdims=True) + NORM_EPS)
    return center * scale, scale


def norm_pull(grad, normal, scale):
    first = jnp.mean(grad, axis=-1, keepdims=True)
    second = jnp.mean(grad * normal, axis=-1, keepdims=True)
    return scale * (grad - first - normal * second)


def column_sum(values):
    return jnp.sum(values, axis=0, keepdims=True)


def block_kernel(
    cols_ref, keep_ref, x_ref, xh_ref, dy_ref, dyh_ref, bias_ref,
    wire_ref,
    out_ref, outh_ref, gx_ref, gxh_ref, gwire_ref, gs_ref,
    wq_ref, wp_ref, wu_ref, wd_ref, bq_ref, bp_ref, bu_ref, bd_ref, g1_ref, b1_ref, g2_ref, b2_ref,
    gwq_ref, gwp_ref, gwu_ref, gwdt_ref,
    gbq_ref, gbp_ref, gbu_ref, gbd_ref, gg1_ref, gb1_ref, gg2_ref, gb2_ref,
    line, xw, dyw, n1s, zs, qkv, prob, ctx, x1s, n2s, h2s, gfs, ys, gh2s, gctx, gqkv, resw, htr, gtr,
):
    step = pl.program_id(0)
    width = cols_ref[0] * WIN
    keep_one = keep_ref[step, 0]
    keep_two = keep_ref[step, 1]
    wide = xw.shape[0] // CELLS
    columns = x_ref.shape[2]
    slabs = C // 128
    own = WIN - SHIFT

    matrices = (wq_ref, wp_ref, wu_ref, wd_ref)
    vectors = (bq_ref, bp_ref, bu_ref, bd_ref, g1_ref, b1_ref, g2_ref, b2_ref)
    vector_grads = (gbq_ref, gbp_ref, gbu_ref, gbd_ref, gg1_ref, gb1_ref, gg2_ref, gb2_ref)

    @pl.when(step == 0)
    def _():
        for ref, (first, slabs, rows) in zip(matrices, slab_plan()):
            for j in range(slabs):
                ref[:, j * 128 : j * 128 + 128] = wire_ref[first + j * rows : first + (j + 1) * rows, :]
        small = jnp.zeros((SMALL_SPAN, 128), F32)
        for i in range(3):
            first = SMALL_START + i * SMALL_SPAN
            small = small + wire_ref[first : first + SMALL_SPAN, :].astype(F32)
        row = 0
        for ref in vectors:
            for j in range(ref.shape[1] // 128):
                ref[:, j * 128 : j * 128 + 128] = small[row : row + 1]
                row += 1
        line[...] = jnp.zeros_like(line)
        qkv[...] = jnp.zeros_like(qkv)
        gctx[...] = jnp.zeros_like(gctx)
        for ref in (gwq_ref, gwp_ref, gwu_ref, gwdt_ref, gs_ref) + vector_grads:
            ref[...] = jnp.zeros_like(ref)

    def to_windows(main, halo, target):
        for a in range(WIN):
            row = main[0, SHIFT + a] if a < own else halo[0, a - own].astype(F32)
            for s in range(slabs):
                part = row[:, s * 128 : s * 128 + 128]
                line[s, a, 0:columns, :] = part
                line[s, a, pl.ds(width, 8), :] = part[0:8]
        for w in range(wide):
            for a in range(WIN):
                for s in range(slabs):
                    target[w * CELLS + a * 8 : w * CELLS + a * 8 + 8, s * 128 : s * 128 + 128] = line[
                        s, a, w * WIN + SHIFT : w * WIN + SHIFT + 8, :
                    ]

    def from_windows(source, main, halo):
        for w in range(wide):
            for a in range(WIN):
                for s in range(slabs):
                    line[s, a, w * WIN + SHIFT : w * WIN + SHIFT + 8, :] = source[
                        w * CELLS + a * 8 : w * CELLS + a * 8 + 8, s * 128 : s * 128 + 128
                    ]
        kept = lax.broadcasted_iota(jnp.int32, (columns, 128), 0) < width
        front = lax.broadcasted_iota(jnp.int32, (8, 128), 0) < SHIFT
        for a in range(WIN):
            for s in range(slabs):
                wrapped = line[s, a, pl.ds(width, 8), :]
                line[s, a, 0:8, :] = jnp.where(front, wrapped, line[s, a, 0:8, :])
                row = jnp.where(kept, line[s, a, 0:columns, :], 0.0)
                if a < own:
                    main[0, SHIFT + a, :, s * 128 : s * 128 + 128] = row
                else:
                    halo[0, a - own, :, s * 128 : s * 128 + 128] = row.astype(BF16)

    to_windows(x_ref, xh_ref, xw)
    to_windows(dy_ref, dyh_ref, dyw)

    normal, scale_one = row_norm(xw[...])
    n1s[...] = normal
    z = normal * g1_ref[...] + b1_ref[...]
    zs[...] = z.astype(BF16)
    triple = nn(zs[...], wq_ref[...]) + bq_ref[...]
    for w in range(wide):
        qkv[w, 0:CELLS, :] = triple[w * CELLS : w * CELLS + CELLS].astype(BF16)

    lane_head = lax.broadcasted_iota(jnp.int32, (1, 128), 1) // HD
    head_bits = [(lane_head == h).astype(F32).astype(BF16) for h in range(GROUP_HEADS)]

    def stack_of(part):
        return jnp.concatenate([part * head_bits[h] for h in range(GROUP_HEADS)], axis=0)

    def unstack(part):
        total = None
        for h in range(GROUP_HEADS):
            piece = jnp.where(lane_head == h, part[h * LANES : h * LANES + CELLS], 0.0)
            total = piece if total is None else total + piece
        return total

    score_scale = HD ** (-0.5)

    def attend(w, _):
        variant = (w == cols_ref[0] - 1).astype(jnp.int32)
        rows = pl.ds(pl.multiple_of(w * CELLS, 8), CELLS)
        for g in range(GROUPS):
            q = qkv[w, :, g * 128 : g * 128 + 128]
            k = qkv[w, 0:CELLS, C + g * 128 : C + g * 128 + 128]
            v = qkv[w, 0:CELLS, 2 * C + g * 128 : 2 * C + g * 128 + 128]
            s = nt(k, stack_of(q)) * (score_scale * LOG2E) + bias_ref[variant, g]
            e = jnp.exp2(s - jnp.max(s, axis=0, keepdims=True))
            a = e * (1.0 / jnp.sum(e, axis=0, keepdims=True))
            prob[w, g] = a
            ctx[rows, g * 128 : g * 128 + 128] = unstack(tn(a.astype(BF16), v))
        return 0

    lax.fori_loop(0, wide, attend, 0, unroll=True)

    ctx_low = ctx[...].astype(BF16)
    x1 = xw[...] + keep_one * (nn(ctx_low, wp_ref[...]) + bp_ref[...])
    x1s[...] = x1
    normal, scale_two = row_norm(x1)
    n2s[...] = normal
    h2 = (normal * g2_ref[...] + b2_ref[...]).astype(BF16)
    h2s[...] = h2
    htr[...] = h2.astype(F32).T.astype(BF16)

    token = lax.broadcasted_iota(jnp.int32, (wide * CELLS, 1), 0)
    valid = ((token % 8 < WIN) & (token < cols_ref[0] * CELLS)).astype(F32)
    gy = dyw[...] * valid
    gf = (gy * keep_two).astype(BF16)
    gfs[...] = gf
    gbd_ref[...] += column_sum(gf.astype(F32))
    gtr[...] = gf.astype(F32).T.astype(BF16)
    ys[...] = jnp.zeros_like(ys)
    gh2s[...] = jnp.zeros_like(gh2s)

    chunk = 512

    def feed(j, _):
        part = pl.ds(pl.multiple_of(j * chunk, chunk), chunk)
        u = nn(h2s[...], wu_ref[:, part]) + bu_ref[:, part]
        gm = nt(gfs[...], wd_ref[part, :])
        m, slope = gelu_pair(u)
        m = m.astype(BF16)
        gu = (gm * slope).astype(BF16)
        ys[...] += nn(m, wd_ref[part, :])
        gwdt_ref[:, part] += nn(gtr[...], m)
        gwu_ref[:, part] += nn(htr[...], gu)
        gbu_ref[:, part] += column_sum(gu.astype(F32))
        gh2s[...] += nt(gu, wu_ref[:, part])
        return 0

    lax.fori_loop(0, FF // chunk, feed, 0, unroll=True)

    resw[...] = (x1s[...] + keep_two * (ys[...] + bd_ref[...])) * valid
    from_windows(resw, out_ref, outh_ref)

    gh2 = gh2s[...]
    gg2_ref[...] += column_sum(gh2 * n2s[...])
    gb2_ref[...] += column_sum(gh2)
    gx1 = dyw[...] * valid + norm_pull(gh2 * g2_ref[...], n2s[...], scale_two)
    x1s[...] = gx1
    ga = (keep_one * gx1).astype(BF16)
    gbp_ref[...] += column_sum(ga.astype(F32))
    gwp_ref[...] += nn(ctx[...].T.astype(BF16), ga)
    gc = nt(ga, wp_ref[...])
    for w in range(wide):
        gctx[w, 0:CELLS, :] = gc[w * CELLS : w * CELLS + CELLS].astype(BF16)

    def pull_scores(w, _):
        rows = pl.ds(pl.multiple_of(w * CELLS, 8), CELLS)
        for g in range(GROUPS):
            v = qkv[w, 0:CELLS, 2 * C + g * 128 : 2 * C + g * 128 + 128]
            gstack = stack_of(gctx[w, :, g * 128 : g * 128 + 128])
            a = prob[w, g]
            grad = nt(v, gstack)
            inner = jnp.sum(grad * a, axis=0, keepdims=True)
            prob[w, g] = a * (grad - inner)
            gqkv[rows, 2 * C + g * 128 : 2 * C + g * 128 + 128] = nn(a.astype(BF16), gstack)
        return 0

    def pull_pairs(w, _):
        rows = pl.ds(pl.multiple_of(w * CELLS, 8), CELLS)
        for g in range(GROUPS):
            q = qkv[w, :, g * 128 : g * 128 + 128]
            k = qkv[w, 0:CELLS, C + g * 128 : C + g * 128 + 128]
            gs = prob[w, g].astype(BF16)
            gqkv[rows, g * 128 : g * 128 + 128] = unstack(tn(gs, k)) * score_scale
            gqkv[rows, C + g * 128 : C + g * 128 + 128] = nn(gs, stack_of(q)) * score_scale
        return 0

    lax.fori_loop(0, wide, pull_scores, 0, unroll=True)
    lax.fori_loop(0, wide, pull_pairs, 0, unroll=True)
    gs_ref[...] += jnp.sum(prob[...], axis=0)

    gtriple = gqkv[...].astype(BF16)
    gbq_ref[...] += column_sum(gtriple.astype(F32))
    gwq_ref[...] += nn(zs[...].astype(F32).T.astype(BF16), gtriple)
    gz = nt(gtriple, wq_ref[...]).astype(BF16).astype(F32)
    gg1_ref[...] += column_sum(gz * n1s[...])
    gb1_ref[...] += column_sum(gz)
    resw[...] = x1s[...] + norm_pull(gz * g1_ref[...], n1s[...], scale_one)
    from_windows(resw, gx_ref, gxh_ref)

    @pl.when(step == pl.num_programs(0) - 1)
    def _():
        for grad, (first, slabs, rows) in zip((gwq_ref, gwp_ref, gwu_ref), slab_plan()):
            for j in range(slabs):
                gwire_ref[first + j * rows : first + (j + 1) * rows, :] = grad[:, j * 128 : j * 128 + 128].astype(BF16)
        first, slabs, rows = slab_plan()[3]
        for j in range(slabs):
            gwire_ref[first + j * rows : first + (j + 1) * rows, :] = gwdt_ref[j * 128 : j * 128 + 128, :].T.astype(BF16)
        pieces = [ref[:, j * 128 : j * 128 + 128] for ref in vector_grads for j in range(ref.shape[1] // 128)]
        spare = gwire_ref.shape[0] - SMALL_START - len(pieces)
        pieces.append(jnp.zeros((spare, 128), F32))
        gwire_ref[SMALL_START:, :] = jnp.concatenate(pieces, axis=0).astype(BF16)


def run_block(cols, keep, x, xh, dy, dyh, bias, wire):
    samples, rows, columns, _ = x.shape
    wide = columns // WIN
    tokens = wide * CELLS

    def per_image(array):
        return pl.BlockSpec((1,) + array.shape[1:], lambda i: (i, 0, 0, 0))

    def whole(shape):
        return pl.BlockSpec(shape, lambda i: (0,) * len(shape))

    smem = pl.BlockSpec(memory_space=pltpu.SMEM)
    full = jax.ShapeDtypeStruct(x.shape, F32)
    part = jax.ShapeDtypeStruct(xh.shape, BF16)
    sums = (GROUPS, CELLS, GROUP_HEADS * LANES)
    vectors = [3 * C, C, FF, C, C, C, C, C]
    return pl.pallas_call(
        block_kernel,
        grid=(samples,),
        in_specs=[smem, smem, per_image(x), per_image(xh), per_image(dy), per_image(dyh), whole(bias.shape)]
        + [whole(wire.shape)],
        out_specs=[per_image(x), per_image(xh), per_image(x), per_image(xh), whole(wire.shape), whole(sums)],
        out_shape=[full, part, full, part, jax.ShapeDtypeStruct(wire.shape, BF16), jax.ShapeDtypeStruct(sums, F32)],
        scratch_shapes=[pltpu.VMEM(s, BF16) for s in ((C, 3 * C), (C, C), (C, FF), (FF, C))]
        + [pltpu.VMEM((1, size), F32) for size in vectors]
        + [pltpu.VMEM(s, F32) for s in ((C, 3 * C), (C, C), (C, FF), (C, FF))]
        + [pltpu.VMEM((1, size), F32) for size in vectors]
        + [
            pltpu.VMEM((C // 128, WIN, columns + 8, 128), F32),
            pltpu.VMEM((tokens, C), F32),
            pltpu.VMEM((tokens, C), F32),
            pltpu.VMEM((tokens, C), F32),
            pltpu.VMEM((tokens, C), BF16),
            pltpu.VMEM((wide, LANES, 3 * C), BF16),
            pltpu.VMEM((wide, GROUPS, CELLS, GROUP_HEADS * LANES), F32),
            pltpu.VMEM((tokens, C), F32),
            pltpu.VMEM((tokens, C), F32),
            pltpu.VMEM((tokens, C), F32),
            pltpu.VMEM((tokens, C), BF16),
            pltpu.VMEM((tokens, C), BF16),
            pltpu.VMEM((tokens, C), F32),
            pltpu.VMEM((tokens, C), F32),
            pltpu.VMEM((wide, LANES, C), BF16),
            pltpu.VMEM((tokens, 3 * C), F32),
            pltpu.VMEM((tokens, C), F32),
            pltpu.VMEM((C, tokens), BF16),
            pltpu.VMEM((C, tokens), BF16),
        ],
        compiler_params=pltpu.CompilerParams(vmem_limit_bytes=58 * 1024 * 1024),
        name="block",
    )(cols, keep, x, xh, dy, dyh, bias, wire)


SMALL_START = 3 * C * C // 128 + C * C // 128 + 2 * C * FF // 128
SMALL_SPAN = 64
WIRE_ROWS = SMALL_START + 3 * SMALL_SPAN


def slab_plan():
    return [
        (0, 3 * C // 128, C),
        (3 * C * C // 128, C // 128, C),
        (4 * C * C // 128, FF // 128, C),
        (4 * C * C // 128 + C * FF // 128, C // 128, FF),
    ]


def wire_rows(device_count):
    unit = 4 * device_count * 16
    return -(-WIRE_ROWS // unit) * unit


def split_three(values):
    high = values.astype(BF16)
    rest = values - high.astype(F32)
    middle = rest.astype(BF16)
    return high, middle, (rest - middle.astype(F32)).astype(BF16)


def dispatch_kernel(me_ref, owner_ref, master_ref, out_ref, rank_ref, start_ref, padded, packed, start_s, sem):
    blocks = owner_ref.shape[0]
    capacity = master_ref.shape[0]
    mine = (owner_ref[...] == me_ref[0]).astype(F32)
    low = mine.astype(BF16)
    row = lax.broadcasted_iota(jnp.int32, (128, 128), 0)
    col = lax.broadcasted_iota(jnp.int32, (128, 128), 1)
    within = nn(low, (row <= col).astype(F32).astype(BF16))
    sums = nn(low, jnp.ones((128, 128), BF16))
    below = lax.broadcasted_iota(jnp.int32, (blocks, blocks), 1) < lax.broadcasted_iota(jnp.int32, (blocks, blocks), 0)
    start = nn(below.astype(F32).astype(BF16), sums.astype(BF16))
    rank_ref[...] = jnp.where(mine > 0, within - 1.0, -1.0)
    start_ref[...] = start.astype(jnp.int32)
    copy = pltpu.make_async_copy(start_ref, start_s, sem)
    copy.start()
    padded[...] = jnp.zeros_like(padded)
    padded[0:capacity, :] = master_ref[...]
    out_ref[...] = jnp.zeros_like(out_ref)
    copy.wait()
    slot = row.astype(F32)

    def block(b, _):
        hot = (slot == rank_ref[pl.ds(b, 1), :]).astype(F32).astype(BF16)
        rows = padded[pl.ds(start_s[b, 0], 128), :].astype(BF16)
        packed[pl.ds(pl.multiple_of(b * 128, 128), 128), :] = tn(hot, rows)
        return 0

    small = SMALL_START // 128
    lax.fori_loop(0, small, block, 0, unroll=4)
    hot = (slot == rank_ref[small : small + 1, :]).astype(F32).astype(BF16)
    for i, piece in enumerate(split_three(padded[pl.ds(start_s[small, 0], 128), :])):
        first = SMALL_START + i * SMALL_SPAN
        out_ref[first : first + SMALL_SPAN, :] = tn(hot, piece)[0:SMALL_SPAN].astype(BF16)
    for first, slabs, rows in slab_plan():
        for j in range(slabs):
            out_ref[first + j * rows : first + (j + 1) * rows, :] = packed[
                pl.ds(first + j, rows, stride=slabs), :
            ].astype(BF16)


def run_dispatch(me, owners, master, wire):
    blocks = owners.shape[0]
    vmem = pl.BlockSpec(memory_space=pltpu.VMEM)
    return pl.pallas_call(
        dispatch_kernel,
        in_specs=[pl.BlockSpec(memory_space=pltpu.SMEM), vmem, vmem],
        out_specs=[vmem] * 3,
        out_shape=[
            jax.ShapeDtypeStruct((wire, 128), BF16),
            jax.ShapeDtypeStruct((blocks, 128), F32),
            jax.ShapeDtypeStruct((blocks, 128), jnp.int32),
        ],
        scratch_shapes=[
            pltpu.VMEM((-(-(master.shape[0] + 128) // 8) * 8, 128), F32),
            pltpu.VMEM((SMALL_START, 128), F32),
            pltpu.SMEM((blocks, 128), jnp.int32),
            pltpu.SemaphoreType.DMA,
        ],
        compiler_params=pltpu.CompilerParams(vmem_limit_bytes=40 * 1024 * 1024),
        name="dispatch",
    )(me, owners, master)


def collect_kernel(start_ref, rank_ref, grad_ref, master_ref, first_ref, second_ref,
                   first_out, second_out, master_out, packed, total):
    capacity = master_ref.shape[0]
    total[...] = jnp.zeros_like(total)
    for first, slabs, rows in slab_plan():
        for j in range(slabs):
            packed[pl.ds(first + j, rows, stride=slabs), :] = grad_ref[
                first + j * rows : first + (j + 1) * rows, :
            ].astype(F32)
    packed[SMALL_START : SMALL_START + SMALL_SPAN, :] = grad_ref[SMALL_START : SMALL_START + SMALL_SPAN, :].astype(F32)
    packed[SMALL_START + SMALL_SPAN : SMALL_START + 128, :] = jnp.zeros((128 - SMALL_SPAN, 128), F32)
    slot = lax.broadcasted_iota(jnp.int32, (128, 128), 0).astype(F32)

    def block(b, _):
        hot = (slot == rank_ref[pl.ds(b, 1), :]).astype(F32).astype(BF16)
        part = nn(hot, packed[pl.ds(pl.multiple_of(b * 128, 128), 128), :].astype(BF16))
        where = pl.ds(start_ref[b, 0], 128)
        total[where, :] = total[where, :] + part
        return 0

    lax.fori_loop(0, SMALL_START // 128 + 1, block, 0)
    slots = lax.broadcasted_iota(jnp.int32, (capacity, 1), 0)
    edges = [edge // 128 for edge in row_edges()[:4]] + [SMALL_START // 128 + 1]
    rates = [2.0 / math.sqrt(C), 2.0 / math.sqrt(C // 8), 2.0 / math.sqrt(C), 2.0 / math.sqrt(FF), 1.0, 0.0]
    rate = jnp.full((capacity, 1), rates[0], F32)
    for edge, amount in zip(edges, rates[1:]):
        rate = jnp.where(slots >= start_ref[edge, 0], amount, rate)
    decay = jnp.where(slots < start_ref[edges[3], 0], DECAY, 0.0)
    grads = total[0:capacity, :]
    weights = master_ref[...]
    first = BETA_ONE * first_ref[...] + (1.0 - BETA_ONE) * grads
    second = BETA_TWO * second_ref[...] + (1.0 - BETA_TWO) * grads * grads
    first_out[...] = first
    second_out[...] = second
    first_hat = first / (1.0 - BETA_ONE**STEP)
    second_hat = second / (1.0 - BETA_TWO**STEP)
    master_out[...] = weights - rate * (first_hat / (jnp.sqrt(second_hat) + ADAM_EPS) + decay * weights)


def run_collect(starts, ranks, grads, master, first, second):
    vmem = pl.BlockSpec(memory_space=pltpu.VMEM)
    return pl.pallas_call(
        collect_kernel,
        in_specs=[pl.BlockSpec(memory_space=pltpu.SMEM)] + [vmem] * 5,
        out_specs=[vmem] * 3,
        out_shape=[jax.ShapeDtypeStruct(master.shape, F32)] * 3,
        scratch_shapes=[
            pltpu.VMEM((SMALL_START + 128, 128), F32),
            pltpu.VMEM((-(-(master.shape[0] + 128) // 8) * 8, 128), F32),
        ],
        compiler_params=pltpu.CompilerParams(vmem_limit_bytes=40 * 1024 * 1024),
        name="collect",
    )(starts, ranks, grads, master, first, second)


def reduce_parts(strips, buckets, rows, orders):
    sizes = {"z": strips // 2, "y": 2, "x": buckets // 2}
    length = rows // 2 // len(orders)
    parts = []
    for order in orders:
        levels, share = [], length
        for axis in order:
            share = share // sizes[axis]
            levels.append((axis, sizes[axis], share))
        parts.append((length, levels))
    return parts


def all_reduce_kernel(strips, buckets, parts, in_ref, out_ref, *scratch):
    strip, bucket = lax.axis_index("strip"), lax.axis_index("bucket")
    sizes = {"z": strips // 2, "y": 2, "x": buckets // 2, "core": 2}
    mine = {"z": strip // 2, "y": strip % 2, "x": bucket // 2, "core": bucket % 2}
    send_sems, recv_sems = scratch[-2:]
    buffers = list(scratch[:-2])

    def peer(axis, offset):
        return lax.rem(mine[axis] + offset, sizes[axis])

    def device(axis, offset):
        place = dict(mine)
        place[axis] = peer(axis, offset)
        return (place["z"] * 2 + place["y"], place["x"] * 2 + place["core"])

    barrier = pltpu.get_barrier_semaphore()
    partners = [(axis, offset) for axis, size in sizes.items() for offset in range(1, size)]
    for axis, offset in partners:
        pl.semaphore_signal(barrier, inc=1, device_id=device(axis, offset), device_id_type=pl.DeviceIdType.MESH)
    pl.semaphore_wait(barrier, len(partners))

    used = [0]

    def send(source, target, axis, offset):
        at = used[0]
        used[0] += 1
        copy = pltpu.make_async_remote_copy(
            src_ref=source, dst_ref=target, send_sem=send_sems.at[at], recv_sem=recv_sems.at[at],
            device_id=device(axis, offset), device_id_type=pl.DeviceIdType.MESH,
        )
        copy.start()
        return copy

    def span(start, length):
        return pl.ds(pl.multiple_of(start, 16), length)

    half = in_ref.shape[0] // 2

    def part_steps(p, length, levels):
        core_in, core_sum = buffers.pop(0), buffers.pop(0)
        boxes = [(buffers.pop(0), buffers.pop(0)) for _ in levels]
        own = mine["core"] * half + p * length
        other = (1 - mine["core"]) * half + p * length
        copy = send(in_ref.at[span(other, length)], core_in, "core", 1)
        yield
        copy.wait()
        core_sum[...] = in_ref[span(own, length), :] + core_in[...]
        held, spans = core_sum, [(own, length)]
        for (axis, size, share), (inbox, total) in zip(levels, boxes):
            copies = [
                send(held.at[span(peer(axis, offset) * share, share)],
                     inbox.at[pl.ds((offset - 1) * share, share)], axis, offset)
                for offset in range(1, size)
            ]
            yield
            for copy in copies:
                copy.wait()
            value = held[span(mine[axis] * share, share), :].astype(F32)
            for offset in range(1, size):
                value = value + inbox[(offset - 1) * share : offset * share, :].astype(F32)
            spans.append((spans[-1][0] + mine[axis] * share, share))
            total[...] = value.astype(BF16)
            held = total
        start, share = spans[-1]
        out_ref[span(start, share), :] = held[...]
        for (axis, size, share), (start, _) in zip(levels[::-1], spans[:0:-1]):
            region = out_ref.at[span(start, share)]
            copies = [send(region, region, axis, offset) for offset in range(1, size)]
            yield
            for copy in copies:
                copy.wait()
        region = out_ref.at[span(own, length)]
        copy = send(region, region, "core", 1)
        yield
        copy.wait()

    running = [part_steps(p, length, levels) for p, (length, levels) in enumerate(parts)]
    waiting, active = running, []
    while waiting or active:
        active, waiting = active + waiting[:2], waiting[2:]
        for steps in list(active):
            if next(steps, steps) is steps:
                active.remove(steps)


def all_reduce(values, strips, buckets, orders):
    rows = values.shape[0]
    parts = reduce_parts(strips, buckets, rows, orders)
    vmem = pl.BlockSpec(memory_space=pltpu.VMEM)
    shapes, copies = [], 0
    for length, levels in parts:
        shapes += [(length, 128), (length, 128)]
        for _, size, share in levels:
            shapes += [((size - 1) * share, 128), (share, 128)]
        copies += 2 + 2 * sum(size - 1 for _, size, _ in levels)
    return pl.pallas_call(
        lambda *refs: all_reduce_kernel(strips, buckets, parts, *refs),
        in_specs=[vmem],
        out_specs=vmem,
        out_shape=jax.ShapeDtypeStruct(values.shape, BF16),
        scratch_shapes=[pltpu.VMEM(shape, BF16) for shape in shapes]
        + [pltpu.SemaphoreType.DMA((copies,)), pltpu.SemaphoreType.DMA((copies,))],
        compiler_params=pltpu.CompilerParams(
            vmem_limit_bytes=40 * 1024 * 1024, collective_id=0, has_side_effects=True
        ),
        name="all_reduce",
    )(values)


ORDERS = (("x", "y", "z"), ("y", "x", "z")) * 2


def shards(
    block_input, cotangent, window_cols, keep_mask, owner_list, master, first_moment, second_moment
):
    strips = lax.axis_size("strip")
    buckets = lax.axis_size("bucket")
    wire_total = wire_rows(strips * buckets)
    x_halo = from_behind(block_input[:, :SHIFT].astype(BF16), "strip", -1)
    dy_halo = from_behind(cotangent[:, :SHIFT].astype(BF16), "strip", -1)
    my_index = lax.axis_index(("strip", "bucket")).astype(jnp.int32).reshape(1)
    blocks = -(-(SMALL_START // 128 + 2) // 8) * 8
    owners = jnp.pad(owner_list, (0, blocks * 128 - owner_list.shape[0]), constant_values=-1).reshape(blocks, 128)
    sparse, ranks, starts = run_dispatch(my_index, owners, master, wire_total)
    wire = all_reduce(sparse, strips, buckets, ORDERS)
    small = [wire[SMALL_START + i * SMALL_SPAN : SMALL_START + (i + 1) * SMALL_SPAN].astype(F32) for i in range(3)]
    pairs = (2 * WIN - 1) ** 2
    table = (small[0] + small[1] + small[2])[SMALL_ROWS : SMALL_ROWS + TABLE_ROWS].reshape(-1)
    table = table[: pairs * HEADS].reshape(pairs, HEADS)
    bias = attention_bias(table, lax.axis_index("strip") == strips - 1)
    keep = keep_mask.astype(F32) / KEEP_PROB
    output, output_halo, grad_input, grad_halo, grad_wire, pair_sums = run_block(
        window_cols, keep, block_input, x_halo, cotangent, dy_halo, bias, wire
    )
    pair_sums = pair_sums.reshape(GROUPS, CELLS, GROUP_HEADS, LANES).transpose(0, 2, 1, 3)
    grad_table = lax.dot_general(
        pair_onehot(), pair_sums.reshape(HEADS, -1), (((0,), (1,)), ((), ())),
        precision=PRECISE, preferred_element_type=F32,
    ).reshape(-1)
    grad_table = jnp.pad(grad_table, (0, TABLE_ROWS * 128 - pairs * HEADS)).reshape(TABLE_ROWS, 128)
    grad_wire = lax.dynamic_update_slice(grad_wire, grad_table.astype(BF16), (SMALL_START + SMALL_ROWS, 0))
    output = output.at[:, :SHIFT].set(from_behind(output_halo, "strip", 1).astype(F32))
    grad_input = grad_input.at[:, :SHIFT].set(from_behind(grad_halo, "strip", 1).astype(F32))
    grads = all_reduce(grad_wire, strips, buckets, ORDERS)
    first, second_new, new_weights = run_collect(starts, ranks, grads, master, first_moment, second_moment)
    return (output, grad_input, first, second_new, new_weights)


def solution(mesh):
    in_specs = (
        P("bucket", "strip", None, None),
        P("bucket", "strip", None, None),
        P("bucket"),
        P("bucket", None),
        P(),
        P(("strip", "bucket"), None),
        P(("strip", "bucket"), None),
        P(("strip", "bucket"), None),
    )
    out_specs = (
        P("bucket", "strip", None, None),
        P("bucket", "strip", None, None),
        P(("strip", "bucket"), None),
        P(("strip", "bucket"), None),
        P(("strip", "bucket"), None),
    )
    return jax.shard_map(shards, mesh=mesh, in_specs=in_specs, out_specs=out_specs, check_vma=False)
```

```python
import math

import jax
import jax.numpy as jnp
import numpy as np
from jax import lax
from jax.experimental import pallas as pl
from jax.experimental.pallas import tpu as pltpu
from jax.sharding import PartitionSpec as P

C = 384
HEADS = 12
HD = 32
FF = 1536
WIN = 7
SHIFT = 3
STEP = 10
SMALL_ROWS = 39
TABLE_ROWS = 16


PRECISE = lax.Precision.HIGHEST
NORM_EPS = 1e-05
KEEP_PROB = 0.8
MASK_FILL = -100.0
BETA_ONE = 0.5
BETA_TWO = 0.5
ADAM_EPS = 1e-08
DECAY = 0.05


def row_edges():
    first = 3 * C * C // 128
    second = first + C * C // 128
    third = second + C * FF // 128
    fourth = third + FF * C // 128
    fifth = fourth + SMALL_ROWS
    return [first, second, third, fourth, fifth]


GROUPS = 3
GROUP_HEADS = HEADS // GROUPS
CELLS = WIN * 8
LANES = 64
LOG2E = math.log2(math.e)
F32 = jnp.float32
BF16 = jnp.bfloat16


def relative_pairs():
    key = np.arange(CELLS)
    query = np.arange(LANES)
    key_row, key_col = key // 8, key % 8
    query_row, query_col = query // 8, query % 8
    index = (query_row[None, :] - key_row[:, None] + WIN - 1) * (2 * WIN - 1)
    index = index + query_col[None, :] - key_col[:, None] + WIN - 1
    real = (key_col < WIN)[:, None] & ((query_col < WIN) & (query_row < WIN))[None, :]
    return np.where(real, index, -1).astype(np.int32)


def pair_onehot():
    pairs = jnp.asarray(relative_pairs().reshape(-1))
    return (pairs[:, None] == jnp.arange((2 * WIN - 1) ** 2, dtype=jnp.int32)[None, :]).astype(F32)


def attention_bias(table, last_strip):
    spread = lax.dot_general(
        table, pair_onehot(), (((0,), (1,)), ((), ())), precision=PRECISE, preferred_element_type=F32
    ).reshape(HEADS, CELLS, LANES)
    key, query = np.arange(CELLS), np.arange(LANES)
    key_low, query_low = key // 8 >= WIN - SHIFT, query // 8 >= WIN - SHIFT
    key_side, query_side = key % 8 >= WIN - SHIFT, query % 8 >= WIN - SHIFT
    by_row = key_low[:, None] != query_low[None, :]
    by_col = key_side[:, None] != query_side[None, :]
    by_row = jnp.asarray(by_row) & last_strip
    both = jnp.stack([by_row, by_row | jnp.asarray(by_col)])
    masking = jnp.where(both, MASK_FILL, 0.0).astype(F32)
    total = spread[None] + masking[:, None]
    total = jnp.where(jnp.asarray(key % 8 < WIN)[None, None, :, None], total * LOG2E, -1e30)
    total = total.reshape(2, GROUPS, GROUP_HEADS, CELLS, LANES).transpose(0, 1, 3, 2, 4)
    return total.reshape(2, GROUPS, CELLS, GROUP_HEADS * LANES)


def nn(left, right):
    return lax.dot_general(left, right, (((1,), (0,)), ((), ())), preferred_element_type=F32)


def nt(left, right):
    return lax.dot_general(left, right, (((1,), (1,)), ((), ())), preferred_element_type=F32)


def tn(left, right):
    return lax.dot_general(left, right, (((0,), (0,)), ((), ())), preferred_element_type=F32)


def gelu_pair(u):
    normal = 0.5 + 0.5 * lax.erf(u * math.sqrt(0.5))
    gauss = jnp.exp2(u * u * (-0.5 * LOG2E))
    return u * normal, normal + u * gauss * (1.0 / math.sqrt(2.0 * math.pi))


def row_norm(values):
    center = values - jnp.mean(values, axis=-1, keepdims=True)
    scale = lax.rsqrt(jnp.mean(center * center, axis=-1, keepdims=True) + NORM_EPS)
    return center * scale, scale


def norm_pull(grad, normal, scale):
    first = jnp.mean(grad, axis=-1, keepdims=True)
    second = jnp.mean(grad * normal, axis=-1, keepdims=True)
    return scale * (grad - first - normal * second)


def column_sum(values):
    return jnp.sum(values, axis=0, keepdims=True)


def block_kernel(
    strips, cols_ref, keep_ref, x_ref, dy_ref, x_any, dy_any, bias_ref, wire_ref,
    out_ref, gx_ref, outh_ref, gxh_ref, gwire_ref, gs_ref,
    fetched, halo_out, halo_in, back_out, back_in, fetch_sem, send_sems, recv_sems,
    wq_ref, wp_ref, wu_ref, wd_ref, bq_ref, bp_ref, bu_ref, bd_ref, g1_ref, b1_ref, g2_ref, b2_ref,
    gwq_ref, gwp_ref, gwu_ref, gwdt_ref,
    gbq_ref, gbp_ref, gbu_ref, gbd_ref, gg1_ref, gb1_ref, gg2_ref, gb2_ref,
    line, xw, dyw, n1s, zs, qkv, prob, ctx, x1s, n2s, h2s, gfs, ys, gh2s, gctx, gqkv, resw, htr, gtr,
):
    step = pl.program_id(0)
    width = cols_ref[0] * WIN
    keep_one = keep_ref[step, 0]
    keep_two = keep_ref[step, 1]
    wide = xw.shape[0] // CELLS
    columns = x_ref.shape[2]
    slabs = C // 128
    own = WIN - SHIFT

    matrices = (wq_ref, wp_ref, wu_ref, wd_ref)
    vectors = (bq_ref, bp_ref, bu_ref, bd_ref, g1_ref, b1_ref, g2_ref, b2_ref)
    vector_grads = (gbq_ref, gbp_ref, gbu_ref, gbd_ref, gg1_ref, gb1_ref, gg2_ref, gb2_ref)

    strip, bucket = lax.axis_index("strip"), lax.axis_index("bucket")
    above = (lax.rem(strip + strips - 1, strips), bucket)
    below = (lax.rem(strip + 1, strips), bucket)

    def halo_copy(kind, image):
        source = halo_out.at[kind, image] if kind < 2 else back_out.at[kind - 2, image]
        target = halo_in.at[kind, image] if kind < 2 else back_in.at[kind - 2, image]
        return pltpu.make_async_remote_copy(
            src_ref=source, dst_ref=target, send_sem=send_sems.at[kind, image], recv_sem=recv_sems.at[kind, image],
            device_id=above if kind < 2 else below, device_id_type=pl.DeviceIdType.MESH,
        )

    @pl.when(step == 0)
    def _():
        barrier = pltpu.get_barrier_semaphore()
        fetches = [
            pltpu.make_async_copy(array.at[:, pl.ds(0, SHIFT)], fetched.at[kind], fetch_sem.at[kind])
            for kind, array in enumerate((x_any, dy_any))
        ]
        for fetch in fetches:
            fetch.start()
        for neighbour in (above, below):
            pl.semaphore_signal(barrier, inc=1, device_id=neighbour, device_id_type=pl.DeviceIdType.MESH)
        pl.semaphore_wait(barrier, 2)
        for fetch in fetches:
            fetch.wait()

        def send_rows(image, _):
            for kind in range(2):
                halo_out[kind, image] = fetched[kind, image].astype(BF16)
                halo_copy(kind, image).start()
            return 0

        lax.fori_loop(0, fetched.shape[1], send_rows, 0)
        for ref, (first, slabs, rows) in zip(matrices, slab_plan()):
            for j in range(slabs):
                ref[:, j * 128 : j * 128 + 128] = wire_ref[first + j * rows : first + (j + 1) * rows, :]
        small = jnp.zeros((SMALL_SPAN, 128), F32)
        for i in range(3):
            first = SMALL_START + i * SMALL_SPAN
            small = small + wire_ref[first : first + SMALL_SPAN, :].astype(F32)
        row = 0
        for ref in vectors:
            for j in range(ref.shape[1] // 128):
                ref[:, j * 128 : j * 128 + 128] = small[row : row + 1]
                row += 1
        line[...] = jnp.zeros_like(line)
        qkv[...] = jnp.zeros_like(qkv)
        gctx[...] = jnp.zeros_like(gctx)
        for ref in (gwq_ref, gwp_ref, gwu_ref, gwdt_ref, gs_ref) + vector_grads:
            ref[...] = jnp.zeros_like(ref)

    def to_windows(main, kind, target):
        halo_copy(kind, step).wait_recv()
        wrapped_row = lax.broadcasted_iota(jnp.int32, (8, 128), 0) >= WIN - SHIFT
        for a in range(WIN):
            row = main[0, SHIFT + a] if a < own else halo_in[kind, step, a - own].astype(F32)
            for s in range(slabs):
                line[s, a, 8 : 8 + columns, :] = row[:, s * 128 : s * 128 + 128]
        for a in range(WIN):
            for s in range(slabs):
                front = line[s, a, 8 - (WIN - SHIFT) : 16 - (WIN - SHIFT), :]
                for w in range(wide):
                    first = 8 + w * WIN + SHIFT
                    tile = jnp.where(wrapped_row & (w == cols_ref[0] - 1), front, line[s, a, first : first + 8, :])
                    target[w * CELLS + a * 8 : w * CELLS + a * 8 + 8, s * 128 : s * 128 + 128] = tile

    def from_windows(source, main, kind):
        for w in range(wide):
            for a in range(WIN):
                for s in range(slabs):
                    first = 8 + w * WIN + SHIFT
                    line[s, a, first : first + 8, :] = source[
                        w * CELLS + a * 8 : w * CELLS + a * 8 + 8, s * 128 : s * 128 + 128
                    ]
        kept = lax.broadcasted_iota(jnp.int32, (columns, 128), 0) < width
        front = lax.broadcasted_iota(jnp.int32, (8, 128), 0) < SHIFT
        for a in range(WIN):
            for s in range(slabs):
                wrapped = line[s, a, pl.ds(width + 8, 8), :]
                line[s, a, 8:16, :] = jnp.where(front, wrapped, line[s, a, 8:16, :])
                row = jnp.where(kept, line[s, a, 8 : 8 + columns, :], 0.0)
                if a < own:
                    main[0, SHIFT + a, :, s * 128 : s * 128 + 128] = row
                else:
                    back_out[kind - 2, step, a - own, :, s * 128 : s * 128 + 128] = row.astype(BF16)
        halo_copy(kind, step).start()

    to_windows(x_ref, 0, xw)
    to_windows(dy_ref, 1, dyw)

    normal, scale_one = row_norm(xw[...])
    n1s[...] = normal
    z = normal * g1_ref[...] + b1_ref[...]
    zs[...] = z.astype(BF16)
    triple = nn(zs[...], wq_ref[...]) + bq_ref[...]
    for w in range(wide):
        qkv[w, 0:CELLS, :] = triple[w * CELLS : w * CELLS + CELLS].astype(BF16)

    lane_head = lax.broadcasted_iota(jnp.int32, (1, 128), 1) // HD
    head_bits = [(lane_head == h).astype(F32).astype(BF16) for h in range(GROUP_HEADS)]

    def stack_of(part):
        return jnp.concatenate([part * head_bits[h] for h in range(GROUP_HEADS)], axis=0)

    def unstack(part):
        total = None
        for h in range(GROUP_HEADS):
            piece = jnp.where(lane_head == h, part[h * LANES : h * LANES + CELLS], 0.0)
            total = piece if total is None else total + piece
        return total

    score_scale = HD ** (-0.5)

    def attend(w, _):
        variant = (w == cols_ref[0] - 1).astype(jnp.int32)
        rows = pl.ds(pl.multiple_of(w * CELLS, 8), CELLS)
        for g in range(GROUPS):
            q = qkv[w, :, g * 128 : g * 128 + 128]
            k = qkv[w, 0:CELLS, C + g * 128 : C + g * 128 + 128]
            v = qkv[w, 0:CELLS, 2 * C + g * 128 : 2 * C + g * 128 + 128]
            s = nt(k, stack_of(q)) * (score_scale * LOG2E) + bias_ref[variant, g]
            e = jnp.exp2(s - jnp.max(s, axis=0, keepdims=True))
            a = e * (1.0 / jnp.sum(e, axis=0, keepdims=True))
            prob[w, g] = a
            ctx[rows, g * 128 : g * 128 + 128] = unstack(tn(a.astype(BF16), v))
        return 0

    lax.fori_loop(0, wide, attend, 0, unroll=True)

    ctx_low = ctx[...].astype(BF16)
    x1 = xw[...] + keep_one * (nn(ctx_low, wp_ref[...]) + bp_ref[...])
    x1s[...] = x1
    normal, scale_two = row_norm(x1)
    n2s[...] = normal
    h2 = (normal * g2_ref[...] + b2_ref[...]).astype(BF16)
    h2s[...] = h2
    htr[...] = h2.astype(F32).T.astype(BF16)

    token = lax.broadcasted_iota(jnp.int32, (wide * CELLS, 1), 0)
    valid = ((token % 8 < WIN) & (token < cols_ref[0] * CELLS)).astype(F32)
    gy = dyw[...] * valid
    gf = (gy * keep_two).astype(BF16)
    gfs[...] = gf
    gbd_ref[...] += column_sum(gf.astype(F32))
    gtr[...] = gf.astype(F32).T.astype(BF16)
    ys[...] = jnp.zeros_like(ys)
    gh2s[...] = jnp.zeros_like(gh2s)

    chunk = 512

    def feed(j, _):
        part = pl.ds(pl.multiple_of(j * chunk, chunk), chunk)
        u = nn(h2s[...], wu_ref[:, part]) + bu_ref[:, part]
        gm = nt(gfs[...], wd_ref[part, :])
        m, slope = gelu_pair(u)
        m = m.astype(BF16)
        gu = (gm * slope).astype(BF16)
        ys[...] += nn(m, wd_ref[part, :])
        gwdt_ref[:, part] += nn(gtr[...], m)
        gwu_ref[:, part] += nn(htr[...], gu)
        gbu_ref[:, part] += column_sum(gu.astype(F32))
        gh2s[...] += nt(gu, wu_ref[:, part])
        return 0

    lax.fori_loop(0, FF // chunk, feed, 0, unroll=True)

    resw[...] = (x1s[...] + keep_two * (ys[...] + bd_ref[...])) * valid
    from_windows(resw, out_ref, 2)

    gh2 = gh2s[...]
    gg2_ref[...] += column_sum(gh2 * n2s[...])
    gb2_ref[...] += column_sum(gh2)
    gx1 = dyw[...] * valid + norm_pull(gh2 * g2_ref[...], n2s[...], scale_two)
    x1s[...] = gx1
    ga = (keep_one * gx1).astype(BF16)
    gbp_ref[...] += column_sum(ga.astype(F32))
    gwp_ref[...] += nn(ctx[...].T.astype(BF16), ga)
    gc = nt(ga, wp_ref[...])
    for w in range(wide):
        gctx[w, 0:CELLS, :] = gc[w * CELLS : w * CELLS + CELLS].astype(BF16)

    def pull_scores(w, _):
        rows = pl.ds(pl.multiple_of(w * CELLS, 8), CELLS)
        for g in range(GROUPS):
            v = qkv[w, 0:CELLS, 2 * C + g * 128 : 2 * C + g * 128 + 128]
            gstack = stack_of(gctx[w, :, g * 128 : g * 128 + 128])
            a = prob[w, g]
            grad = nt(v, gstack)
            inner = jnp.sum(grad * a, axis=0, keepdims=True)
            prob[w, g] = a * (grad - inner)
            gqkv[rows, 2 * C + g * 128 : 2 * C + g * 128 + 128] = nn(a.astype(BF16), gstack)
        return 0

    def pull_pairs(w, _):
        rows = pl.ds(pl.multiple_of(w * CELLS, 8), CELLS)
        for g in range(GROUPS):
            q = qkv[w, :, g * 128 : g * 128 + 128]
            k = qkv[w, 0:CELLS, C + g * 128 : C + g * 128 + 128]
            gs = prob[w, g].astype(BF16)
            gqkv[rows, g * 128 : g * 128 + 128] = unstack(tn(gs, k)) * score_scale
            gqkv[rows, C + g * 128 : C + g * 128 + 128] = nn(gs, stack_of(q)) * score_scale
        return 0

    lax.fori_loop(0, wide, pull_scores, 0, unroll=True)
    lax.fori_loop(0, wide, pull_pairs, 0, unroll=True)
    gs_ref[...] += jnp.sum(prob[...], axis=0)

    gtriple = gqkv[...].astype(BF16)
    gbq_ref[...] += column_sum(gtriple.astype(F32))
    gwq_ref[...] += nn(zs[...].astype(F32).T.astype(BF16), gtriple)
    gz = nt(gtriple, wq_ref[...]).astype(BF16).astype(F32)
    gg1_ref[...] += column_sum(gz * n1s[...])
    gb1_ref[...] += column_sum(gz)
    resw[...] = x1s[...] + norm_pull(gz * g1_ref[...], n1s[...], scale_one)
    from_windows(resw, gx_ref, 3)

    @pl.when(step == pl.num_programs(0) - 1)
    def _():
        for grad, (first, slabs, rows) in zip((gwq_ref, gwp_ref, gwu_ref), slab_plan()):
            for j in range(slabs):
                gwire_ref[first + j * rows : first + (j + 1) * rows, :] = grad[:, j * 128 : j * 128 + 128].astype(BF16)
        first, slabs, rows = slab_plan()[3]
        for j in range(slabs):
            gwire_ref[first + j * rows : first + (j + 1) * rows, :] = gwdt_ref[j * 128 : j * 128 + 128, :].T.astype(BF16)
        pieces = [ref[:, j * 128 : j * 128 + 128] for ref in vector_grads for j in range(ref.shape[1] // 128)]
        spare = gwire_ref.shape[0] - SMALL_START - len(pieces)
        pieces.append(jnp.zeros((spare, 128), F32))
        gwire_ref[SMALL_START:, :] = jnp.concatenate(pieces, axis=0).astype(BF16)

        def finish(image, _):
            for kind in range(2):
                halo_copy(kind, image).wait_send()
            for kind in range(2, 4):
                halo_copy(kind, image).wait()
            outh_ref[image] = back_in[0, image]
            gxh_ref[image] = back_in[1, image]
            return 0

        lax.fori_loop(0, fetched.shape[1], finish, 0)


def run_block(cols, keep, x, dy, bias, wire, strips):
    samples, rows, columns, _ = x.shape
    wide = columns // WIN
    tokens = wide * CELLS

    def per_image(array):
        return pl.BlockSpec((1,) + array.shape[1:], lambda i: (i, 0, 0, 0))

    def whole(shape):
        return pl.BlockSpec(shape, lambda i: (0,) * len(shape))

    smem = pl.BlockSpec(memory_space=pltpu.SMEM)
    vmem = pl.BlockSpec(memory_space=pltpu.VMEM)
    hbm = pl.BlockSpec(memory_space=pl.ANY)
    full = jax.ShapeDtypeStruct(x.shape, F32)
    halo = (samples, SHIFT, columns, C)
    part = jax.ShapeDtypeStruct(halo, BF16)
    sums = (GROUPS, CELLS, GROUP_HEADS * LANES)
    vectors = [3 * C, C, FF, C, C, C, C, C]
    return pl.pallas_call(
        lambda *refs: block_kernel(strips, *refs),
        grid=(samples,),
        in_specs=[smem, smem, per_image(x), per_image(dy), hbm, hbm, whole(bias.shape), whole(wire.shape)],
        out_specs=[per_image(x), per_image(x), vmem, vmem, whole(wire.shape), whole(sums)],
        out_shape=[full, full, part, part, jax.ShapeDtypeStruct(wire.shape, BF16), jax.ShapeDtypeStruct(sums, F32)],
        scratch_shapes=[
            pltpu.VMEM((2,) + halo, F32),
            pltpu.VMEM((2,) + halo, BF16),
            pltpu.VMEM((2,) + halo, BF16),
            pltpu.VMEM((2,) + halo, BF16),
            pltpu.VMEM((2,) + halo, BF16),
            pltpu.SemaphoreType.DMA((2,)),
            pltpu.SemaphoreType.DMA((4, samples)),
            pltpu.SemaphoreType.DMA((4, samples)),
        ]
        + [pltpu.VMEM(s, BF16) for s in ((C, 3 * C), (C, C), (C, FF), (FF, C))]
        + [pltpu.VMEM((1, size), F32) for size in vectors]
        + [pltpu.VMEM(s, F32) for s in ((C, 3 * C), (C, C), (C, FF), (C, FF))]
        + [pltpu.VMEM((1, size), F32) for size in vectors]
        + [
            pltpu.VMEM((C // 128, WIN, columns + 16, 128), F32),
            pltpu.VMEM((tokens, C), F32),
            pltpu.VMEM((tokens, C), F32),
            pltpu.VMEM((tokens, C), F32),
            pltpu.VMEM((tokens, C), BF16),
            pltpu.VMEM((wide, LANES, 3 * C), BF16),
            pltpu.VMEM((wide, GROUPS, CELLS, GROUP_HEADS * LANES), F32),
            pltpu.VMEM((tokens, C), F32),
            pltpu.VMEM((tokens, C), F32),
            pltpu.VMEM((tokens, C), F32),
            pltpu.VMEM((tokens, C), BF16),
            pltpu.VMEM((tokens, C), BF16),
            pltpu.VMEM((tokens, C), F32),
            pltpu.VMEM((tokens, C), F32),
            pltpu.VMEM((wide, LANES, C), BF16),
            pltpu.VMEM((tokens, 3 * C), F32),
            pltpu.VMEM((tokens, C), F32),
            pltpu.VMEM((C, tokens), BF16),
            pltpu.VMEM((C, tokens), BF16),
        ],
        compiler_params=pltpu.CompilerParams(vmem_limit_bytes=60 * 1024 * 1024, collective_id=1, has_side_effects=True),
        name="block",
    )(cols, keep, x, dy, x, dy, bias, wire)


SMALL_START = 3 * C * C // 128 + C * C // 128 + 2 * C * FF // 128
SMALL_SPAN = 64
WIRE_ROWS = SMALL_START + 3 * SMALL_SPAN


def slab_plan():
    return [
        (0, 3 * C // 128, C),
        (3 * C * C // 128, C // 128, C),
        (4 * C * C // 128, FF // 128, C),
        (4 * C * C // 128 + C * FF // 128, C // 128, FF),
    ]


def wire_rows(device_count):
    unit = 4 * device_count * 16
    return -(-WIRE_ROWS // unit) * unit


def split_three(values):
    high = values.astype(BF16)
    rest = values - high.astype(F32)
    middle = rest.astype(BF16)
    return high, middle, (rest - middle.astype(F32)).astype(BF16)


def dispatch_kernel(me_ref, owner_ref, master_ref, out_ref, rank_ref, start_ref, padded, packed, start_s, sem):
    blocks = owner_ref.shape[0]
    capacity = master_ref.shape[0]
    mine = (owner_ref[...] == me_ref[0]).astype(F32)
    low = mine.astype(BF16)
    row = lax.broadcasted_iota(jnp.int32, (128, 128), 0)
    col = lax.broadcasted_iota(jnp.int32, (128, 128), 1)
    within = nn(low, (row <= col).astype(F32).astype(BF16))
    sums = nn(low, jnp.ones((128, 128), BF16))
    below = lax.broadcasted_iota(jnp.int32, (blocks, blocks), 1) < lax.broadcasted_iota(jnp.int32, (blocks, blocks), 0)
    start = nn(below.astype(F32).astype(BF16), sums.astype(BF16))
    rank_ref[...] = jnp.where(mine > 0, within - 1.0, -1.0)
    start_ref[...] = start.astype(jnp.int32)
    copy = pltpu.make_async_copy(start_ref, start_s, sem)
    copy.start()
    padded[...] = jnp.zeros_like(padded)
    padded[0:capacity, :] = master_ref[...]
    out_ref[...] = jnp.zeros_like(out_ref)
    copy.wait()
    slot = row.astype(F32)

    def block(b, _):
        hot = (slot == rank_ref[pl.ds(b, 1), :]).astype(F32).astype(BF16)
        rows = padded[pl.ds(start_s[b, 0], 128), :].astype(BF16)
        packed[pl.ds(pl.multiple_of(b * 128, 128), 128), :] = tn(hot, rows)
        return 0

    small = SMALL_START // 128
    lax.fori_loop(0, small, block, 0, unroll=4)
    hot = (slot == rank_ref[small : small + 1, :]).astype(F32).astype(BF16)
    for i, piece in enumerate(split_three(padded[pl.ds(start_s[small, 0], 128), :])):
        first = SMALL_START + i * SMALL_SPAN
        out_ref[first : first + SMALL_SPAN, :] = tn(hot, piece)[0:SMALL_SPAN].astype(BF16)
    for first, slabs, rows in slab_plan():
        for j in range(slabs):
            out_ref[first + j * rows : first + (j + 1) * rows, :] = packed[
                pl.ds(first + j, rows, stride=slabs), :
            ].astype(BF16)


def run_dispatch(me, owners, master, wire):
    blocks = owners.shape[0]
    vmem = pl.BlockSpec(memory_space=pltpu.VMEM)
    return pl.pallas_call(
        dispatch_kernel,
        in_specs=[pl.BlockSpec(memory_space=pltpu.SMEM), vmem, vmem],
        out_specs=[vmem] * 3,
        out_shape=[
            jax.ShapeDtypeStruct((wire, 128), BF16),
            jax.ShapeDtypeStruct((blocks, 128), F32),
            jax.ShapeDtypeStruct((blocks, 128), jnp.int32),
        ],
        scratch_shapes=[
            pltpu.VMEM((-(-(master.shape[0] + 128) // 8) * 8, 128), F32),
            pltpu.VMEM((SMALL_START, 128), F32),
            pltpu.SMEM((blocks, 128), jnp.int32),
            pltpu.SemaphoreType.DMA,
        ],
        compiler_params=pltpu.CompilerParams(vmem_limit_bytes=40 * 1024 * 1024),
        name="dispatch",
    )(me, owners, master)


def collect_kernel(start_ref, rank_ref, grad_ref, master_ref, first_ref, second_ref,
                   first_out, second_out, master_out, packed, total):
    capacity = master_ref.shape[0]
    total[...] = jnp.zeros_like(total)
    for first, slabs, rows in slab_plan():
        for j in range(slabs):
            packed[pl.ds(first + j, rows, stride=slabs), :] = grad_ref[
                first + j * rows : first + (j + 1) * rows, :
            ].astype(F32)
    packed[SMALL_START : SMALL_START + SMALL_SPAN, :] = grad_ref[SMALL_START : SMALL_START + SMALL_SPAN, :].astype(F32)
    packed[SMALL_START + SMALL_SPAN : SMALL_START + 128, :] = jnp.zeros((128 - SMALL_SPAN, 128), F32)
    slot = lax.broadcasted_iota(jnp.int32, (128, 128), 0).astype(F32)

    def block(b, _):
        hot = (slot == rank_ref[pl.ds(b, 1), :]).astype(F32).astype(BF16)
        part = nn(hot, packed[pl.ds(pl.multiple_of(b * 128, 128), 128), :].astype(BF16))
        where = pl.ds(start_ref[b, 0], 128)
        total[where, :] = total[where, :] + part
        return 0

    lax.fori_loop(0, SMALL_START // 128 + 1, block, 0)
    slots = lax.broadcasted_iota(jnp.int32, (capacity, 1), 0)
    edges = [edge // 128 for edge in row_edges()[:4]] + [SMALL_START // 128 + 1]
    rates = [2.0 / math.sqrt(C), 2.0 / math.sqrt(C // 8), 2.0 / math.sqrt(C), 2.0 / math.sqrt(FF), 1.0, 0.0]
    rate = jnp.full((capacity, 1), rates[0], F32)
    for edge, amount in zip(edges, rates[1:]):
        rate = jnp.where(slots >= start_ref[edge, 0], amount, rate)
    decay = jnp.where(slots < start_ref[edges[3], 0], DECAY, 0.0)
    grads = total[0:capacity, :]
    weights = master_ref[...]
    first = BETA_ONE * first_ref[...] + (1.0 - BETA_ONE) * grads
    second = BETA_TWO * second_ref[...] + (1.0 - BETA_TWO) * grads * grads
    first_out[...] = first
    second_out[...] = second
    first_hat = first / (1.0 - BETA_ONE**STEP)
    second_hat = second / (1.0 - BETA_TWO**STEP)
    master_out[...] = weights - rate * (first_hat / (jnp.sqrt(second_hat) + ADAM_EPS) + decay * weights)


def run_collect(starts, ranks, grads, master, first, second):
    vmem = pl.BlockSpec(memory_space=pltpu.VMEM)
    return pl.pallas_call(
        collect_kernel,
        in_specs=[pl.BlockSpec(memory_space=pltpu.SMEM)] + [vmem] * 5,
        out_specs=[vmem] * 3,
        out_shape=[jax.ShapeDtypeStruct(master.shape, F32)] * 3,
        scratch_shapes=[
            pltpu.VMEM((SMALL_START + 128, 128), F32),
            pltpu.VMEM((-(-(master.shape[0] + 128) // 8) * 8, 128), F32),
        ],
        compiler_params=pltpu.CompilerParams(vmem_limit_bytes=40 * 1024 * 1024),
        name="collect",
    )(starts, ranks, grads, master, first, second)


def reduce_parts(strips, buckets, rows, orders):
    sizes = {"z": strips // 2, "y": 2, "x": buckets // 2}
    length = rows // 2 // len(orders)
    parts = []
    for order in orders:
        levels, share = [], length
        for axis in order:
            share = share // sizes[axis]
            levels.append((axis, sizes[axis], share))
        parts.append((length, levels))
    return parts


def all_reduce_kernel(strips, buckets, parts, in_ref, out_ref, *scratch):
    strip, bucket = lax.axis_index("strip"), lax.axis_index("bucket")
    sizes = {"z": strips // 2, "y": 2, "x": buckets // 2, "core": 2}
    mine = {"z": strip // 2, "y": strip % 2, "x": bucket // 2, "core": bucket % 2}
    send_sems, recv_sems = scratch[-2:]
    buffers = list(scratch[:-2])

    def peer(axis, offset):
        return lax.rem(mine[axis] + offset, sizes[axis])

    def device(axis, offset):
        place = dict(mine)
        place[axis] = peer(axis, offset)
        return (place["z"] * 2 + place["y"], place["x"] * 2 + place["core"])

    barrier = pltpu.get_barrier_semaphore()
    partners = [(axis, offset) for axis, size in sizes.items() for offset in range(1, size)]
    for axis, offset in partners:
        pl.semaphore_signal(barrier, inc=1, device_id=device(axis, offset), device_id_type=pl.DeviceIdType.MESH)
    pl.semaphore_wait(barrier, len(partners))

    used = [0]

    def send(source, target, axis, offset):
        at = used[0]
        used[0] += 1
        copy = pltpu.make_async_remote_copy(
            src_ref=source, dst_ref=target, send_sem=send_sems.at[at], recv_sem=recv_sems.at[at],
            device_id=device(axis, offset), device_id_type=pl.DeviceIdType.MESH,
        )
        copy.start()
        return copy

    def span(start, length):
        return pl.ds(pl.multiple_of(start, 16), length)

    half = in_ref.shape[0] // 2

    def part_steps(p, length, levels):
        core_in, core_sum = buffers.pop(0), buffers.pop(0)
        boxes = [(buffers.pop(0), buffers.pop(0)) for _ in levels]
        own = mine["core"] * half + p * length
        other = (1 - mine["core"]) * half + p * length
        copy = send(in_ref.at[span(other, length)], core_in, "core", 1)
        yield
        copy.wait()
        core_sum[...] = in_ref[span(own, length), :] + core_in[...]
        held, spans = core_sum, [(own, length)]
        for (axis, size, share), (inbox, total) in zip(levels, boxes):
            copies = [
                send(held.at[span(peer(axis, offset) * share, share)],
                     inbox.at[pl.ds((offset - 1) * share, share)], axis, offset)
                for offset in range(1, size)
            ]
            yield
            for copy in copies:
                copy.wait()
            value = held[span(mine[axis] * share, share), :].astype(F32)
            for offset in range(1, size):
                value = value + inbox[(offset - 1) * share : offset * share, :].astype(F32)
            spans.append((spans[-1][0] + mine[axis] * share, share))
            total[...] = value.astype(BF16)
            held = total
        start, share = spans[-1]
        out_ref[span(start, share), :] = held[...]
        for (axis, size, share), (start, _) in zip(levels[::-1], spans[:0:-1]):
            region = out_ref.at[span(start, share)]
            copies = [send(region, region, axis, offset) for offset in range(1, size)]
            yield
            for copy in copies:
                copy.wait()
        region = out_ref.at[span(own, length)]
        copy = send(region, region, "core", 1)
        yield
        copy.wait()

    running = [part_steps(p, length, levels) for p, (length, levels) in enumerate(parts)]
    waiting, active = running, []
    while waiting or active:
        active, waiting = active + waiting[:2], waiting[2:]
        for steps in list(active):
            if next(steps, steps) is steps:
                active.remove(steps)


def all_reduce(values, strips, buckets, orders):
    rows = values.shape[0]
    parts = reduce_parts(strips, buckets, rows, orders)
    vmem = pl.BlockSpec(memory_space=pltpu.VMEM)
    shapes, copies = [], 0
    for length, levels in parts:
        shapes += [(length, 128), (length, 128)]
        for _, size, share in levels:
            shapes += [((size - 1) * share, 128), (share, 128)]
        copies += 2 + 2 * sum(size - 1 for _, size, _ in levels)
    return pl.pallas_call(
        lambda *refs: all_reduce_kernel(strips, buckets, parts, *refs),
        in_specs=[vmem],
        out_specs=vmem,
        out_shape=jax.ShapeDtypeStruct(values.shape, BF16),
        scratch_shapes=[pltpu.VMEM(shape, BF16) for shape in shapes]
        + [pltpu.SemaphoreType.DMA((copies,)), pltpu.SemaphoreType.DMA((copies,))],
        compiler_params=pltpu.CompilerParams(
            vmem_limit_bytes=40 * 1024 * 1024, collective_id=0, has_side_effects=True
        ),
        name="all_reduce",
    )(values)


ORDERS = (("x", "y", "z"), ("y", "x", "z")) * 2


def shards(
    block_input, cotangent, window_cols, keep_mask, owner_list, master, first_moment, second_moment
):
    strips = lax.axis_size("strip")
    buckets = lax.axis_size("bucket")
    wire_total = wire_rows(strips * buckets)
    my_index = lax.axis_index(("strip", "bucket")).astype(jnp.int32).reshape(1)
    blocks = -(-(SMALL_START // 128 + 2) // 8) * 8
    owners = jnp.pad(owner_list, (0, blocks * 128 - owner_list.shape[0]), constant_values=-1).reshape(blocks, 128)
    sparse, ranks, starts = run_dispatch(my_index, owners, master, wire_total)
    wire = all_reduce(sparse, strips, buckets, ORDERS)
    small = [wire[SMALL_START + i * SMALL_SPAN : SMALL_START + (i + 1) * SMALL_SPAN].astype(F32) for i in range(3)]
    pairs = (2 * WIN - 1) ** 2
    table = (small[0] + small[1] + small[2])[SMALL_ROWS : SMALL_ROWS + TABLE_ROWS].reshape(-1)
    table = table[: pairs * HEADS].reshape(pairs, HEADS)
    bias = attention_bias(table, lax.axis_index("strip") == strips - 1)
    keep = keep_mask.astype(F32) / KEEP_PROB
    output, grad_input, output_halo, grad_halo, grad_wire, pair_sums = run_block(
        window_cols, keep, block_input, cotangent, bias, wire, strips
    )
    pair_sums = pair_sums.reshape(GROUPS, CELLS, GROUP_HEADS, LANES).transpose(0, 2, 1, 3)
    grad_table = lax.dot_general(
        pair_onehot(), pair_sums.reshape(HEADS, -1), (((0,), (1,)), ((), ())),
        precision=PRECISE, preferred_element_type=F32,
    ).reshape(-1)
    grad_table = jnp.pad(grad_table, (0, TABLE_ROWS * 128 - pairs * HEADS)).reshape(TABLE_ROWS, 128)
    grad_wire = lax.dynamic_update_slice(grad_wire, grad_table.astype(BF16), (SMALL_START + SMALL_ROWS, 0))
    output = output.at[:, :SHIFT].set(output_halo.astype(F32))
    grad_input = grad_input.at[:, :SHIFT].set(grad_halo.astype(F32))
    grads = all_reduce(grad_wire, strips, buckets, ORDERS)
    first, second_new, new_weights = run_collect(starts, ranks, grads, master, first_moment, second_moment)
    return (output, grad_input, first, second_new, new_weights)


def solution(mesh):
    in_specs = (
        P("bucket", "strip", None, None),
        P("bucket", "strip", None, None),
        P("bucket"),
        P("bucket", None),
        P(),
        P(("strip", "bucket"), None),
        P(("strip", "bucket"), None),
        P(("strip", "bucket"), None),
    )
    out_specs = (
        P("bucket", "strip", None, None),
        P("bucket", "strip", None, None),
        P(("strip", "bucket"), None),
        P(("strip", "bucket"), None),
        P(("strip", "bucket"), None),
    )
    return jax.shard_map(shards, mesh=mesh, in_specs=in_specs, out_specs=out_specs, check_vma=False)
```

```python
import functools
import math

import jax
import jax.numpy as jnp
from jax import lax
from jax.experimental import pallas as pl
from jax.experimental.pallas import tpu as pltpu
from jax.sharding import PartitionSpec as P

C = 384
HEADS = 12
HD = 32
FF = 1536
WIN = 7
SHIFT = 3
STEP = 10
SMALL_ROWS = 39
TABLE_ROWS = 16


PRECISE = lax.Precision.HIGHEST
NORM_EPS = 1e-05
KEEP_PROB = 0.8
MASK_FILL = -100.0
BETA_ONE = 0.5
BETA_TWO = 0.5
ADAM_EPS = 1e-08
DECAY = 0.05


def row_edges():
    first = 3 * C * C // 128
    second = first + C * C // 128
    third = second + C * FF // 128
    fourth = third + FF * C // 128
    fifth = fourth + SMALL_ROWS
    return [first, second, third, fourth, fifth]


GROUPS = 3
GROUP_HEADS = HEADS // GROUPS
CELLS = WIN * 8
LANES = 64
LOG2E = math.log2(math.e)
F32 = jnp.float32
BF16 = jnp.bfloat16


def nn(left, right):
    return lax.dot_general(left, right, (((1,), (0,)), ((), ())), preferred_element_type=F32)


def nt(left, right):
    return lax.dot_general(left, right, (((1,), (1,)), ((), ())), preferred_element_type=F32)


def tn(left, right):
    return lax.dot_general(left, right, (((0,), (0,)), ((), ())), preferred_element_type=F32)


def gelu_pair(u):
    normal = 0.5 + 0.5 * lax.erf(u * math.sqrt(0.5))
    gauss = jnp.exp2(u * u * (-0.5 * LOG2E))
    return u * normal, normal + u * gauss * (1.0 / math.sqrt(2.0 * math.pi))


def row_norm(values):
    center = values - jnp.mean(values, axis=-1, keepdims=True)
    scale = lax.rsqrt(jnp.mean(center * center, axis=-1, keepdims=True) + NORM_EPS)
    return center * scale, scale


def norm_pull(grad, normal, scale):
    first = jnp.mean(grad, axis=-1, keepdims=True)
    second = jnp.mean(grad * normal, axis=-1, keepdims=True)
    return scale * (grad - first - normal * second)


def column_sum(values):
    return jnp.sum(values, axis=0, keepdims=True)


SMALL_START = 3 * C * C // 128 + C * C // 128 + 2 * C * FF // 128
SMALL_SPAN = 64


def slab_plan():
    return [
        (0, 3 * C // 128, C),
        (3 * C * C // 128, C // 128, C),
        (4 * C * C // 128, FF // 128, C),
        (4 * C * C // 128 + C * FF // 128, C // 128, FF),
    ]


ORDERS = (("x", "y", "z"), ("y", "x", "z")) * 2
LAG = 2
FIRST_ROWS = 3 * C * C // 128


def split_three(values):
    high = values.astype(BF16)
    rest = values - high.astype(F32)
    middle = rest.astype(BF16)
    return high, middle, (rest - middle.astype(F32)).astype(BF16)


def wire_rows(rows, strips, buckets):
    unit = 16 * strips * buckets
    return -(-rows // unit) * unit


def reduce_plan(strips, buckets, rows, orders):
    sizes = {"z": strips // 2, "y": 2, "x": buckets // 2}
    unit = 8 * strips * buckets
    units = rows // 2 // unit
    orders = orders[:units]
    parts, first = [], 0
    for p, order in enumerate(orders):
        length = (units // len(orders) + (p < units % len(orders))) * unit
        levels, share = [], length
        for axis in order:
            share = share // sizes[axis]
            levels.append((axis, sizes[axis], share))
        parts.append((first, length, levels))
        first += length
    return parts


def reduce_scratch(plan):
    shapes, copies = [], 0
    for _, length, levels in plan:
        shapes += [(length, 128), (length, 128)]
        for _, size, share in levels:
            shapes += [((size - 1) * share, 128), (share, 128)]
        copies += 2 + 2 * sum(size - 1 for _, size, _ in levels)
    return [pltpu.VMEM(shape, BF16) for shape in shapes] + [
        pltpu.SemaphoreType.DMA((copies,)), pltpu.SemaphoreType.DMA((copies,))
    ]


class Place:
    def __init__(self, strips, buckets):
        strip, bucket = lax.axis_index("strip"), lax.axis_index("bucket")
        self.sizes = {"z": strips // 2, "y": 2, "x": buckets // 2, "core": 2}
        self.mine = {"z": strip // 2, "y": strip % 2, "x": bucket // 2, "core": bucket % 2}
        self.above = (lax.rem(strip + strips - 1, strips), bucket)
        self.below = (lax.rem(strip + 1, strips), bucket)

    def peer(self, axis, offset):
        return lax.rem(self.mine[axis] + offset, self.sizes[axis])

    def device(self, axis, offset):
        place = dict(self.mine)
        place[axis] = self.peer(axis, offset)
        return (place["z"] * 2 + place["y"], place["x"] * 2 + place["core"])

    def greet(self, halos):
        barrier = pltpu.get_barrier_semaphore()
        partners = [self.device(axis, offset) for axis, size in self.sizes.items() for offset in range(1, size)]
        partners += [self.above, self.below] if halos else []
        for partner in partners:
            pl.semaphore_signal(barrier, inc=1, device_id=partner, device_id_type=pl.DeviceIdType.MESH)
        pl.semaphore_wait(barrier, len(partners))


def reduce_stages(place, plan, wire, scratch):
    buffers, send_sems, recv_sems = list(scratch[:-2]), scratch[-2], scratch[-1]
    half = wire.shape[0] // 2
    counter = [0]

    def span(start, length):
        return pl.ds(pl.multiple_of(start, 16), length)

    def copies_of(count):
        first = counter[0]
        counter[0] += count
        return first

    def copy(at, source, target, axis, offset):
        return pltpu.make_async_remote_copy(
            src_ref=source, dst_ref=target, send_sem=send_sems.at[at], recv_sem=recv_sems.at[at],
            device_id=place.device(axis, offset), device_id_type=pl.DeviceIdType.MESH,
        )

    def part_stages(first, length, levels):
        core_in, core_sum = buffers.pop(0), buffers.pop(0)
        boxes = [(buffers.pop(0), buffers.pop(0)) for _ in levels]
        held = [core_sum] + [total for _, total in boxes]

        def own():
            return place.mine["core"] * half + first

        def start_of(level):
            start = own()
            for axis, _, share in levels[:level]:
                start = start + place.mine[axis] * share
            return start

        core_at, back_at = copies_of(1), copies_of(1)
        down_at = [copies_of(size - 1) for _, size, _ in levels]
        up_at = [copies_of(size - 1) for _, size, _ in levels]

        def core_out():
            other = (1 - place.mine["core"]) * half + first
            return [copy(core_at, wire.at[span(other, length)], core_in, "core", 1)]

        def down(level):
            axis, size, share = levels[level]
            inbox = boxes[level][0]
            return [
                copy(down_at[level] + offset - 1, held[level].at[span(place.peer(axis, offset) * share, share)],
                     inbox.at[pl.ds((offset - 1) * share, share)], axis, offset)
                for offset in range(1, size)
            ]

        def up(level):
            axis, size, share = levels[level]
            region = wire.at[span(start_of(level + 1), share)]
            return [copy(up_at[level] + offset - 1, region, region, axis, offset) for offset in range(1, size)]

        def core_back():
            region = wire.at[span(own(), length)]
            return [copy(back_at, region, region, "core", 1)]

        def add_core():
            core_sum[...] = wire[span(own(), length), :] + core_in[...]

        def add(level):
            axis, size, share = levels[level]
            inbox, total = boxes[level]
            value = held[level][span(place.mine[axis] * share, share), :].astype(F32)
            for offset in range(1, size):
                value = value + inbox[(offset - 1) * share : offset * share, :].astype(F32)
            if level + 1 < len(levels):
                total[...] = value.astype(BF16)
            else:
                wire[span(start_of(len(levels)), share), :] = value.astype(BF16)

        count = len(levels)
        moves = [core_out] + [functools.partial(down, level) for level in range(count)]
        moves += [functools.partial(up, level) for level in reversed(range(count))] + [core_back]
        work = {1: add_core}
        for level in range(count):
            work[level + 2] = functools.partial(add, level)

        def stage(index):
            if index > 0:
                for one in moves[index - 1]():
                    one.wait()
            if index in work:
                work[index]()
            if index < len(moves):
                for one in moves[index]():
                    one.start()

        return [functools.partial(stage, index) for index in range(len(moves) + 1)]

    return [part_stages(*part) for part in plan]


def reduce_ticks(parts):
    ticks = []
    for p, stages in enumerate(parts):
        for index, stage in enumerate(stages):
            at = index + p // 2
            while len(ticks) <= at:
                ticks.append([])
            ticks[at].append(stage)

    def run(tick):
        for stage in tick:
            stage()

    return [functools.partial(run, tick) for tick in ticks]


def tick_slots(ticks, slots):
    return [[tick for i, tick in enumerate(ticks) if i * slots // len(ticks) == slot] for slot in range(slots)]


def head_bits():
    lane_head = lax.broadcasted_iota(jnp.int32, (1, 128), 1) // HD
    return [(lane_head == h).astype(F32).astype(BF16) for h in range(GROUP_HEADS)]


def stack_of(part, bits):
    return jnp.concatenate([part * bit for bit in bits], axis=0)


def unstack(part):
    lane_head = lax.broadcasted_iota(jnp.int32, (1, 128), 1) // HD
    total = None
    for h in range(GROUP_HEADS):
        piece = jnp.where(lane_head == h, part[h * LANES : h * LANES + CELLS], 0.0)
        total = piece if total is None else total + piece
    return total


def load_matrix(target, wire, first, rows):
    for j in range(target.shape[1] // 128):
        target[:, j * 128 : j * 128 + 128] = wire[first + j * rows : first + (j + 1) * rows, :]


def load_vectors(refs, wire, first):
    small = jnp.zeros((SMALL_SPAN, 128), F32)
    for i in range(3):
        small = small + wire[FIRST_ROWS + i * SMALL_SPAN : FIRST_ROWS + (i + 1) * SMALL_SPAN, :].astype(F32)
    for ref, row in zip(refs, first):
        for j in range(ref.shape[1] // 128):
            ref[:, j * 128 : j * 128 + 128] = small[row + j : row + j + 1]


def to_windows(line, last, main, halo, step, target):
    slabs, columns = C // 128, main.shape[2]
    wide, own = columns // WIN, WIN - SHIFT
    wrapped_row = lax.broadcasted_iota(jnp.int32, (8, 128), 0) >= own
    for a in range(WIN):
        row = main[0, SHIFT + a] if a < own else halo[step, a - own].astype(F32)
        for s in range(slabs):
            line[s, a, 8 : 8 + columns, :] = row[:, s * 128 : s * 128 + 128]
    for a in range(WIN):
        for s in range(slabs):
            front = line[s, a, 8 - own : 16 - own, :]
            for w in range(wide):
                first = 8 + w * WIN + SHIFT
                tile = jnp.where(wrapped_row & (w == last), front, line[s, a, first : first + 8, :])
                target[w * CELLS + a * 8 : w * CELLS + a * 8 + 8, s * 128 : s * 128 + 128] = tile


def from_windows(line, width, source, main, halo, step):
    slabs, columns = C // 128, main.shape[2]
    wide, own = columns // WIN, WIN - SHIFT
    for w in range(wide):
        for a in range(WIN):
            for s in range(slabs):
                first = 8 + w * WIN + SHIFT
                line[s, a, first : first + 8, :] = source[
                    w * CELLS + a * 8 : w * CELLS + a * 8 + 8, s * 128 : s * 128 + 128
                ]
    kept = lax.broadcasted_iota(jnp.int32, (columns, 128), 0) < width
    front = lax.broadcasted_iota(jnp.int32, (8, 128), 0) < SHIFT
    for a in range(WIN):
        for s in range(slabs):
            wrapped = line[s, a, pl.ds(width + 8, 8), :]
            line[s, a, 8:16, :] = jnp.where(front, wrapped, line[s, a, 8:16, :])
            row = jnp.where(kept, line[s, a, 8 : 8 + columns, :], 0.0)
            if a < own:
                main[0, a, :, s * 128 : s * 128 + 128] = row
            else:
                halo[step, a - own, :, s * 128 : s * 128 + 128] = row.astype(BF16)


def place_onehot(row):
    shape = (128, HEADS * LANES)
    source = lax.broadcasted_iota(jnp.int32, shape, 0)
    lane = lax.broadcasted_iota(jnp.int32, shape, 1)
    return (lane == source // 8 * LANES + row * 8 + source % 8).astype(F32).astype(BF16)


def offset_onehot(column):
    shape = (256, 128)
    source = lax.broadcasted_iota(jnp.int32, shape, 0)
    lane = lax.broadcasted_iota(jnp.int32, shape, 1)
    wanted = (lane % 8 - column + WIN - 1) * HEADS + lane // 8
    return ((source == wanted) & (lane < HEADS * 8)).astype(F32).astype(BF16)


SPAN = 2 * WIN - 1


def build_bias(raw, last_strip, offsets, spread, bias):
    flat = jnp.concatenate([raw[r : r + 1] for r in range(TABLE_ROWS)], axis=1)
    offsets[...] = jnp.zeros_like(offsets)
    spread[...] = jnp.zeros_like(spread)
    for d in range(SPAN):
        offsets[SPAN - 1 - d : SPAN - d, 0 : SPAN * HEADS] = flat[:, d * SPAN * HEADS : (d + 1) * SPAN * HEADS]
    terms = split_three(offsets[...])
    for column in range(WIN):
        pick = offset_onehot(column)
        part = nn(terms[0], pick) + nn(terms[1], pick) + nn(terms[2], pick)
        spread[pl.ds(column, SPAN, stride=8), :] = part[0:SPAN]
    terms = split_three(spread[...])
    total = jnp.zeros((CELLS, HEADS * LANES), F32)
    for row in range(WIN):
        pick = place_onehot(row)
        for term in terms:
            total = total + nn(term[8 * (WIN - 1 - row) : 8 * (WIN - 1 - row) + CELLS], pick)
    shape = (CELLS, HEADS * LANES)
    key = lax.broadcasted_iota(jnp.int32, shape, 0)
    query = lax.broadcasted_iota(jnp.int32, shape, 1) % LANES
    edge = WIN - SHIFT
    by_row = ((key // 8 >= edge) != (query // 8 >= edge)) & last_strip
    by_col = (key % 8 >= edge) != (query % 8 >= edge)
    for variant, masked in enumerate((by_row, by_row | by_col)):
        value = (total + jnp.where(masked, MASK_FILL, 0.0)) * LOG2E
        value = jnp.where(key % 8 < WIN, value, -1e30)
        for g in range(GROUPS):
            bias[variant, g] = value[:, g * GROUP_HEADS * LANES : (g + 1) * GROUP_HEADS * LANES]


def pull_bias(sums, spread):
    grads = jnp.concatenate([sums[g] for g in range(GROUPS)], axis=1)
    high, middle, _ = split_three(grads)
    spread[...] = jnp.zeros_like(spread)
    for row in range(WIN):
        pick = place_onehot(row)
        first = 8 * (WIN - 1 - row)
        spread[first : first + CELLS, :] += nt(high, pick) + nt(middle, pick)
    total = jnp.zeros((SPAN, 256), F32)
    for column in range(WIN):
        pick = offset_onehot(column)
        high, middle, _ = split_three(spread[pl.ds(column, SPAN, stride=8), :])
        total = total + nt(high, pick) + nt(middle, pick)
    flat = [total[SPAN - 1 - d : SPAN - d, 0 : SPAN * HEADS] for d in range(SPAN)]
    flat.append(jnp.zeros((1, TABLE_ROWS * 128 - SPAN * SPAN * HEADS), F32))
    flat = jnp.concatenate(flat, axis=1)
    return jnp.concatenate([flat[:, r * 128 : r * 128 + 128] for r in range(TABLE_ROWS)], axis=0)


def block_kernel(
    strips, buckets, images, plan_one, plan_two,
    cols_ref, keep_ref, x_ref, dy_ref, x_any, dy_any, one_any, two_any,
    out_ref, gx_ref, outh_any, gxh_any, gone_any, gtwo_any,
    wq_ref, wp_ref, wu_ref, wd_ref, bq_ref, bp_ref, bu_ref, bd_ref, g1_ref, b1_ref, g2_ref, b2_ref,
    gwq_ref, gwp_ref, gwu_ref, gwdt_ref, gbq_ref, gbp_ref, gbu_ref, gbd_ref, gg1_ref, gb1_ref, gg2_ref, gb2_ref,
    bias, gs_ref, offsets, spread,
    xw, zs, qkv, prob, ctx, gctx, gx1s,
    line, dyw, x1s, n2s, h2s, gfs, ys, gh2s, resw, htr, gtr, gscores, gqkv,
    fetched, halo_out, halo_in, back_in, wire_one, wire_two,
    local_sems, send_sems, recv_sems, *scratch,
):
    step = pl.program_id(0)
    tokens = dyw.shape[0]
    wide = tokens // CELLS
    place = Place(strips, buckets)
    last = cols_ref[0] - 1
    width = cols_ref[0] * WIN
    count_one = len(reduce_scratch(plan_one))
    parts_one = reduce_stages(place, plan_one, wire_one, scratch[:count_one])
    parts_two = reduce_stages(place, plan_two, wire_two, scratch[count_one:])
    gather_ticks = reduce_ticks(parts_one + parts_two)
    early = len(parts_one[0])
    one_ticks, two_ticks = reduce_ticks(parts_one), reduce_ticks(parts_two)

    def halo(kind, image):
        return pltpu.make_async_remote_copy(
            src_ref=halo_out.at[kind % 2, image], dst_ref=(halo_in if kind < 2 else back_in).at[kind % 2, image],
            send_sem=send_sems.at[kind, image], recv_sem=recv_sems.at[kind, image],
            device_id=place.above if kind < 2 else place.below, device_id_type=pl.DeviceIdType.MESH,
        )

    def fetch(array, image, kind):
        return pltpu.make_async_copy(array.at[image, pl.ds(0, SHIFT)], fetched.at[kind], local_sems.at[kind])

    def send_rows(kind, image, held):
        halo_out[kind, image] = fetched[held].astype(BF16)
        halo(kind, image).start()

    @pl.when(step == 0)
    def _():
        loads = [
            pltpu.make_async_copy(source, target, local_sems.at[2 + i])
            for i, (source, target) in enumerate(((one_any, wire_one), (two_any, wire_two)))
        ]
        first = [fetch(x_any, image, image) for image in range(2)]
        for copy in loads + first:
            copy.start()
        place.greet(True)
        for copy in loads:
            copy.wait()
        gather_ticks[0]()
        for image in range(2):
            first[image].wait()
            send_rows(0, image, image)
        fetch(x_any, 2, 0).start()
        fetch(dy_any, 0, 1).start()
        line[...] = jnp.zeros_like(line)
        for ref in (gwq_ref, gwp_ref, gwu_ref, gwdt_ref, gbq_ref, gbp_ref, gbu_ref, gbd_ref,
                    gg1_ref, gb1_ref, gg2_ref, gb2_ref, gs_ref, qkv, gctx):
            ref[...] = jnp.zeros_like(ref)
        for tick in gather_ticks[1:early]:
            tick()
        load_matrix(wq_ref, wire_one, 0, C)
        load_vectors((bq_ref, bp_ref, bu_ref, bd_ref, g1_ref, b1_ref, g2_ref, b2_ref), wire_one,
                     (0, 9, 12, 24, 27, 30, 33, 36))
        raw = jnp.zeros((SMALL_SPAN, 128), F32)
        for i in range(3):
            raw = raw + wire_one[FIRST_ROWS + i * SMALL_SPAN : FIRST_ROWS + (i + 1) * SMALL_SPAN, :].astype(F32)
        build_bias(raw[SMALL_ROWS : SMALL_ROWS + TABLE_ROWS], lax.axis_index("strip") == strips - 1, offsets, spread, bias)

    @pl.when((step > 0) & (step + 1 < images))
    def _():
        fetch(x_any, step + 1, 0).wait()
        send_rows(0, step + 1, 0)

    @pl.when((step > 0) & (step + 2 < images))
    def _():
        fetch(x_any, step + 2, 0).start()

    @pl.when((step > 0) & (step - 1 < images))
    def _():
        fetch(dy_any, step - 1, 1).wait()
        send_rows(1, step - 1, 1)

    @pl.when((step > 0) & (step < images))
    def _():
        fetch(dy_any, step, 1).start()

    bits = head_bits()

    def attend(image):
        at = lax.rem(image, LAG)
        halo(0, image).wait_recv()
        to_windows(line, last, x_ref, halo_in.at[0], image, xw.at[at])
        normal, _ = row_norm(xw[at])
        zs[at] = (normal * g1_ref[...] + b1_ref[...]).astype(BF16)
        triple = nn(zs[at], wq_ref[...]) + bq_ref[...]
        for w in range(wide):
            qkv[at, w, 0:CELLS, :] = triple[w * CELLS : w * CELLS + CELLS].astype(BF16)
        for w in range(wide):
            variant = (w == last).astype(jnp.int32)
            for g in range(GROUPS):
                q = qkv[at, w, :, g * 128 : g * 128 + 128]
                k = qkv[at, w, 0:CELLS, C + g * 128 : C + g * 128 + 128]
                v = qkv[at, w, 0:CELLS, 2 * C + g * 128 : 2 * C + g * 128 + 128]
                s = nt(k, stack_of(q, bits)) * (HD ** (-0.5) * LOG2E) + bias[variant, g]
                e = jnp.exp2(s - jnp.max(s, axis=0, keepdims=True))
                a = (e * (1.0 / jnp.sum(e, axis=0, keepdims=True))).astype(BF16)
                prob[at, w, g] = a
                resw[w * CELLS : w * CELLS + CELLS, g * 128 : g * 128 + 128] = unstack(tn(a, v))
        ctx[at] = resw[...].astype(BF16)

    def feed(image):
        at = lax.rem(image, LAG)
        keep_one = keep_ref[image, 0]
        keep_two = keep_ref[image, 1]
        x1 = xw[at] + keep_one * (nn(ctx[at], wp_ref[...]) + bp_ref[...])
        x1s[...] = x1
        normal, scale_two = row_norm(x1)
        n2s[...] = normal
        h2 = (normal * g2_ref[...] + b2_ref[...]).astype(BF16)
        h2s[...] = h2
        htr[...] = h2.astype(F32).T.astype(BF16)

        halo(1, image).wait_recv()
        to_windows(line, last, dy_ref, halo_in.at[1], image, dyw)
        token = lax.broadcasted_iota(jnp.int32, (tokens, 1), 0)
        valid = ((token % 8 < WIN) & (token < cols_ref[0] * CELLS)).astype(F32)
        gy = dyw[...] * valid
        gf = (gy * keep_two).astype(BF16)
        gfs[...] = gf
        gbd_ref[...] += column_sum(gf.astype(F32))
        gtr[...] = gf.astype(F32).T.astype(BF16)
        ys[...] = jnp.zeros_like(ys)
        gh2s[...] = jnp.zeros_like(gh2s)
        chunk = 512
        for j in range(FF // chunk):
            part = slice(j * chunk, (j + 1) * chunk)
            u = nn(h2s[...], wu_ref[:, part]) + bu_ref[:, part]
            gm = nt(gfs[...], wd_ref[part, :])
            m, slope = gelu_pair(u)
            m = m.astype(BF16)
            gu = (gm * slope).astype(BF16)
            ys[...] += nn(m, wd_ref[part, :])
            gwdt_ref[:, part] += nn(gtr[...], m)
            gwu_ref[:, part] += nn(htr[...], gu)
            gbu_ref[:, part] += column_sum(gu.astype(F32))
            gh2s[...] += nt(gu, wu_ref[:, part])

        resw[...] = (x1s[...] + keep_two * (ys[...] + bd_ref[...])) * valid
        halo(1, image).wait_send()
        from_windows(line, width, resw, out_ref, halo_out.at[1], image)
        halo(3, image).start()

        gh2 = gh2s[...]
        gg2_ref[...] += column_sum(gh2 * n2s[...])
        gb2_ref[...] += column_sum(gh2)
        gx1 = dyw[...] * valid + norm_pull(gh2 * g2_ref[...], n2s[...], scale_two)
        gx1s[at] = gx1
        ga = (keep_one * gx1).astype(BF16)
        gbp_ref[...] += column_sum(ga.astype(F32))
        gwp_ref[...] += nn(ctx[at].astype(F32).T.astype(BF16), ga)
        gc = nt(ga, wp_ref[...])
        for w in range(wide):
            gctx[at, w, 0:CELLS, :] = gc[w * CELLS : w * CELLS + CELLS].astype(BF16)

    def pull(image, middle):
        at = lax.rem(image, LAG)
        scale = HD ** (-0.5)
        for w in range(wide):
            rows = slice(w * CELLS, w * CELLS + CELLS)
            for g in range(GROUPS):
                v = qkv[at, w, 0:CELLS, 2 * C + g * 128 : 2 * C + g * 128 + 128]
                gstack = stack_of(gctx[at, w, :, g * 128 : g * 128 + 128], bits)
                low = prob[at, w, g]
                a = low.astype(F32)
                grad = nt(v, gstack)
                inner = jnp.sum(grad * a, axis=0, keepdims=True)
                gscores[w, g] = a * (grad - inner)
                gqkv[rows, 2 * C + g * 128 : 2 * C + g * 128 + 128] = nn(low, gstack)
        middle()
        for w in range(wide):
            rows = slice(w * CELLS, w * CELLS + CELLS)
            for g in range(GROUPS):
                q = qkv[at, w, :, g * 128 : g * 128 + 128]
                k = qkv[at, w, 0:CELLS, C + g * 128 : C + g * 128 + 128]
                gs = gscores[w, g].astype(BF16)
                gqkv[rows, g * 128 : g * 128 + 128] = unstack(tn(gs, k)) * scale
                gqkv[rows, C + g * 128 : C + g * 128 + 128] = nn(gs, stack_of(q, bits)) * scale
        gs_ref[...] += jnp.sum(gscores[...], axis=0)

        gtriple = gqkv[...].astype(BF16)
        gbq_ref[...] += column_sum(gtriple.astype(F32))
        gwq_ref[...] += nn(zs[at].astype(F32).T.astype(BF16), gtriple)
        gz = nt(gtriple, wq_ref[...]).astype(BF16).astype(F32)
        normal, scale_one = row_norm(xw[at])
        gg1_ref[...] += column_sum(gz * normal)
        gb1_ref[...] += column_sum(gz)
        resw[...] = gx1s[at] + norm_pull(gz * g1_ref[...], normal, scale_one)
        halo(0, image).wait_send()
        from_windows(line, width, resw, gx_ref, halo_out.at[0], image)
        halo(2, image).start()

    def pack_two():
        first = 0
        for grad in (gwp_ref, gwu_ref):
            for j in range(grad.shape[1] // 128):
                wire_two[first : first + C, :] = grad[:, j * 128 : j * 128 + 128].astype(BF16)
                first += C
        for j in range(C // 128):
            wire_two[first : first + FF, :] = gwdt_ref[j * 128 : j * 128 + 128, :].T.astype(BF16)
            first += FF
        wire_two[first:, :] = jnp.zeros((wire_two.shape[0] - first, 128), BF16)

    def pack_one():
        for j in range(3 * C // 128):
            wire_one[j * C : (j + 1) * C, :] = gwq_ref[:, j * 128 : j * 128 + 128].astype(BF16)
        vectors = (gbq_ref, gbp_ref, gbu_ref, gbd_ref, gg1_ref, gb1_ref, gg2_ref, gb2_ref)
        pieces = [ref[:, j * 128 : j * 128 + 128] for ref in vectors for j in range(ref.shape[1] // 128)]
        pieces.append(pull_bias(gs_ref, spread))
        pieces.append(jnp.zeros((wire_one.shape[0] - FIRST_ROWS - SMALL_ROWS - TABLE_ROWS, 128), F32))
        wire_one[FIRST_ROWS:, :] = jnp.concatenate(pieces, axis=0).astype(BF16)

    @pl.when(step == LAG)
    def _():
        first = 0
        for ref, rows in ((wp_ref, C), (wu_ref, C), (wd_ref, FF)):
            load_matrix(ref, wire_two, first, rows)
            first += ref.shape[1] // 128 * rows

    @pl.when((step >= LAG) & (step < images + LAG))
    def _():
        feed(step - LAG)

    @pl.when((step >= LAG) & (step < images))
    def _():
        pull(step - LAG, lambda: None)

    @pl.when(step < images)
    def _():
        attend(step)

    late = gather_ticks[early:]
    for k in range(LAG):
        mine = late[k * len(late) // LAG : (k + 1) * len(late) // LAG]

        @pl.when(step == k)
        def _(mine=mine):
            for tick in mine:
                tick()

    @pl.when(step == images + LAG - 1)
    def _():
        pack_two()
        two_ticks[0]()

    for k in range(LAG):

        @pl.when(step == images + LAG + k)
        def _(k=k):
            two_ticks[2 * k + 1]()
            pull(images - LAG + k, two_ticks[2 * k + 2])

    @pl.when(step == images + 2 * LAG - 1)
    def _():
        pack_one()
        rest = two_ticks[2 * LAG + 1 :]
        for i in range(max(len(rest), len(one_ticks))):
            for ticks in (one_ticks, rest):
                if i < len(ticks):
                    ticks[i]()
        for image in range(images):
            for kind in range(2, 4):
                halo(kind, image).wait()
        stores = [
            pltpu.make_async_copy(source, target, local_sems.at[i])
            for i, (source, target) in enumerate(
                ((wire_one, gone_any), (wire_two, gtwo_any), (back_in.at[0], gxh_any), (back_in.at[1], outh_any))
            )
        ]
        for copy in stores:
            copy.start()
        for copy in stores:
            copy.wait()


SMEM_SPEC = pl.BlockSpec(memory_space=pltpu.SMEM)
HBM_SPEC = pl.BlockSpec(memory_space=pl.ANY)


def run_block(cols, keep, x, dy, one, two, strips, buckets):
    samples, rows, columns, _ = x.shape
    wide = columns // WIN
    tokens = wide * CELLS
    own = rows - SHIFT
    halo = (samples, SHIFT, columns, C)
    plan_one = reduce_plan(strips, buckets, one.shape[0], ORDERS[:2])
    plan_two = reduce_plan(strips, buckets, two.shape[0], ORDERS)
    top = samples - 1

    def attended(i):
        return (jnp.minimum(i, top), 0, 0, 0)

    def fed(i):
        return (jnp.minimum(jnp.maximum(i - LAG, 0), top), 0, 0, 0)

    def pulled(i):
        early = jnp.minimum(jnp.maximum(i - LAG, 0), top - LAG)
        return (early + jnp.maximum(i - (samples + LAG) + 1, 0), 0, 0, 0)

    vectors = [3 * C, C, FF, C, C, C, C, C]
    sums = (GROUPS, CELLS, GROUP_HEADS * LANES)

    def struct(shape, dtype=F32):
        return jax.ShapeDtypeStruct(shape, dtype)

    token = pltpu.VMEM((tokens, C), F32)
    low = pltpu.VMEM((tokens, C), BF16)
    turned = pltpu.VMEM((C, tokens), BF16)
    scratch = [pltpu.VMEM(s, BF16) for s in ((C, 3 * C), (C, C), (C, FF), (FF, C))]
    scratch += [pltpu.VMEM((1, size), F32) for size in vectors]
    scratch += [pltpu.VMEM(s, F32) for s in ((C, 3 * C), (C, C), (C, FF), (C, FF))]
    scratch += [pltpu.VMEM((1, size), F32) for size in vectors]
    scratch += [
        pltpu.VMEM((2,) + sums, F32), pltpu.VMEM(sums, F32),
        pltpu.VMEM((16, 256), F32), pltpu.VMEM((SPAN * 8, 128), F32),
        pltpu.VMEM((LAG, tokens, C), F32), pltpu.VMEM((LAG, tokens, C), BF16),
        pltpu.VMEM((LAG, wide, LANES, 3 * C), BF16), pltpu.VMEM((LAG, wide) + sums, BF16),
        pltpu.VMEM((LAG, tokens, C), BF16), pltpu.VMEM((LAG, wide, LANES, C), BF16),
        pltpu.VMEM((LAG, tokens, C), F32),
        pltpu.VMEM((C // 128, WIN, columns + 16, 128), F32),
        token, token, token, low, low, token, token, token, turned, turned,
        pltpu.VMEM((wide,) + sums, F32), pltpu.VMEM((tokens, 3 * C), F32),
        pltpu.VMEM((2,) + halo[1:], F32),
        pltpu.VMEM((2,) + halo, BF16), pltpu.VMEM((2,) + halo, BF16), pltpu.VMEM((2,) + halo, BF16),
        pltpu.VMEM(one.shape, BF16), pltpu.VMEM(two.shape, BF16),
        pltpu.SemaphoreType.DMA((4,)), pltpu.SemaphoreType.DMA((4, samples)), pltpu.SemaphoreType.DMA((4, samples)),
    ]
    block = (1, rows, columns, C)
    part = (1, own, columns, C)
    return pl.pallas_call(
        lambda *refs: block_kernel(strips, buckets, samples, plan_one, plan_two, *refs),
        grid=(samples + 2 * LAG,),
        in_specs=[SMEM_SPEC, SMEM_SPEC, pl.BlockSpec(block, attended), pl.BlockSpec(block, fed)] + [HBM_SPEC] * 4,
        out_specs=[pl.BlockSpec(part, fed), pl.BlockSpec(part, pulled)] + [HBM_SPEC] * 4,
        out_shape=[struct((samples, own, columns, C)), struct((samples, own, columns, C)), struct(halo, BF16),
                   struct(halo, BF16), struct(one.shape, BF16), struct(two.shape, BF16)],
        scratch_shapes=scratch + reduce_scratch(plan_one) + reduce_scratch(plan_two),
        compiler_params=pltpu.CompilerParams(
            vmem_limit_bytes=62 * 1024 * 1024, collective_id=1, has_side_effects=True
        ),
        name="block",
    )(cols, keep, x, dy, x, dy, one, two)


def dispatch_kernel(me_ref, owner_ref, master_ref, one_ref, two_ref, rank_ref, start_ref, padded, packed, start_s, sem):
    blocks = owner_ref.shape[0]
    capacity = master_ref.shape[0]
    mine = (owner_ref[...] == me_ref[0]).astype(F32)
    low = mine.astype(BF16)
    row = lax.broadcasted_iota(jnp.int32, (128, 128), 0)
    col = lax.broadcasted_iota(jnp.int32, (128, 128), 1)
    within = nn(low, (row <= col).astype(F32).astype(BF16))
    sums = nn(low, jnp.ones((128, 128), BF16))
    below = lax.broadcasted_iota(jnp.int32, (blocks, blocks), 1) < lax.broadcasted_iota(jnp.int32, (blocks, blocks), 0)
    start = nn(below.astype(F32).astype(BF16), sums.astype(BF16))
    rank_ref[...] = jnp.where(mine > 0, within - 1.0, -1.0)
    start_ref[...] = start.astype(jnp.int32)
    copy = pltpu.make_async_copy(start_ref, start_s, sem)
    copy.start()
    padded[...] = jnp.zeros_like(padded)
    padded[0:capacity, :] = master_ref[...]
    one_ref[FIRST_ROWS:, :] = jnp.zeros((one_ref.shape[0] - FIRST_ROWS, 128), BF16)
    used = SMALL_START - FIRST_ROWS
    two_ref[used:, :] = jnp.zeros((two_ref.shape[0] - used, 128), BF16)
    copy.wait()
    slot = row.astype(F32)

    def block(b, _):
        hot = (slot == rank_ref[pl.ds(b, 1), :]).astype(F32).astype(BF16)
        rows = padded[pl.ds(start_s[b, 0], 128), :].astype(BF16)
        packed[pl.ds(pl.multiple_of(b * 128, 128), 128), :] = tn(hot, rows)
        return 0

    small = SMALL_START // 128
    lax.fori_loop(0, small, block, 0, unroll=4)
    hot = (slot == rank_ref[small : small + 1, :]).astype(F32).astype(BF16)
    for i, piece in enumerate(split_three(padded[pl.ds(start_s[small, 0], 128), :])):
        first = FIRST_ROWS + i * SMALL_SPAN
        one_ref[first : first + SMALL_SPAN, :] = tn(hot, piece)[0:SMALL_SPAN].astype(BF16)
    for first, slabs, rows in slab_plan():
        for j in range(slabs):
            target, offset = (one_ref, 0) if first < FIRST_ROWS else (two_ref, FIRST_ROWS)
            target[first - offset + j * rows : first - offset + (j + 1) * rows, :] = packed[
                pl.ds(first + j, rows, stride=slabs), :
            ].astype(BF16)


def run_dispatch(me, owners, master, one_rows, two_rows):
    blocks = owners.shape[0]
    vmem = pl.BlockSpec(memory_space=pltpu.VMEM)
    return pl.pallas_call(
        dispatch_kernel,
        in_specs=[pl.BlockSpec(memory_space=pltpu.SMEM), vmem, vmem],
        out_specs=[vmem] * 4,
        out_shape=[
            jax.ShapeDtypeStruct((one_rows, 128), BF16),
            jax.ShapeDtypeStruct((two_rows, 128), BF16),
            jax.ShapeDtypeStruct((blocks, 128), F32),
            jax.ShapeDtypeStruct((blocks, 128), jnp.int32),
        ],
        scratch_shapes=[
            pltpu.VMEM((-(-(master.shape[0] + 128) // 8) * 8, 128), F32),
            pltpu.VMEM((SMALL_START, 128), F32),
            pltpu.SMEM((blocks, 128), jnp.int32),
            pltpu.SemaphoreType.DMA,
        ],
        compiler_params=pltpu.CompilerParams(vmem_limit_bytes=62 * 1024 * 1024),
        name="dispatch",
    )(me, owners, master)


def collect_kernel(
    start_ref, rank_ref, one_ref, two_ref, master_ref, first_ref, second_ref, outh_ref, gxh_ref, out_any, gx_any,
    first_out, second_out, master_out, out_final, gx_final, packed, total, wide, sems,
):
    own = out_any.shape[1]
    moves = [
        pltpu.make_async_copy(main, final.at[:, pl.ds(SHIFT, own)], sems.at[i])
        for i, (main, final) in enumerate(((out_any, out_final), (gx_any, gx_final)))
    ]
    for i, (halo, final) in enumerate(((outh_ref, out_final), (gxh_ref, gx_final))):
        wide[i] = halo[...].astype(F32)
        moves.append(pltpu.make_async_copy(wide.at[i], final.at[:, pl.ds(0, SHIFT)], sems.at[2 + i]))
    for move in moves:
        move.start()
    capacity = master_ref.shape[0]
    total[...] = jnp.zeros_like(total)
    for first, slabs, rows in slab_plan():
        for j in range(slabs):
            source, offset = (one_ref, 0) if first < FIRST_ROWS else (two_ref, FIRST_ROWS)
            packed[pl.ds(first + j, rows, stride=slabs), :] = source[
                first - offset + j * rows : first - offset + (j + 1) * rows, :
            ].astype(F32)
    packed[SMALL_START : SMALL_START + SMALL_SPAN, :] = one_ref[FIRST_ROWS : FIRST_ROWS + SMALL_SPAN, :].astype(F32)
    packed[SMALL_START + SMALL_SPAN : SMALL_START + 128, :] = jnp.zeros((128 - SMALL_SPAN, 128), F32)
    slot = lax.broadcasted_iota(jnp.int32, (128, 128), 0).astype(F32)

    def block(b, _):
        hot = (slot == rank_ref[pl.ds(b, 1), :]).astype(F32).astype(BF16)
        part = nn(hot, packed[pl.ds(pl.multiple_of(b * 128, 128), 128), :].astype(BF16))
        where = pl.ds(start_ref[b, 0], 128)
        total[where, :] = total[where, :] + part
        return 0

    lax.fori_loop(0, SMALL_START // 128 + 1, block, 0, unroll=4)
    slots = lax.broadcasted_iota(jnp.int32, (capacity, 1), 0)
    edges = [edge // 128 for edge in row_edges()[:4]] + [SMALL_START // 128 + 1]
    rates = [2.0 / math.sqrt(C), 2.0 / math.sqrt(C // 8), 2.0 / math.sqrt(C), 2.0 / math.sqrt(FF), 1.0, 0.0]
    rate = jnp.full((capacity, 1), rates[0], F32)
    for edge, amount in zip(edges, rates[1:]):
        rate = jnp.where(slots >= start_ref[edge, 0], amount, rate)
    decay = jnp.where(slots < start_ref[edges[3], 0], DECAY, 0.0)
    grads = total[0:capacity, :]
    weights = master_ref[...]
    first = BETA_ONE * first_ref[...] + (1.0 - BETA_ONE) * grads
    second = BETA_TWO * second_ref[...] + (1.0 - BETA_TWO) * grads * grads
    first_out[...] = first
    second_out[...] = second
    first_hat = first / (1.0 - BETA_ONE**STEP)
    second_hat = second / (1.0 - BETA_TWO**STEP)
    master_out[...] = weights - rate * (first_hat / (jnp.sqrt(second_hat) + ADAM_EPS) + decay * weights)
    for move in moves:
        move.wait()


def run_collect(starts, ranks, one, two, master, first, second, outh, gxh, out, gx):
    vmem = pl.BlockSpec(memory_space=pltpu.VMEM)
    samples, own, columns, channels = out.shape
    final = jax.ShapeDtypeStruct((samples, own + SHIFT, columns, channels), F32)
    return pl.pallas_call(
        collect_kernel,
        in_specs=[SMEM_SPEC] + [vmem] * 8 + [HBM_SPEC] * 2,
        out_specs=[vmem] * 3 + [HBM_SPEC] * 2,
        out_shape=[jax.ShapeDtypeStruct(master.shape, F32)] * 3 + [final, final],
        scratch_shapes=[
            pltpu.VMEM((SMALL_START + 128, 128), F32),
            pltpu.VMEM((-(-(master.shape[0] + 128) // 8) * 8, 128), F32),
            pltpu.VMEM((2,) + outh.shape, F32),
            pltpu.SemaphoreType.DMA((4,)),
        ],
        compiler_params=pltpu.CompilerParams(vmem_limit_bytes=62 * 1024 * 1024),
        name="collect",
    )(starts, ranks, one, two, master, first, second, outh, gxh, out, gx)


def shards(
    block_input, cotangent, window_cols, keep_mask, owner_list, master, first_moment, second_moment
):
    strips = lax.axis_size("strip")
    buckets = lax.axis_size("bucket")
    my_index = lax.axis_index(("strip", "bucket")).astype(jnp.int32).reshape(1)
    blocks = -(-(SMALL_START // 128 + 2) // 8) * 8
    owners = jnp.pad(owner_list, (0, blocks * 128 - owner_list.shape[0]), constant_values=-1).reshape(blocks, 128)
    one_rows = wire_rows(FIRST_ROWS + 3 * SMALL_SPAN, strips, buckets)
    two_rows = wire_rows(SMALL_START - FIRST_ROWS, strips, buckets)
    one, two, ranks, starts = run_dispatch(my_index, owners, master, one_rows, two_rows)
    keep = keep_mask.astype(F32) / KEEP_PROB
    output, grad_input, output_halo, grad_halo, gone, gtwo = run_block(
        window_cols, keep, block_input, cotangent, one, two, strips, buckets
    )
    first, second_new, new_weights, output, grad_input = run_collect(
        starts, ranks, gone, gtwo, master, first_moment, second_moment, output_halo, grad_halo, output, grad_input
    )
    return (output, grad_input, first, second_new, new_weights)


def solution(mesh):
    in_specs = (
        P("bucket", "strip", None, None),
        P("bucket", "strip", None, None),
        P("bucket"),
        P("bucket", None),
        P(),
        P(("strip", "bucket"), None),
        P(("strip", "bucket"), None),
        P(("strip", "bucket"), None),
    )
    out_specs = (
        P("bucket", "strip", None, None),
        P("bucket", "strip", None, None),
        P(("strip", "bucket"), None),
        P(("strip", "bucket"), None),
        P(("strip", "bucket"), None),
    )
    return jax.shard_map(shards, mesh=mesh, in_specs=in_specs, out_specs=out_specs, check_vma=False)
```

```python
import functools
import math

import jax
import jax.numpy as jnp
from jax import lax
from jax.experimental import pallas as pl
from jax.experimental.pallas import tpu as pltpu
from jax.sharding import PartitionSpec as P

C = 384
HEADS = 12
HD = 32
FF = 1536
WIN = 7
SHIFT = 3
STEP = 10
SMALL_ROWS = 39
TABLE_ROWS = 16


PRECISE = lax.Precision.HIGHEST
NORM_EPS = 1e-05
KEEP_PROB = 0.8
MASK_FILL = -100.0
BETA_ONE = 0.5
BETA_TWO = 0.5
ADAM_EPS = 1e-08
DECAY = 0.05


def row_edges():
    first = 3 * C * C // 128
    second = first + C * C // 128
    third = second + C * FF // 128
    fourth = third + FF * C // 128
    fifth = fourth + SMALL_ROWS
    return [first, second, third, fourth, fifth]


GROUPS = 3
GROUP_HEADS = HEADS // GROUPS
CELLS = WIN * 8
LANES = 64
LOG2E = math.log2(math.e)
F32 = jnp.float32
BF16 = jnp.bfloat16


def nn(left, right):
    return lax.dot_general(left, right, (((1,), (0,)), ((), ())), preferred_element_type=F32)


def nt(left, right):
    return lax.dot_general(left, right, (((1,), (1,)), ((), ())), preferred_element_type=F32)


def tn(left, right):
    return lax.dot_general(left, right, (((0,), (0,)), ((), ())), preferred_element_type=F32)


def gelu_pair(u):
    normal = 0.5 + 0.5 * lax.erf(u * math.sqrt(0.5))
    gauss = jnp.exp2(u * u * (-0.5 * LOG2E))
    return u * normal, normal + u * gauss * (1.0 / math.sqrt(2.0 * math.pi))


def row_norm(values):
    center = values - jnp.mean(values, axis=-1, keepdims=True)
    scale = lax.rsqrt(jnp.mean(center * center, axis=-1, keepdims=True) + NORM_EPS)
    return center * scale, scale


def norm_pull(grad, normal, scale):
    first = jnp.mean(grad, axis=-1, keepdims=True)
    second = jnp.mean(grad * normal, axis=-1, keepdims=True)
    return scale * (grad - first - normal * second)


def column_sum(values):
    return jnp.sum(values, axis=0, keepdims=True)


SMALL_START = 3 * C * C // 128 + C * C // 128 + 2 * C * FF // 128
SMALL_SPAN = 64


def slab_plan():
    return [
        (0, 3 * C // 128, C),
        (3 * C * C // 128, C // 128, C),
        (4 * C * C // 128, FF // 128, C),
        (4 * C * C // 128 + C * FF // 128, C // 128, FF),
    ]


ORDERS = (("x", "y", "z"), ("y", "x", "z")) * 2
LAG = 2
FIRST_ROWS = 3 * C * C // 128


def split_three(values):
    high = values.astype(BF16)
    rest = values - high.astype(F32)
    middle = rest.astype(BF16)
    return high, middle, (rest - middle.astype(F32)).astype(BF16)


def wire_rows(rows, strips, buckets):
    unit = 16 * strips * buckets
    return -(-rows // unit) * unit


def reduce_plan(strips, buckets, rows, orders):
    sizes = {"z": strips // 2, "y": 2, "x": buckets // 2}
    unit = 8 * strips * buckets
    units = rows // 2 // unit
    orders = orders[:units]
    parts, first = [], 0
    for p, order in enumerate(orders):
        length = (units // len(orders) + (p < units % len(orders))) * unit
        levels, share = [], length
        for axis in order:
            share = share // sizes[axis]
            levels.append((axis, sizes[axis], share))
        parts.append((first, length, levels))
        first += length
    return parts


def reduce_scratch(plan):
    shapes, copies = [], 0
    for _, length, levels in plan:
        shapes += [(length, 128), (length, 128)]
        for _, size, share in levels:
            shapes += [((size - 1) * share, 128), (share, 128)]
        copies += 2 + 2 * sum(size - 1 for _, size, _ in levels)
    return [pltpu.VMEM(shape, BF16) for shape in shapes] + [
        pltpu.SemaphoreType.DMA((copies,)), pltpu.SemaphoreType.DMA((copies,))
    ]


class Place:
    def __init__(self, strips, buckets):
        strip, bucket = lax.axis_index("strip"), lax.axis_index("bucket")
        self.sizes = {"z": strips // 2, "y": 2, "x": buckets // 2, "core": 2}
        self.mine = {"z": strip // 2, "y": strip % 2, "x": bucket // 2, "core": bucket % 2}
        self.above = (lax.rem(strip + strips - 1, strips), bucket)
        self.below = (lax.rem(strip + 1, strips), bucket)

    def peer(self, axis, offset):
        return lax.rem(self.mine[axis] + offset, self.sizes[axis])

    def device(self, axis, offset):
        place = dict(self.mine)
        place[axis] = self.peer(axis, offset)
        return (place["z"] * 2 + place["y"], place["x"] * 2 + place["core"])

    def greet(self, halos):
        barrier = pltpu.get_barrier_semaphore()
        partners = [self.device(axis, offset) for axis, size in self.sizes.items() for offset in range(1, size)]
        partners += [self.above, self.below] if halos else []
        for partner in partners:
            pl.semaphore_signal(barrier, inc=1, device_id=partner, device_id_type=pl.DeviceIdType.MESH)
        pl.semaphore_wait(barrier, len(partners))


def reduce_stages(place, plan, wire, scratch):
    buffers, send_sems, recv_sems = list(scratch[:-2]), scratch[-2], scratch[-1]
    half = wire.shape[0] // 2
    counter = [0]

    def span(start, length):
        return pl.ds(pl.multiple_of(start, 16), length)

    def copies_of(count):
        first = counter[0]
        counter[0] += count
        return first

    def copy(at, source, target, axis, offset):
        return pltpu.make_async_remote_copy(
            src_ref=source, dst_ref=target, send_sem=send_sems.at[at], recv_sem=recv_sems.at[at],
            device_id=place.device(axis, offset), device_id_type=pl.DeviceIdType.MESH,
        )

    def part_stages(first, length, levels):
        core_in, core_sum = buffers.pop(0), buffers.pop(0)
        boxes = [(buffers.pop(0), buffers.pop(0)) for _ in levels]
        held = [core_sum] + [total for _, total in boxes]

        def own():
            return place.mine["core"] * half + first

        def start_of(level):
            start = own()
            for axis, _, share in levels[:level]:
                start = start + place.mine[axis] * share
            return start

        core_at, back_at = copies_of(1), copies_of(1)
        down_at = [copies_of(size - 1) for _, size, _ in levels]
        up_at = [copies_of(size - 1) for _, size, _ in levels]

        def core_out():
            other = (1 - place.mine["core"]) * half + first
            return [copy(core_at, wire.at[span(other, length)], core_in, "core", 1)]

        def down(level):
            axis, size, share = levels[level]
            inbox = boxes[level][0]
            return [
                copy(down_at[level] + offset - 1, held[level].at[span(place.peer(axis, offset) * share, share)],
                     inbox.at[pl.ds((offset - 1) * share, share)], axis, offset)
                for offset in range(1, size)
            ]

        def up(level):
            axis, size, share = levels[level]
            region = wire.at[span(start_of(level + 1), share)]
            return [copy(up_at[level] + offset - 1, region, region, axis, offset) for offset in range(1, size)]

        def core_back():
            region = wire.at[span(own(), length)]
            return [copy(back_at, region, region, "core", 1)]

        def add_core():
            core_sum[...] = wire[span(own(), length), :] + core_in[...]

        def add(level):
            axis, size, share = levels[level]
            inbox, total = boxes[level]
            value = held[level][span(place.mine[axis] * share, share), :].astype(F32)
            for offset in range(1, size):
                value = value + inbox[(offset - 1) * share : offset * share, :].astype(F32)
            if level + 1 < len(levels):
                total[...] = value.astype(BF16)
            else:
                wire[span(start_of(len(levels)), share), :] = value.astype(BF16)

        count = len(levels)
        moves = [core_out] + [functools.partial(down, level) for level in range(count)]
        moves += [functools.partial(up, level) for level in reversed(range(count))] + [core_back]
        work = {1: add_core}
        for level in range(count):
            work[level + 2] = functools.partial(add, level)

        def stage(index):
            if index > 0:
                for one in moves[index - 1]():
                    one.wait()
            if index in work:
                work[index]()
            if index < len(moves):
                for one in moves[index]():
                    one.start()

        return [functools.partial(stage, index) for index in range(len(moves) + 1)]

    return [part_stages(*part) for part in plan]


def reduce_ticks(parts):
    ticks = []
    for p, stages in enumerate(parts):
        for index, stage in enumerate(stages):
            at = index + p // 2
            while len(ticks) <= at:
                ticks.append([])
            ticks[at].append(stage)

    def run(tick):
        for stage in tick:
            stage()

    return [functools.partial(run, tick) for tick in ticks]


def tick_slots(ticks, slots):
    return [[tick for i, tick in enumerate(ticks) if i * slots // len(ticks) == slot] for slot in range(slots)]


def head_bits():
    lane_head = lax.broadcasted_iota(jnp.int32, (1, 128), 1) // HD
    return [(lane_head == h).astype(F32).astype(BF16) for h in range(GROUP_HEADS)]


def stack_of(part, bits):
    return jnp.concatenate([part * bit for bit in bits], axis=0)


def unstack(part):
    lane_head = lax.broadcasted_iota(jnp.int32, (1, 128), 1) // HD
    total = None
    for h in range(GROUP_HEADS):
        piece = jnp.where(lane_head == h, part[h * LANES : h * LANES + CELLS], 0.0)
        total = piece if total is None else total + piece
    return total


def load_matrix(target, wire, first, rows):
    for j in range(target.shape[1] // 128):
        target[:, j * 128 : j * 128 + 128] = wire[first + j * rows : first + (j + 1) * rows, :]


def load_vectors(refs, wire, first):
    small = jnp.zeros((SMALL_SPAN, 128), F32)
    for i in range(3):
        small = small + wire[FIRST_ROWS + i * SMALL_SPAN : FIRST_ROWS + (i + 1) * SMALL_SPAN, :].astype(F32)
    for ref, row in zip(refs, first):
        for j in range(ref.shape[1] // 128):
            ref[:, j * 128 : j * 128 + 128] = small[row + j : row + j + 1]


def to_windows(line, last, main, halo, step, target):
    slabs, columns = C // 128, main.shape[2]
    wide, own = columns // WIN, WIN - SHIFT
    wrapped_row = lax.broadcasted_iota(jnp.int32, (8, 128), 0) >= own
    for a in range(WIN):
        row = main[0, SHIFT + a] if a < own else halo[step, a - own].astype(F32)
        for s in range(slabs):
            line[s, a, 8 : 8 + columns, :] = row[:, s * 128 : s * 128 + 128]
    for a in range(WIN):
        for s in range(slabs):
            front = line[s, a, 8 - own : 16 - own, :]
            for w in range(wide):
                first = 8 + w * WIN + SHIFT
                tile = jnp.where(wrapped_row & (w == last), front, line[s, a, first : first + 8, :])
                target[w * CELLS + a * 8 : w * CELLS + a * 8 + 8, s * 128 : s * 128 + 128] = tile


def from_windows(line, width, source, main, halo, step):
    slabs, columns = C // 128, main.shape[2]
    wide, own = columns // WIN, WIN - SHIFT
    for w in range(wide):
        for a in range(WIN):
            for s in range(slabs):
                first = 8 + w * WIN + SHIFT
                line[s, a, first : first + 8, :] = source[
                    w * CELLS + a * 8 : w * CELLS + a * 8 + 8, s * 128 : s * 128 + 128
                ]
    kept = lax.broadcasted_iota(jnp.int32, (columns, 128), 0) < width
    front = lax.broadcasted_iota(jnp.int32, (8, 128), 0) < SHIFT
    for a in range(WIN):
        for s in range(slabs):
            wrapped = line[s, a, pl.ds(width + 8, 8), :]
            line[s, a, 8:16, :] = jnp.where(front, wrapped, line[s, a, 8:16, :])
            row = jnp.where(kept, line[s, a, 8 : 8 + columns, :], 0.0)
            if a < own:
                main[0, a, :, s * 128 : s * 128 + 128] = row
            else:
                halo[step, a - own, :, s * 128 : s * 128 + 128] = row.astype(BF16)


def place_onehot(row):
    shape = (128, HEADS * LANES)
    source = lax.broadcasted_iota(jnp.int32, shape, 0)
    lane = lax.broadcasted_iota(jnp.int32, shape, 1)
    return (lane == source // 8 * LANES + row * 8 + source % 8).astype(F32).astype(BF16)


def offset_onehot(column):
    shape = (256, 128)
    source = lax.broadcasted_iota(jnp.int32, shape, 0)
    lane = lax.broadcasted_iota(jnp.int32, shape, 1)
    wanted = (lane % 8 - column + WIN - 1) * HEADS + lane // 8
    return ((source == wanted) & (lane < HEADS * 8)).astype(F32).astype(BF16)


SPAN = 2 * WIN - 1


def build_bias(raw, last_strip, offsets, spread, bias):
    flat = jnp.concatenate([raw[r : r + 1] for r in range(TABLE_ROWS)], axis=1)
    offsets[...] = jnp.zeros_like(offsets)
    spread[...] = jnp.zeros_like(spread)
    for d in range(SPAN):
        offsets[SPAN - 1 - d : SPAN - d, 0 : SPAN * HEADS] = flat[:, d * SPAN * HEADS : (d + 1) * SPAN * HEADS]
    terms = split_three(offsets[...])
    for column in range(WIN):
        pick = offset_onehot(column)
        part = nn(terms[0], pick) + nn(terms[1], pick) + nn(terms[2], pick)
        spread[pl.ds(column, SPAN, stride=8), :] = part[0:SPAN]
    terms = split_three(spread[...])
    total = jnp.zeros((CELLS, HEADS * LANES), F32)
    for row in range(WIN):
        pick = place_onehot(row)
        for term in terms:
            total = total + nn(term[8 * (WIN - 1 - row) : 8 * (WIN - 1 - row) + CELLS], pick)
    shape = (CELLS, HEADS * LANES)
    key = lax.broadcasted_iota(jnp.int32, shape, 0)
    query = lax.broadcasted_iota(jnp.int32, shape, 1) % LANES
    edge = WIN - SHIFT
    by_row = ((key // 8 >= edge) != (query // 8 >= edge)) & last_strip
    by_col = (key % 8 >= edge) != (query % 8 >= edge)
    for variant, masked in enumerate((by_row, by_row | by_col)):
        value = (total + jnp.where(masked, MASK_FILL, 0.0)) * LOG2E
        value = jnp.where(key % 8 < WIN, value, -1e30)
        for g in range(GROUPS):
            bias[variant, g] = value[:, g * GROUP_HEADS * LANES : (g + 1) * GROUP_HEADS * LANES]


def pull_bias(sums, spread):
    grads = jnp.concatenate([sums[g] for g in range(GROUPS)], axis=1)
    high, middle, _ = split_three(grads)
    spread[...] = jnp.zeros_like(spread)
    for row in range(WIN):
        pick = place_onehot(row)
        first = 8 * (WIN - 1 - row)
        spread[first : first + CELLS, :] += nt(high, pick) + nt(middle, pick)
    total = jnp.zeros((SPAN, 256), F32)
    for column in range(WIN):
        pick = offset_onehot(column)
        high, middle, _ = split_three(spread[pl.ds(column, SPAN, stride=8), :])
        total = total + nt(high, pick) + nt(middle, pick)
    flat = [total[SPAN - 1 - d : SPAN - d, 0 : SPAN * HEADS] for d in range(SPAN)]
    flat.append(jnp.zeros((1, TABLE_ROWS * 128 - SPAN * SPAN * HEADS), F32))
    flat = jnp.concatenate(flat, axis=1)
    return jnp.concatenate([flat[:, r * 128 : r * 128 + 128] for r in range(TABLE_ROWS)], axis=0)


def block_kernel(
    strips, buckets, images, plan_one, plan_two,
    cols_ref, keep_ref, x_ref, dy_ref, x_any, dy_any, one_any, two_any,
    out_ref, gx_ref, outh_any, gxh_any, gone_any, gtwo_any,
    wq_ref, wp_ref, wu_ref, wd_ref, bq_ref, bp_ref, bu_ref, bd_ref, g1_ref, b1_ref, g2_ref, b2_ref,
    gwq_ref, gwp_ref, gwu_ref, gwdt_ref, gbq_ref, gbp_ref, gbu_ref, gbd_ref, gg1_ref, gb1_ref, gg2_ref, gb2_ref,
    bias, gs_ref, offsets, spread,
    xw, zs, qkv, prob, ctx, gctx, gx1s,
    line, dyw, x1s, n2s, h2s, gfs, ys, gh2s, resw, htr, gtr, gscores, gqkv,
    fetched, halo_out, halo_in, back_in, wire_one, wire_two,
    local_sems, send_sems, recv_sems, *scratch,
):
    step = pl.program_id(0)
    tokens = dyw.shape[0]
    wide = tokens // CELLS
    place = Place(strips, buckets)
    last = cols_ref[0] - 1
    width = cols_ref[0] * WIN
    count_one = len(reduce_scratch(plan_one))
    parts_one = reduce_stages(place, plan_one, wire_one, scratch[:count_one])
    parts_two = reduce_stages(place, plan_two, wire_two, scratch[count_one:])
    gather_ticks = reduce_ticks(parts_one + parts_two)
    early = len(parts_one[0])
    one_ticks, two_ticks = reduce_ticks(parts_one), reduce_ticks(parts_two)

    def halo(kind, image):
        return pltpu.make_async_remote_copy(
            src_ref=halo_out.at[kind % 2, image], dst_ref=(halo_in if kind < 2 else back_in).at[kind % 2, image],
            send_sem=send_sems.at[kind, image], recv_sem=recv_sems.at[kind, image],
            device_id=place.above if kind < 2 else place.below, device_id_type=pl.DeviceIdType.MESH,
        )

    def fetch(array, image, kind):
        return pltpu.make_async_copy(array.at[image, pl.ds(0, SHIFT)], fetched.at[kind], local_sems.at[kind])

    def send_rows(kind, image, held):
        halo_out[kind, image] = fetched[held].astype(BF16)
        halo(kind, image).start()

    @pl.when(step == 0)
    def _():
        loads = [
            pltpu.make_async_copy(source, target, local_sems.at[2 + i])
            for i, (source, target) in enumerate(((one_any, wire_one), (two_any, wire_two)))
        ]
        first = [fetch(x_any, image, image) for image in range(2)]
        for copy in loads + first:
            copy.start()
        place.greet(True)
        for copy in loads:
            copy.wait()
        gather_ticks[0]()
        for image in range(2):
            first[image].wait()
            send_rows(0, image, image)
        fetch(x_any, 2, 0).start()
        fetch(dy_any, 0, 1).start()
        line[...] = jnp.zeros_like(line)
        for ref in (gwq_ref, gwp_ref, gwu_ref, gwdt_ref, gbq_ref, gbp_ref, gbu_ref, gbd_ref,
                    gg1_ref, gb1_ref, gg2_ref, gb2_ref, gs_ref, qkv, gctx):
            ref[...] = jnp.zeros_like(ref)
        for tick in gather_ticks[1:early]:
            tick()
        load_matrix(wq_ref, wire_one, 0, C)
        load_vectors((bq_ref, bp_ref, bu_ref, bd_ref, g1_ref, b1_ref, g2_ref, b2_ref), wire_one,
                     (0, 9, 12, 24, 27, 30, 33, 36))
        raw = jnp.zeros((SMALL_SPAN, 128), F32)
        for i in range(3):
            raw = raw + wire_one[FIRST_ROWS + i * SMALL_SPAN : FIRST_ROWS + (i + 1) * SMALL_SPAN, :].astype(F32)
        build_bias(raw[SMALL_ROWS : SMALL_ROWS + TABLE_ROWS], lax.axis_index("strip") == strips - 1, offsets, spread, bias)

    @pl.when((step > 0) & (step + 1 < images))
    def _():
        fetch(x_any, step + 1, 0).wait()
        send_rows(0, step + 1, 0)

    @pl.when((step > 0) & (step + 2 < images))
    def _():
        fetch(x_any, step + 2, 0).start()

    @pl.when((step > 0) & (step - 1 < images))
    def _():
        fetch(dy_any, step - 1, 1).wait()
        send_rows(1, step - 1, 1)

    @pl.when((step > 0) & (step < images))
    def _():
        fetch(dy_any, step, 1).start()

    bits = head_bits()

    def attend(image):
        at = lax.rem(image, LAG)
        halo(0, image).wait_recv()
        to_windows(line, last, x_ref, halo_in.at[0], image, xw.at[at])
        normal, _ = row_norm(xw[at])
        zs[at] = (normal * g1_ref[...] + b1_ref[...]).astype(BF16)
        triple = nn(zs[at], wq_ref[...]) + bq_ref[...]
        for w in range(wide):
            qkv[at, w, 0:CELLS, :] = triple[w * CELLS : w * CELLS + CELLS].astype(BF16)
        for w in range(wide):
            variant = (w == last).astype(jnp.int32)
            for g in range(GROUPS):
                q = qkv[at, w, :, g * 128 : g * 128 + 128]
                k = qkv[at, w, 0:CELLS, C + g * 128 : C + g * 128 + 128]
                v = qkv[at, w, 0:CELLS, 2 * C + g * 128 : 2 * C + g * 128 + 128]
                s = nt(k, stack_of(q, bits)) * (HD ** (-0.5) * LOG2E) + bias[variant, g]
                e = jnp.exp2(s - jnp.max(s, axis=0, keepdims=True))
                a = (e * (1.0 / jnp.sum(e, axis=0, keepdims=True))).astype(BF16)
                prob[at, w, g] = a
                resw[w * CELLS : w * CELLS + CELLS, g * 128 : g * 128 + 128] = unstack(tn(a, v))
        ctx[at] = resw[...].astype(BF16)

    def feed(image):
        at = lax.rem(image, LAG)
        keep_one = keep_ref[image, 0]
        keep_two = keep_ref[image, 1]
        x1 = xw[at] + keep_one * (nn(ctx[at], wp_ref[...]) + bp_ref[...])
        x1s[...] = x1
        normal, scale_two = row_norm(x1)
        n2s[...] = normal
        h2 = (normal * g2_ref[...] + b2_ref[...]).astype(BF16)
        h2s[...] = h2
        htr[...] = h2.astype(F32).T.astype(BF16)

        halo(1, image).wait_recv()
        to_windows(line, last, dy_ref, halo_in.at[1], image, dyw)
        token = lax.broadcasted_iota(jnp.int32, (tokens, 1), 0)
        valid = ((token % 8 < WIN) & (token < cols_ref[0] * CELLS)).astype(F32)
        gy = dyw[...] * valid
        gf = (gy * keep_two).astype(BF16)
        gfs[...] = gf
        gbd_ref[...] += column_sum(gf.astype(F32))
        gtr[...] = gf.astype(F32).T.astype(BF16)
        ys[...] = jnp.zeros_like(ys)
        gh2s[...] = jnp.zeros_like(gh2s)
        chunk = 512
        for j in range(FF // chunk):
            part = slice(j * chunk, (j + 1) * chunk)
            u = nn(h2s[...], wu_ref[:, part]) + bu_ref[:, part]
            gm = nt(gfs[...], wd_ref[part, :])
            m, slope = gelu_pair(u)
            m = m.astype(BF16)
            gu = (gm * slope).astype(BF16)
            ys[...] += nn(m, wd_ref[part, :])
            gwdt_ref[:, part] += nn(gtr[...], m)
            gwu_ref[:, part] += nn(htr[...], gu)
            gbu_ref[:, part] += column_sum(gu.astype(F32))
            gh2s[...] += nt(gu, wu_ref[:, part])

        resw[...] = (x1s[...] + keep_two * (ys[...] + bd_ref[...])) * valid
        halo(1, image).wait_send()
        from_windows(line, width, resw, out_ref, halo_out.at[1], image)
        halo(3, image).start()

        gh2 = gh2s[...]
        gg2_ref[...] += column_sum(gh2 * n2s[...])
        gb2_ref[...] += column_sum(gh2)
        gx1 = dyw[...] * valid + norm_pull(gh2 * g2_ref[...], n2s[...], scale_two)
        gx1s[at] = gx1
        ga = (keep_one * gx1).astype(BF16)
        gbp_ref[...] += column_sum(ga.astype(F32))
        gwp_ref[...] += nn(ctx[at].astype(F32).T.astype(BF16), ga)
        gc = nt(ga, wp_ref[...])
        for w in range(wide):
            gctx[at, w, 0:CELLS, :] = gc[w * CELLS : w * CELLS + CELLS].astype(BF16)

    def pull(image, middle):
        at = lax.rem(image, LAG)
        scale = HD ** (-0.5)
        for w in range(wide):
            rows = slice(w * CELLS, w * CELLS + CELLS)
            for g in range(GROUPS):
                v = qkv[at, w, 0:CELLS, 2 * C + g * 128 : 2 * C + g * 128 + 128]
                gstack = stack_of(gctx[at, w, :, g * 128 : g * 128 + 128], bits)
                low = prob[at, w, g]
                a = low.astype(F32)
                grad = nt(v, gstack)
                inner = jnp.sum(grad * a, axis=0, keepdims=True)
                gscores[w, g] = a * (grad - inner)
                gqkv[rows, 2 * C + g * 128 : 2 * C + g * 128 + 128] = nn(low, gstack)
        middle()
        for w in range(wide):
            rows = slice(w * CELLS, w * CELLS + CELLS)
            for g in range(GROUPS):
                q = qkv[at, w, :, g * 128 : g * 128 + 128]
                k = qkv[at, w, 0:CELLS, C + g * 128 : C + g * 128 + 128]
                gs = gscores[w, g].astype(BF16)
                gqkv[rows, g * 128 : g * 128 + 128] = unstack(tn(gs, k)) * scale
                gqkv[rows, C + g * 128 : C + g * 128 + 128] = nn(gs, stack_of(q, bits)) * scale
        gs_ref[...] += jnp.sum(gscores[...], axis=0)

        gtriple = gqkv[...].astype(BF16)
        gbq_ref[...] += column_sum(gtriple.astype(F32))
        gwq_ref[...] += nn(zs[at].astype(F32).T.astype(BF16), gtriple)
        gz = nt(gtriple, wq_ref[...]).astype(BF16).astype(F32)
        normal, scale_one = row_norm(xw[at])
        gg1_ref[...] += column_sum(gz * normal)
        gb1_ref[...] += column_sum(gz)
        resw[...] = gx1s[at] + norm_pull(gz * g1_ref[...], normal, scale_one)
        halo(0, image).wait_send()
        from_windows(line, width, resw, gx_ref, halo_out.at[0], image)
        halo(2, image).start()

    def pack_two():
        first = 0
        for grad in (gwp_ref, gwu_ref):
            for j in range(grad.shape[1] // 128):
                wire_two[first : first + C, :] = grad[:, j * 128 : j * 128 + 128].astype(BF16)
                first += C
        for j in range(C // 128):
            wire_two[first : first + FF, :] = gwdt_ref[j * 128 : j * 128 + 128, :].T.astype(BF16)
            first += FF
        wire_two[first:, :] = jnp.zeros((wire_two.shape[0] - first, 128), BF16)

    def pack_one():
        for j in range(3 * C // 128):
            wire_one[j * C : (j + 1) * C, :] = gwq_ref[:, j * 128 : j * 128 + 128].astype(BF16)
        vectors = (gbq_ref, gbp_ref, gbu_ref, gbd_ref, gg1_ref, gb1_ref, gg2_ref, gb2_ref)
        pieces = [ref[:, j * 128 : j * 128 + 128] for ref in vectors for j in range(ref.shape[1] // 128)]
        pieces.append(pull_bias(gs_ref, spread))
        pieces.append(jnp.zeros((wire_one.shape[0] - FIRST_ROWS - SMALL_ROWS - TABLE_ROWS, 128), F32))
        wire_one[FIRST_ROWS:, :] = jnp.concatenate(pieces, axis=0).astype(BF16)

    @pl.when(step == LAG)
    def _():
        first = 0
        for ref, rows in ((wp_ref, C), (wu_ref, C), (wd_ref, FF)):
            load_matrix(ref, wire_two, first, rows)
            first += ref.shape[1] // 128 * rows

    @pl.when((step >= LAG) & (step < images + LAG))
    def _():
        feed(step - LAG)

    @pl.when((step >= LAG) & (step < images))
    def _():
        pull(step - LAG, lambda: None)

    @pl.when(step < images)
    def _():
        attend(step)

    late = gather_ticks[early:]
    for k in range(LAG):
        mine = late[k * len(late) // LAG : (k + 1) * len(late) // LAG]

        @pl.when(step == k)
        def _(mine=mine):
            for tick in mine:
                tick()

    @pl.when(step == images + LAG - 1)
    def _():
        pack_two()
        two_ticks[0]()

    for k in range(LAG):

        @pl.when(step == images + LAG + k)
        def _(k=k):
            two_ticks[2 * k + 1]()
            pull(images - LAG + k, two_ticks[2 * k + 2])

    @pl.when(step == images + 2 * LAG - 1)
    def _():
        pack_one()
        rest = two_ticks[2 * LAG + 1 :]
        for i in range(max(len(rest), len(one_ticks))):
            for ticks in (one_ticks, rest):
                if i < len(ticks):
                    ticks[i]()
        for image in range(images):
            for kind in range(2, 4):
                halo(kind, image).wait()
        stores = [
            pltpu.make_async_copy(source, target, local_sems.at[i])
            for i, (source, target) in enumerate(
                ((wire_one, gone_any), (wire_two, gtwo_any), (back_in.at[0], gxh_any), (back_in.at[1], outh_any))
            )
        ]
        for copy in stores:
            copy.start()
        for copy in stores:
            copy.wait()


SMEM_SPEC = pl.BlockSpec(memory_space=pltpu.SMEM)
HBM_SPEC = pl.BlockSpec(memory_space=pl.ANY)


def run_block(cols, keep, x, dy, one, two, strips, buckets):
    samples, rows, columns, _ = x.shape
    wide = columns // WIN
    tokens = wide * CELLS
    own = rows - SHIFT
    halo = (samples, SHIFT, columns, C)
    plan_one = reduce_plan(strips, buckets, one.shape[0], ORDERS[:2])
    plan_two = reduce_plan(strips, buckets, two.shape[0], ORDERS)
    top = samples - 1

    def attended(i):
        return (jnp.minimum(i, top), 0, 0, 0)

    def fed(i):
        return (jnp.minimum(jnp.maximum(i - LAG, 0), top), 0, 0, 0)

    def pulled(i):
        early = jnp.minimum(jnp.maximum(i - LAG, 0), top - LAG)
        return (early + jnp.maximum(i - (samples + LAG) + 1, 0), 0, 0, 0)

    vectors = [3 * C, C, FF, C, C, C, C, C]
    sums = (GROUPS, CELLS, GROUP_HEADS * LANES)

    def struct(shape, dtype=F32):
        return jax.ShapeDtypeStruct(shape, dtype)

    token = pltpu.VMEM((tokens, C), F32)
    low = pltpu.VMEM((tokens, C), BF16)
    turned = pltpu.VMEM((C, tokens), BF16)
    scratch = [pltpu.VMEM(s, BF16) for s in ((C, 3 * C), (C, C), (C, FF), (FF, C))]
    scratch += [pltpu.VMEM((1, size), F32) for size in vectors]
    scratch += [pltpu.VMEM(s, F32) for s in ((C, 3 * C), (C, C), (C, FF), (C, FF))]
    scratch += [pltpu.VMEM((1, size), F32) for size in vectors]
    scratch += [
        pltpu.VMEM((2,) + sums, F32), pltpu.VMEM(sums, F32),
        pltpu.VMEM((16, 256), F32), pltpu.VMEM((SPAN * 8, 128), F32),
        pltpu.VMEM((LAG, tokens, C), F32), pltpu.VMEM((LAG, tokens, C), BF16),
        pltpu.VMEM((LAG, wide, LANES, 3 * C), BF16), pltpu.VMEM((LAG, wide) + sums, BF16),
        pltpu.VMEM((LAG, tokens, C), BF16), pltpu.VMEM((LAG, wide, LANES, C), BF16),
        pltpu.VMEM((LAG, tokens, C), F32),
        pltpu.VMEM((C // 128, WIN, columns + 16, 128), F32),
        token, token, token, low, low, token, token, token, turned, turned,
        pltpu.VMEM((wide,) + sums, F32), pltpu.VMEM((tokens, 3 * C), F32),
        pltpu.VMEM((2,) + halo[1:], F32),
        pltpu.VMEM((2,) + halo, BF16), pltpu.VMEM((2,) + halo, BF16), pltpu.VMEM((2,) + halo, BF16),
        pltpu.VMEM(one.shape, BF16), pltpu.VMEM(two.shape, BF16),
        pltpu.SemaphoreType.DMA((4,)), pltpu.SemaphoreType.DMA((4, samples)), pltpu.SemaphoreType.DMA((4, samples)),
    ]
    block = (1, rows, columns, C)
    part = (1, own, columns, C)
    return pl.pallas_call(
        lambda *refs: block_kernel(strips, buckets, samples, plan_one, plan_two, *refs),
        grid=(samples + 2 * LAG,),
        in_specs=[SMEM_SPEC, SMEM_SPEC, pl.BlockSpec(block, attended), pl.BlockSpec(block, fed)] + [HBM_SPEC] * 4,
        out_specs=[pl.BlockSpec(part, fed), pl.BlockSpec(part, pulled)] + [HBM_SPEC] * 4,
        out_shape=[struct((samples, own, columns, C)), struct((samples, own, columns, C)), struct(halo, BF16),
                   struct(halo, BF16), struct(one.shape, BF16), struct(two.shape, BF16)],
        scratch_shapes=scratch + reduce_scratch(plan_one) + reduce_scratch(plan_two),
        compiler_params=pltpu.CompilerParams(
            vmem_limit_bytes=62 * 1024 * 1024, collective_id=1, has_side_effects=True
        ),
        name="block",
    )(cols, keep, x, dy, x, dy, one, two)


def dispatch_kernel(me_ref, owner_ref, master_ref, one_ref, two_ref, rank_ref, start_ref, padded, packed, start_s, sem):
    blocks = owner_ref.shape[0]
    capacity = master_ref.shape[0]
    mine = (owner_ref[...] == me_ref[0]).astype(F32)
    low = mine.astype(BF16)
    row = lax.broadcasted_iota(jnp.int32, (128, 128), 0)
    col = lax.broadcasted_iota(jnp.int32, (128, 128), 1)
    within = nn(low, (row <= col).astype(F32).astype(BF16))
    sums = nn(low, jnp.ones((128, 128), BF16))
    below = lax.broadcasted_iota(jnp.int32, (blocks, blocks), 1) < lax.broadcasted_iota(jnp.int32, (blocks, blocks), 0)
    start = nn(below.astype(F32).astype(BF16), sums.astype(BF16))
    rank_ref[...] = jnp.where(mine > 0, within - 1.0, -1.0)
    start_ref[...] = start.astype(jnp.int32)
    copy = pltpu.make_async_copy(start_ref, start_s, sem)
    copy.start()
    padded[...] = jnp.zeros_like(padded)
    padded[0:capacity, :] = master_ref[...]
    one_ref[FIRST_ROWS:, :] = jnp.zeros((one_ref.shape[0] - FIRST_ROWS, 128), BF16)
    used = SMALL_START - FIRST_ROWS
    two_ref[used:, :] = jnp.zeros((two_ref.shape[0] - used, 128), BF16)
    copy.wait()
    slot = row.astype(F32)

    def block(b, _):
        hot = (slot == rank_ref[pl.ds(b, 1), :]).astype(F32).astype(BF16)
        rows = padded[pl.ds(start_s[b, 0], 128), :].astype(BF16)
        packed[pl.ds(pl.multiple_of(b * 128, 128), 128), :] = tn(hot, rows)
        return 0

    small = SMALL_START // 128
    lax.fori_loop(0, small, block, 0, unroll=4)
    hot = (slot == rank_ref[small : small + 1, :]).astype(F32).astype(BF16)
    for i, piece in enumerate(split_three(padded[pl.ds(start_s[small, 0], 128), :])):
        first = FIRST_ROWS + i * SMALL_SPAN
        one_ref[first : first + SMALL_SPAN, :] = tn(hot, piece)[0:SMALL_SPAN].astype(BF16)
    for first, slabs, rows in slab_plan():
        for j in range(slabs):
            target, offset = (one_ref, 0) if first < FIRST_ROWS else (two_ref, FIRST_ROWS)
            target[first - offset + j * rows : first - offset + (j + 1) * rows, :] = packed[
                pl.ds(first + j, rows, stride=slabs), :
            ].astype(BF16)


def run_dispatch(me, owners, master, one_rows, two_rows):
    blocks = owners.shape[0]
    vmem = pl.BlockSpec(memory_space=pltpu.VMEM)
    return pl.pallas_call(
        dispatch_kernel,
        in_specs=[pl.BlockSpec(memory_space=pltpu.SMEM), vmem, vmem],
        out_specs=[vmem] * 4,
        out_shape=[
            jax.ShapeDtypeStruct((one_rows, 128), BF16),
            jax.ShapeDtypeStruct((two_rows, 128), BF16),
            jax.ShapeDtypeStruct((blocks, 128), F32),
            jax.ShapeDtypeStruct((blocks, 128), jnp.int32),
        ],
        scratch_shapes=[
            pltpu.VMEM((-(-(master.shape[0] + 128) // 8) * 8, 128), F32),
            pltpu.VMEM((SMALL_START, 128), F32),
            pltpu.SMEM((blocks, 128), jnp.int32),
            pltpu.SemaphoreType.DMA,
        ],
        compiler_params=pltpu.CompilerParams(vmem_limit_bytes=62 * 1024 * 1024),
        name="dispatch",
    )(me, owners, master)


def collect_kernel(
    start_ref, rank_ref, one_ref, two_ref, master_ref, first_ref, second_ref, outh_ref, gxh_ref, out_any, gx_any,
    first_out, second_out, master_out, out_final, gx_final, packed, total, wide, sems,
):
    own = out_any.shape[1]
    loads = [
        pltpu.make_async_copy(main, wide.at[i, :, pl.ds(SHIFT, own)], sems.at[i])
        for i, main in enumerate((out_any, gx_any))
    ]
    stores = [pltpu.make_async_copy(wide.at[i], final, sems.at[2 + i]) for i, final in enumerate((out_final, gx_final))]
    for load in loads:
        load.start()
    for i, halo in enumerate((outh_ref, gxh_ref)):
        wide[i, :, 0:SHIFT] = halo[...].astype(F32)
    for load, store in zip(loads, stores):
        load.wait()
        store.start()
    capacity = master_ref.shape[0]
    total[...] = jnp.zeros_like(total)
    for first, slabs, rows in slab_plan():
        for j in range(slabs):
            source, offset = (one_ref, 0) if first < FIRST_ROWS else (two_ref, FIRST_ROWS)
            packed[pl.ds(first + j, rows, stride=slabs), :] = source[
                first - offset + j * rows : first - offset + (j + 1) * rows, :
            ].astype(F32)
    packed[SMALL_START : SMALL_START + SMALL_SPAN, :] = one_ref[FIRST_ROWS : FIRST_ROWS + SMALL_SPAN, :].astype(F32)
    packed[SMALL_START + SMALL_SPAN : SMALL_START + 128, :] = jnp.zeros((128 - SMALL_SPAN, 128), F32)
    slot = lax.broadcasted_iota(jnp.int32, (128, 128), 0).astype(F32)

    def block(b, _):
        hot = (slot == rank_ref[pl.ds(b, 1), :]).astype(F32).astype(BF16)
        part = nn(hot, packed[pl.ds(pl.multiple_of(b * 128, 128), 128), :].astype(BF16))
        where = pl.ds(start_ref[b, 0], 128)
        total[where, :] = total[where, :] + part
        return 0

    lax.fori_loop(0, SMALL_START // 128 + 1, block, 0, unroll=4)
    slots = lax.broadcasted_iota(jnp.int32, (capacity, 1), 0)
    edges = [edge // 128 for edge in row_edges()[:4]] + [SMALL_START // 128 + 1]
    rates = [2.0 / math.sqrt(C), 2.0 / math.sqrt(C // 8), 2.0 / math.sqrt(C), 2.0 / math.sqrt(FF), 1.0, 0.0]
    rate = jnp.full((capacity, 1), rates[0], F32)
    for edge, amount in zip(edges, rates[1:]):
        rate = jnp.where(slots >= start_ref[edge, 0], amount, rate)
    decay = jnp.where(slots < start_ref[edges[3], 0], DECAY, 0.0)
    grads = total[0:capacity, :]
    weights = master_ref[...]
    first = BETA_ONE * first_ref[...] + (1.0 - BETA_ONE) * grads
    second = BETA_TWO * second_ref[...] + (1.0 - BETA_TWO) * grads * grads
    first_out[...] = first
    second_out[...] = second
    first_hat = first / (1.0 - BETA_ONE**STEP)
    second_hat = second / (1.0 - BETA_TWO**STEP)
    master_out[...] = weights - rate * (first_hat / (jnp.sqrt(second_hat) + ADAM_EPS) + decay * weights)
    for store in stores:
        store.wait()


def run_collect(starts, ranks, one, two, master, first, second, outh, gxh, out, gx):
    vmem = pl.BlockSpec(memory_space=pltpu.VMEM)
    samples, own, columns, channels = out.shape
    final = jax.ShapeDtypeStruct((samples, own + SHIFT, columns, channels), F32)
    return pl.pallas_call(
        collect_kernel,
        in_specs=[SMEM_SPEC] + [vmem] * 8 + [HBM_SPEC] * 2,
        out_specs=[vmem] * 3 + [HBM_SPEC] * 2,
        out_shape=[jax.ShapeDtypeStruct(master.shape, F32)] * 3 + [final, final],
        scratch_shapes=[
            pltpu.VMEM((SMALL_START + 128, 128), F32),
            pltpu.VMEM((-(-(master.shape[0] + 128) // 8) * 8, 128), F32),
            pltpu.VMEM((2,) + final.shape, F32),
            pltpu.SemaphoreType.DMA((4,)),
        ],
        compiler_params=pltpu.CompilerParams(vmem_limit_bytes=62 * 1024 * 1024),
        name="collect",
    )(starts, ranks, one, two, master, first, second, outh, gxh, out, gx)


def shards(
    block_input, cotangent, window_cols, keep_mask, owner_list, master, first_moment, second_moment
):
    strips = lax.axis_size("strip")
    buckets = lax.axis_size("bucket")
    my_index = lax.axis_index(("strip", "bucket")).astype(jnp.int32).reshape(1)
    blocks = -(-(SMALL_START // 128 + 2) // 8) * 8
    owners = jnp.pad(owner_list, (0, blocks * 128 - owner_list.shape[0]), constant_values=-1).reshape(blocks, 128)
    one_rows = wire_rows(FIRST_ROWS + 3 * SMALL_SPAN, strips, buckets)
    two_rows = wire_rows(SMALL_START - FIRST_ROWS, strips, buckets)
    one, two, ranks, starts = run_dispatch(my_index, owners, master, one_rows, two_rows)
    keep = keep_mask.astype(F32) / KEEP_PROB
    output, grad_input, output_halo, grad_halo, gone, gtwo = run_block(
        window_cols, keep, block_input, cotangent, one, two, strips, buckets
    )
    first, second_new, new_weights, output, grad_input = run_collect(
        starts, ranks, gone, gtwo, master, first_moment, second_moment, output_halo, grad_halo, output, grad_input
    )
    return (output, grad_input, first, second_new, new_weights)


def solution(mesh):
    in_specs = (
        P("bucket", "strip", None, None),
        P("bucket", "strip", None, None),
        P("bucket"),
        P("bucket", None),
        P(),
        P(("strip", "bucket"), None),
        P(("strip", "bucket"), None),
        P(("strip", "bucket"), None),
    )
    out_specs = (
        P("bucket", "strip", None, None),
        P("bucket", "strip", None, None),
        P(("strip", "bucket"), None),
        P(("strip", "bucket"), None),
        P(("strip", "bucket"), None),
    )
    return jax.shard_map(shards, mesh=mesh, in_specs=in_specs, out_specs=out_specs, check_vma=False)
```

```python
import functools
import math

import jax
import jax.numpy as jnp
from jax import lax
from jax.experimental import pallas as pl
from jax.experimental.pallas import tpu as pltpu
from jax.sharding import PartitionSpec as P

C = 384
HEADS = 12
HD = 32
FF = 1536
WIN = 7
SHIFT = 3
STEP = 10
SMALL_ROWS = 39
TABLE_ROWS = 16


PRECISE = lax.Precision.HIGHEST
NORM_EPS = 1e-05
KEEP_PROB = 0.8
MASK_FILL = -100.0
BETA_ONE = 0.5
BETA_TWO = 0.5
ADAM_EPS = 1e-08
DECAY = 0.05


def row_edges():
    first = 3 * C * C // 128
    second = first + C * C // 128
    third = second + C * FF // 128
    fourth = third + FF * C // 128
    fifth = fourth + SMALL_ROWS
    return [first, second, third, fourth, fifth]


GROUPS = 3
GROUP_HEADS = HEADS // GROUPS
CELLS = WIN * 8
LANES = 64
LOG2E = math.log2(math.e)
F32 = jnp.float32
BF16 = jnp.bfloat16


def nn(left, right):
    return lax.dot_general(left, right, (((1,), (0,)), ((), ())), preferred_element_type=F32)


def nt(left, right):
    return lax.dot_general(left, right, (((1,), (1,)), ((), ())), preferred_element_type=F32)


def tn(left, right):
    return lax.dot_general(left, right, (((0,), (0,)), ((), ())), preferred_element_type=F32)


def gelu_pair(u):
    normal = 0.5 + 0.5 * lax.erf(u * math.sqrt(0.5))
    gauss = jnp.exp2(u * u * (-0.5 * LOG2E))
    return u * normal, normal + u * gauss * (1.0 / math.sqrt(2.0 * math.pi))


def row_norm(values):
    center = values - jnp.mean(values, axis=-1, keepdims=True)
    scale = lax.rsqrt(jnp.mean(center * center, axis=-1, keepdims=True) + NORM_EPS)
    return center * scale, scale


def norm_pull(grad, normal, scale):
    first = jnp.mean(grad, axis=-1, keepdims=True)
    second = jnp.mean(grad * normal, axis=-1, keepdims=True)
    return scale * (grad - first - normal * second)


def column_sum(values):
    return jnp.sum(values, axis=0, keepdims=True)


SMALL_START = 3 * C * C // 128 + C * C // 128 + 2 * C * FF // 128
SMALL_SPAN = 64


def slab_plan():
    return [
        (0, 3 * C // 128, C),
        (3 * C * C // 128, C // 128, C),
        (4 * C * C // 128, FF // 128, C),
        (4 * C * C // 128 + C * FF // 128, C // 128, FF),
    ]


ORDERS = (("x", "y", "z"), ("y", "x", "z")) * 2
LAG = 2
FIRST_ROWS = 3 * C * C // 128


def split_three(values):
    high = values.astype(BF16)
    rest = values - high.astype(F32)
    middle = rest.astype(BF16)
    return high, middle, (rest - middle.astype(F32)).astype(BF16)


def wire_rows(rows, strips, buckets):
    unit = 16 * strips * buckets
    return -(-rows // unit) * unit


def reduce_plan(strips, buckets, rows, orders):
    sizes = {"z": strips // 2, "y": 2, "x": buckets // 2}
    unit = 8 * strips * buckets
    units = rows // 2 // unit
    orders = orders[:units]
    parts, first = [], 0
    for p, order in enumerate(orders):
        length = (units // len(orders) + (p < units % len(orders))) * unit
        levels, share = [], length
        for axis in order:
            share = share // sizes[axis]
            levels.append((axis, sizes[axis], share))
        parts.append((first, length, levels))
        first += length
    return parts


def reduce_scratch(plan):
    shapes, copies = [], 0
    for _, length, levels in plan:
        shapes += [(length, 128), (length, 128)]
        for _, size, share in levels:
            shapes += [((size - 1) * share, 128), (share, 128)]
        copies += 2 + 2 * sum(size - 1 for _, size, _ in levels)
    return [pltpu.VMEM(shape, BF16) for shape in shapes] + [
        pltpu.SemaphoreType.DMA((copies,)), pltpu.SemaphoreType.DMA((copies,))
    ]


class Place:
    def __init__(self, strips, buckets):
        strip, bucket = lax.axis_index("strip"), lax.axis_index("bucket")
        self.sizes = {"z": strips // 2, "y": 2, "x": buckets // 2, "core": 2}
        self.mine = {"z": strip // 2, "y": strip % 2, "x": bucket // 2, "core": bucket % 2}
        self.above = (lax.rem(strip + strips - 1, strips), bucket)
        self.below = (lax.rem(strip + 1, strips), bucket)

    def peer(self, axis, offset):
        return lax.rem(self.mine[axis] + offset, self.sizes[axis])

    def device(self, axis, offset):
        place = dict(self.mine)
        place[axis] = self.peer(axis, offset)
        return (place["z"] * 2 + place["y"], place["x"] * 2 + place["core"])

    def greet(self, halos):
        barrier = pltpu.get_barrier_semaphore()
        partners = [self.device(axis, offset) for axis, size in self.sizes.items() for offset in range(1, size)]
        partners += [self.above, self.below] if halos else []
        for partner in partners:
            pl.semaphore_signal(barrier, inc=1, device_id=partner, device_id_type=pl.DeviceIdType.MESH)
        pl.semaphore_wait(barrier, len(partners))


def reduce_stages(place, plan, wire, scratch):
    buffers, send_sems, recv_sems = list(scratch[:-2]), scratch[-2], scratch[-1]
    half = wire.shape[0] // 2
    counter = [0]

    def span(start, length):
        return pl.ds(pl.multiple_of(start, 16), length)

    def copies_of(count):
        first = counter[0]
        counter[0] += count
        return first

    def copy(at, source, target, axis, offset):
        return pltpu.make_async_remote_copy(
            src_ref=source, dst_ref=target, send_sem=send_sems.at[at], recv_sem=recv_sems.at[at],
            device_id=place.device(axis, offset), device_id_type=pl.DeviceIdType.MESH,
        )

    def part_stages(first, length, levels):
        core_in, core_sum = buffers.pop(0), buffers.pop(0)
        boxes = [(buffers.pop(0), buffers.pop(0)) for _ in levels]
        held = [core_sum] + [total for _, total in boxes]

        def own():
            return place.mine["core"] * half + first

        def start_of(level):
            start = own()
            for axis, _, share in levels[:level]:
                start = start + place.mine[axis] * share
            return start

        core_at, back_at = copies_of(1), copies_of(1)
        down_at = [copies_of(size - 1) for _, size, _ in levels]
        up_at = [copies_of(size - 1) for _, size, _ in levels]

        def core_out():
            other = (1 - place.mine["core"]) * half + first
            return [copy(core_at, wire.at[span(other, length)], core_in, "core", 1)]

        def down(level):
            axis, size, share = levels[level]
            inbox = boxes[level][0]
            return [
                copy(down_at[level] + offset - 1, held[level].at[span(place.peer(axis, offset) * share, share)],
                     inbox.at[pl.ds((offset - 1) * share, share)], axis, offset)
                for offset in range(1, size)
            ]

        def up(level):
            axis, size, share = levels[level]
            region = wire.at[span(start_of(level + 1), share)]
            return [copy(up_at[level] + offset - 1, region, region, axis, offset) for offset in range(1, size)]

        def core_back():
            region = wire.at[span(own(), length)]
            return [copy(back_at, region, region, "core", 1)]

        def add_core():
            core_sum[...] = wire[span(own(), length), :] + core_in[...]

        def add(level):
            axis, size, share = levels[level]
            inbox, total = boxes[level]
            value = held[level][span(place.mine[axis] * share, share), :].astype(F32)
            for offset in range(1, size):
                value = value + inbox[(offset - 1) * share : offset * share, :].astype(F32)
            if level + 1 < len(levels):
                total[...] = value.astype(BF16)
            else:
                wire[span(start_of(len(levels)), share), :] = value.astype(BF16)

        count = len(levels)
        moves = [core_out] + [functools.partial(down, level) for level in range(count)]
        moves += [functools.partial(up, level) for level in reversed(range(count))] + [core_back]
        work = {1: add_core}
        for level in range(count):
            work[level + 2] = functools.partial(add, level)

        def stage(index):
            if index > 0:
                for one in moves[index - 1]():
                    one.wait()
            if index in work:
                work[index]()
            if index < len(moves):
                for one in moves[index]():
                    one.start()

        return [functools.partial(stage, index) for index in range(len(moves) + 1)]

    return [part_stages(*part) for part in plan]


def reduce_ticks(parts):
    ticks = []
    for p, stages in enumerate(parts):
        for index, stage in enumerate(stages):
            at = index + p // 2
            while len(ticks) <= at:
                ticks.append([])
            ticks[at].append(stage)

    def run(tick):
        for stage in tick:
            stage()

    return [functools.partial(run, tick) for tick in ticks]


def tick_slots(ticks, slots):
    return [[tick for i, tick in enumerate(ticks) if i * slots // len(ticks) == slot] for slot in range(slots)]


def head_bits():
    lane_head = lax.broadcasted_iota(jnp.int32, (1, 128), 1) // HD
    return [(lane_head == h).astype(F32).astype(BF16) for h in range(GROUP_HEADS)]


def stack_of(part, bits):
    return jnp.concatenate([part * bit for bit in bits], axis=0)


def unstack(part):
    lane_head = lax.broadcasted_iota(jnp.int32, (1, 128), 1) // HD
    total = None
    for h in range(GROUP_HEADS):
        piece = jnp.where(lane_head == h, part[h * LANES : h * LANES + CELLS], 0.0)
        total = piece if total is None else total + piece
    return total


def load_matrix(target, wire, first, rows):
    for j in range(target.shape[1] // 128):
        target[:, j * 128 : j * 128 + 128] = wire[first + j * rows : first + (j + 1) * rows, :]


def load_vectors(refs, wire, first):
    small = jnp.zeros((SMALL_SPAN, 128), F32)
    for i in range(3):
        small = small + wire[FIRST_ROWS + i * SMALL_SPAN : FIRST_ROWS + (i + 1) * SMALL_SPAN, :].astype(F32)
    for ref, row in zip(refs, first):
        for j in range(ref.shape[1] // 128):
            ref[:, j * 128 : j * 128 + 128] = small[row + j : row + j + 1]


def to_windows(line, last, main, halo, step, target):
    slabs, columns = C // 128, main.shape[2]
    wide, own = columns // WIN, WIN - SHIFT
    wrapped_row = lax.broadcasted_iota(jnp.int32, (8, 128), 0) >= own
    for a in range(WIN):
        row = main[0, SHIFT + a] if a < own else halo[step, a - own].astype(F32)
        for s in range(slabs):
            line[s, a, 8 : 8 + columns, :] = row[:, s * 128 : s * 128 + 128]
    for a in range(WIN):
        for s in range(slabs):
            front = line[s, a, 8 - own : 16 - own, :]
            for w in range(wide):
                first = 8 + w * WIN + SHIFT
                tile = jnp.where(wrapped_row & (w == last), front, line[s, a, first : first + 8, :])
                target[w * CELLS + a * 8 : w * CELLS + a * 8 + 8, s * 128 : s * 128 + 128] = tile


def from_windows(line, width, source, main, halo, step):
    slabs, columns = C // 128, main.shape[2]
    wide, own = columns // WIN, WIN - SHIFT
    for w in range(wide):
        for a in range(WIN):
            for s in range(slabs):
                first = 8 + w * WIN + SHIFT
                line[s, a, first : first + 8, :] = source[
                    w * CELLS + a * 8 : w * CELLS + a * 8 + 8, s * 128 : s * 128 + 128
                ]
    kept = lax.broadcasted_iota(jnp.int32, (columns, 128), 0) < width
    front = lax.broadcasted_iota(jnp.int32, (8, 128), 0) < SHIFT
    for a in range(WIN):
        for s in range(slabs):
            wrapped = line[s, a, pl.ds(width + 8, 8), :]
            line[s, a, 8:16, :] = jnp.where(front, wrapped, line[s, a, 8:16, :])
            row = jnp.where(kept, line[s, a, 8 : 8 + columns, :], 0.0)
            if a < own:
                main[0, a, :, s * 128 : s * 128 + 128] = row
            else:
                halo[step, a - own, :, s * 128 : s * 128 + 128] = row.astype(BF16)


def place_onehot(row):
    shape = (128, HEADS * LANES)
    source = lax.broadcasted_iota(jnp.int32, shape, 0)
    lane = lax.broadcasted_iota(jnp.int32, shape, 1)
    return (lane == source // 8 * LANES + row * 8 + source % 8).astype(F32).astype(BF16)


def offset_onehot(column):
    shape = (256, 128)
    source = lax.broadcasted_iota(jnp.int32, shape, 0)
    lane = lax.broadcasted_iota(jnp.int32, shape, 1)
    wanted = (lane % 8 - column + WIN - 1) * HEADS + lane // 8
    return ((source == wanted) & (lane < HEADS * 8)).astype(F32).astype(BF16)


SPAN = 2 * WIN - 1


def build_bias(raw, last_strip, offsets, spread, bias):
    flat = jnp.concatenate([raw[r : r + 1] for r in range(TABLE_ROWS)], axis=1)
    offsets[...] = jnp.zeros_like(offsets)
    spread[...] = jnp.zeros_like(spread)
    for d in range(SPAN):
        offsets[SPAN - 1 - d : SPAN - d, 0 : SPAN * HEADS] = flat[:, d * SPAN * HEADS : (d + 1) * SPAN * HEADS]
    terms = split_three(offsets[...])
    for column in range(WIN):
        pick = offset_onehot(column)
        part = nn(terms[0], pick) + nn(terms[1], pick) + nn(terms[2], pick)
        spread[pl.ds(column, SPAN, stride=8), :] = part[0:SPAN]
    terms = split_three(spread[...])
    total = jnp.zeros((CELLS, HEADS * LANES), F32)
    for row in range(WIN):
        pick = place_onehot(row)
        for term in terms:
            total = total + nn(term[8 * (WIN - 1 - row) : 8 * (WIN - 1 - row) + CELLS], pick)
    shape = (CELLS, HEADS * LANES)
    key = lax.broadcasted_iota(jnp.int32, shape, 0)
    query = lax.broadcasted_iota(jnp.int32, shape, 1) % LANES
    edge = WIN - SHIFT
    by_row = ((key // 8 >= edge) != (query // 8 >= edge)) & last_strip
    by_col = (key % 8 >= edge) != (query % 8 >= edge)
    for variant, masked in enumerate((by_row, by_row | by_col)):
        value = (total + jnp.where(masked, MASK_FILL, 0.0)) * LOG2E
        value = jnp.where(key % 8 < WIN, value, -1e30)
        for g in range(GROUPS):
            bias[variant, g] = value[:, g * GROUP_HEADS * LANES : (g + 1) * GROUP_HEADS * LANES]


def pull_bias(sums, spread):
    grads = jnp.concatenate([sums[g] for g in range(GROUPS)], axis=1)
    high, middle, _ = split_three(grads)
    spread[...] = jnp.zeros_like(spread)
    for row in range(WIN):
        pick = place_onehot(row)
        first = 8 * (WIN - 1 - row)
        spread[first : first + CELLS, :] += nt(high, pick) + nt(middle, pick)
    total = jnp.zeros((SPAN, 256), F32)
    for column in range(WIN):
        pick = offset_onehot(column)
        high, middle, _ = split_three(spread[pl.ds(column, SPAN, stride=8), :])
        total = total + nt(high, pick) + nt(middle, pick)
    flat = [total[SPAN - 1 - d : SPAN - d, 0 : SPAN * HEADS] for d in range(SPAN)]
    flat.append(jnp.zeros((1, TABLE_ROWS * 128 - SPAN * SPAN * HEADS), F32))
    flat = jnp.concatenate(flat, axis=1)
    return jnp.concatenate([flat[:, r * 128 : r * 128 + 128] for r in range(TABLE_ROWS)], axis=0)


def rank_rows(me, owner_ref, rank_ref, start_ref):
    blocks = owner_ref.shape[0]
    mine = (owner_ref[...] == me).astype(F32)
    low = mine.astype(BF16)
    row = lax.broadcasted_iota(jnp.int32, (128, 128), 0)
    col = lax.broadcasted_iota(jnp.int32, (128, 128), 1)
    within = nn(low, (row <= col).astype(F32).astype(BF16))
    sums = nn(low, jnp.ones((128, 128), BF16))
    below = lax.broadcasted_iota(jnp.int32, (blocks, blocks), 1) < lax.broadcasted_iota(jnp.int32, (blocks, blocks), 0)
    start = nn(below.astype(F32).astype(BF16), sums.astype(BF16))
    rank_ref[...] = jnp.where(mine > 0, within - 1.0, -1.0)
    start_ref[...] = start.astype(jnp.int32)


def spread_rows(first, slabs, rows, target, offset, rank_ref, start_s, padded, packed):
    slot = lax.broadcasted_iota(jnp.int32, (128, 128), 0).astype(F32)

    def block(b, _):
        at = first // 128 + b
        hot = (slot == rank_ref[pl.ds(at, 1), :]).astype(F32).astype(BF16)
        begin = jnp.clip(start_s[at, 0], 0, padded.shape[0] - 128)
        held = padded[pl.ds(begin, 128), :].astype(BF16)
        packed[pl.ds(pl.multiple_of(b * 128, 128), 128), :] = tn(hot, held)
        return 0

    count = slabs * rows // 128
    lax.fori_loop(0, count, block, 0, unroll=3 if count % 3 == 0 else 1)
    for j in range(slabs):
        target[offset + j * rows : offset + (j + 1) * rows, :] = packed[pl.ds(j, rows, stride=slabs), :].astype(BF16)


def spread_small(target, rank_ref, start_s, padded):
    slot = lax.broadcasted_iota(jnp.int32, (128, 128), 0).astype(F32)
    small = SMALL_START // 128
    hot = (slot == rank_ref[small : small + 1, :]).astype(F32).astype(BF16)
    begin = jnp.clip(start_s[small, 0], 0, padded.shape[0] - 128)
    for i, piece in enumerate(split_three(padded[pl.ds(begin, 128), :])):
        first = FIRST_ROWS + i * SMALL_SPAN
        target[first : first + SMALL_SPAN, :] = tn(hot, piece)[0:SMALL_SPAN].astype(BF16)
    used = FIRST_ROWS + 3 * SMALL_SPAN
    target[used:, :] = jnp.zeros((target.shape[0] - used, 128), BF16)


def block_kernel(
    strips, buckets, images, plan_one, plan_two,
    cols_ref, keep_ref, x_ref, dy_ref, x_any, dy_any, owner_ref, master_ref,
    out_ref, gx_ref, rank_ref, start_ref, outh_any, gxh_any, gone_any, gtwo_any,
    wq_ref, wp_ref, wu_ref, wd_ref, bq_ref, bp_ref, bu_ref, bd_ref, g1_ref, b1_ref, g2_ref, b2_ref,
    gwq_ref, gwp_ref, gwu_ref, gwdt_ref, gbq_ref, gbp_ref, gbu_ref, gbd_ref, gg1_ref, gb1_ref, gg2_ref, gb2_ref,
    bias, gs_ref, offsets, spread,
    xw, zs, qkv, prob, ctx, gctx, gx1s,
    line, dyw, x1s, n2s, h2s, gfs, ys, gh2s, resw, htr, gtr, gscores, gqkv,
    fetched, halo_out, halo_in, back_in, wire_one, wire_two, padded, packed, start_s,
    local_sems, send_sems, recv_sems, *scratch,
):
    step = pl.program_id(0)
    tokens = dyw.shape[0]
    wide = tokens // CELLS
    place = Place(strips, buckets)
    last = cols_ref[0] - 1
    width = cols_ref[0] * WIN
    count_one = len(reduce_scratch(plan_one))
    parts_one = reduce_stages(place, plan_one, wire_one, scratch[:count_one])
    parts_two = reduce_stages(place, plan_two, wire_two, scratch[count_one:])
    gather_ticks = reduce_ticks(parts_one + [[]] * (4 - len(parts_one)) + parts_two)
    early = len(parts_one[0])
    one_ticks, two_ticks = reduce_ticks(parts_one), reduce_ticks(parts_two)

    def halo(kind, image):
        return pltpu.make_async_remote_copy(
            src_ref=halo_out.at[kind % 2, image], dst_ref=(halo_in if kind < 2 else back_in).at[kind % 2, image],
            send_sem=send_sems.at[kind, image], recv_sem=recv_sems.at[kind, image],
            device_id=place.above if kind < 2 else place.below, device_id_type=pl.DeviceIdType.MESH,
        )

    def fetch(array, image, kind):
        return pltpu.make_async_copy(array.at[image, pl.ds(0, SHIFT)], fetched.at[kind], local_sems.at[kind])

    def send_rows(kind, image, held):
        halo_out[kind, image] = fetched[held].astype(BF16)
        halo(kind, image).start()

    @pl.when(step == 0)
    def _():
        first = [fetch(x_any, image, image) for image in range(2)]
        for copy in first:
            copy.start()
        me = lax.axis_index("strip") * buckets + lax.axis_index("bucket")
        rank_rows(me, owner_ref, rank_ref, start_ref)
        starts = pltpu.make_async_copy(start_ref, start_s, local_sems.at[2])
        starts.start()
        capacity = master_ref.shape[0]
        padded[0:capacity, :] = master_ref[...]
        padded[capacity:, :] = jnp.zeros((padded.shape[0] - capacity, 128), F32)
        starts.wait()
        plans = slab_plan()
        spread_rows(*plans[0], wire_one, 0, rank_ref, start_s, padded, packed)
        spread_small(wire_one, rank_ref, start_s, padded)
        place.greet(True)
        gather_ticks[0]()
        for image in range(2):
            first[image].wait()
            send_rows(0, image, image)
        fetch(x_any, 2, 0).start()
        fetch(dy_any, 0, 1).start()
        for plan in plans[1:3]:
            spread_rows(*plan, wire_two, plan[0] - FIRST_ROWS, rank_ref, start_s, padded, packed)
        gather_ticks[1]()
        spread_rows(*plans[3], wire_two, plans[3][0] - FIRST_ROWS, rank_ref, start_s, padded, packed)
        used = SMALL_START - FIRST_ROWS
        wire_two[used:, :] = jnp.zeros((wire_two.shape[0] - used, 128), BF16)
        gather_ticks[2]()
        line[...] = jnp.zeros_like(line)
        for ref in (gwq_ref, gwp_ref, gwu_ref, gwdt_ref, gbq_ref, gbp_ref, gbu_ref, gbd_ref,
                    gg1_ref, gb1_ref, gg2_ref, gb2_ref, gs_ref, qkv, gctx):
            ref[...] = jnp.zeros_like(ref)
        for tick in gather_ticks[3:early]:
            tick()
        load_matrix(wq_ref, wire_one, 0, C)
        load_vectors((bq_ref, bp_ref, bu_ref, bd_ref, g1_ref, b1_ref, g2_ref, b2_ref), wire_one,
                     (0, 9, 12, 24, 27, 30, 33, 36))
        raw = jnp.zeros((SMALL_SPAN, 128), F32)
        for i in range(3):
            raw = raw + wire_one[FIRST_ROWS + i * SMALL_SPAN : FIRST_ROWS + (i + 1) * SMALL_SPAN, :].astype(F32)
        build_bias(raw[SMALL_ROWS : SMALL_ROWS + TABLE_ROWS], lax.axis_index("strip") == strips - 1, offsets, spread, bias)

    @pl.when((step > 0) & (step + 1 < images))
    def _():
        fetch(x_any, step + 1, 0).wait()
        send_rows(0, step + 1, 0)

    @pl.when((step > 0) & (step + 2 < images))
    def _():
        fetch(x_any, step + 2, 0).start()

    @pl.when((step > 0) & (step - 1 < images))
    def _():
        fetch(dy_any, step - 1, 1).wait()
        send_rows(1, step - 1, 1)

    @pl.when((step > 0) & (step < images))
    def _():
        fetch(dy_any, step, 1).start()

    bits = head_bits()

    def attend(image):
        at = lax.rem(image, LAG)
        halo(0, image).wait_recv()
        to_windows(line, last, x_ref, halo_in.at[0], image, xw.at[at])
        normal, _ = row_norm(xw[at])
        zs[at] = (normal * g1_ref[...] + b1_ref[...]).astype(BF16)
        triple = nn(zs[at], wq_ref[...]) + bq_ref[...]
        for w in range(wide):
            qkv[at, w, 0:CELLS, :] = triple[w * CELLS : w * CELLS + CELLS].astype(BF16)
        for w in range(wide):
            variant = (w == last).astype(jnp.int32)
            for g in range(GROUPS):
                q = qkv[at, w, :, g * 128 : g * 128 + 128]
                k = qkv[at, w, 0:CELLS, C + g * 128 : C + g * 128 + 128]
                v = qkv[at, w, 0:CELLS, 2 * C + g * 128 : 2 * C + g * 128 + 128]
                s = nt(k, stack_of(q, bits)) * (HD ** (-0.5) * LOG2E) + bias[variant, g]
                e = jnp.exp2(s - jnp.max(s, axis=0, keepdims=True))
                a = (e * (1.0 / jnp.sum(e, axis=0, keepdims=True))).astype(BF16)
                prob[at, w, g] = a
                resw[w * CELLS : w * CELLS + CELLS, g * 128 : g * 128 + 128] = unstack(tn(a, v))
        ctx[at] = resw[...].astype(BF16)

    def feed(image):
        at = lax.rem(image, LAG)
        keep_one = keep_ref[image, 0].astype(F32) * (1.0 / KEEP_PROB)
        keep_two = keep_ref[image, 1].astype(F32) * (1.0 / KEEP_PROB)
        x1 = xw[at] + keep_one * (nn(ctx[at], wp_ref[...]) + bp_ref[...])
        x1s[...] = x1
        normal, scale_two = row_norm(x1)
        n2s[...] = normal
        h2 = (normal * g2_ref[...] + b2_ref[...]).astype(BF16)
        h2s[...] = h2
        htr[...] = h2.astype(F32).T.astype(BF16)

        halo(1, image).wait_recv()
        to_windows(line, last, dy_ref, halo_in.at[1], image, dyw)
        token = lax.broadcasted_iota(jnp.int32, (tokens, 1), 0)
        valid = ((token % 8 < WIN) & (token < cols_ref[0] * CELLS)).astype(F32)
        gy = dyw[...] * valid
        gf = (gy * keep_two).astype(BF16)
        gfs[...] = gf
        gbd_ref[...] += column_sum(gf.astype(F32))
        gtr[...] = gf.astype(F32).T.astype(BF16)
        ys[...] = jnp.zeros_like(ys)
        gh2s[...] = jnp.zeros_like(gh2s)
        chunk = 512
        for j in range(FF // chunk):
            part = slice(j * chunk, (j + 1) * chunk)
            u = nn(h2s[...], wu_ref[:, part]) + bu_ref[:, part]
            gm = nt(gfs[...], wd_ref[part, :])
            m, slope = gelu_pair(u)
            m = m.astype(BF16)
            gu = (gm * slope).astype(BF16)
            ys[...] += nn(m, wd_ref[part, :])
            gwdt_ref[:, part] += nn(gtr[...], m)
            gwu_ref[:, part] += nn(htr[...], gu)
            gbu_ref[:, part] += column_sum(gu.astype(F32))
            gh2s[...] += nt(gu, wu_ref[:, part])

        resw[...] = (x1s[...] + keep_two * (ys[...] + bd_ref[...])) * valid
        halo(1, image).wait_send()
        from_windows(line, width, resw, out_ref, halo_out.at[1], image)
        halo(3, image).start()

        gh2 = gh2s[...]
        gg2_ref[...] += column_sum(gh2 * n2s[...])
        gb2_ref[...] += column_sum(gh2)
        gx1 = dyw[...] * valid + norm_pull(gh2 * g2_ref[...], n2s[...], scale_two)
        gx1s[at] = gx1
        ga = (keep_one * gx1).astype(BF16)
        gbp_ref[...] += column_sum(ga.astype(F32))
        gwp_ref[...] += nn(ctx[at].astype(F32).T.astype(BF16), ga)
        gc = nt(ga, wp_ref[...])
        for w in range(wide):
            gctx[at, w, 0:CELLS, :] = gc[w * CELLS : w * CELLS + CELLS].astype(BF16)

    def pull(image, middle):
        at = lax.rem(image, LAG)
        scale = HD ** (-0.5)
        for w in range(wide):
            rows = slice(w * CELLS, w * CELLS + CELLS)
            for g in range(GROUPS):
                v = qkv[at, w, 0:CELLS, 2 * C + g * 128 : 2 * C + g * 128 + 128]
                gstack = stack_of(gctx[at, w, :, g * 128 : g * 128 + 128], bits)
                low = prob[at, w, g]
                a = low.astype(F32)
                grad = nt(v, gstack)
                inner = jnp.sum(grad * a, axis=0, keepdims=True)
                gscores[w, g] = a * (grad - inner)
                gqkv[rows, 2 * C + g * 128 : 2 * C + g * 128 + 128] = nn(low, gstack)
        middle()
        for w in range(wide):
            rows = slice(w * CELLS, w * CELLS + CELLS)
            for g in range(GROUPS):
                q = qkv[at, w, :, g * 128 : g * 128 + 128]
                k = qkv[at, w, 0:CELLS, C + g * 128 : C + g * 128 + 128]
                gs = gscores[w, g].astype(BF16)
                gqkv[rows, g * 128 : g * 128 + 128] = unstack(tn(gs, k)) * scale
                gqkv[rows, C + g * 128 : C + g * 128 + 128] = nn(gs, stack_of(q, bits)) * scale
        gs_ref[...] += jnp.sum(gscores[...], axis=0)

        gtriple = gqkv[...].astype(BF16)
        gbq_ref[...] += column_sum(gtriple.astype(F32))
        gwq_ref[...] += nn(zs[at].astype(F32).T.astype(BF16), gtriple)
        gz = nt(gtriple, wq_ref[...]).astype(BF16).astype(F32)
        normal, scale_one = row_norm(xw[at])
        gg1_ref[...] += column_sum(gz * normal)
        gb1_ref[...] += column_sum(gz)
        resw[...] = gx1s[at] + norm_pull(gz * g1_ref[...], normal, scale_one)
        halo(0, image).wait_send()
        from_windows(line, width, resw, gx_ref, halo_out.at[0], image)
        halo(2, image).start()

    def pack_two():
        first = 0
        for grad in (gwp_ref, gwu_ref):
            for j in range(grad.shape[1] // 128):
                wire_two[first : first + C, :] = grad[:, j * 128 : j * 128 + 128].astype(BF16)
                first += C
        for j in range(C // 128):
            wire_two[first : first + FF, :] = gwdt_ref[j * 128 : j * 128 + 128, :].T.astype(BF16)
            first += FF
        wire_two[first:, :] = jnp.zeros((wire_two.shape[0] - first, 128), BF16)

    def pack_one():
        for j in range(3 * C // 128):
            wire_one[j * C : (j + 1) * C, :] = gwq_ref[:, j * 128 : j * 128 + 128].astype(BF16)
        vectors = (gbq_ref, gbp_ref, gbu_ref, gbd_ref, gg1_ref, gb1_ref, gg2_ref, gb2_ref)
        pieces = [ref[:, j * 128 : j * 128 + 128] for ref in vectors for j in range(ref.shape[1] // 128)]
        pieces.append(pull_bias(gs_ref, spread))
        pieces.append(jnp.zeros((wire_one.shape[0] - FIRST_ROWS - SMALL_ROWS - TABLE_ROWS, 128), F32))
        wire_one[FIRST_ROWS:, :] = jnp.concatenate(pieces, axis=0).astype(BF16)

    @pl.when(step == LAG)
    def _():
        first = 0
        for ref, rows in ((wp_ref, C), (wu_ref, C), (wd_ref, FF)):
            load_matrix(ref, wire_two, first, rows)
            first += ref.shape[1] // 128 * rows

    @pl.when((step >= LAG) & (step < images + LAG))
    def _():
        feed(step - LAG)

    @pl.when((step >= LAG) & (step < images))
    def _():
        pull(step - LAG, lambda: None)

    @pl.when(step < images)
    def _():
        attend(step)

    late = gather_ticks[early:]
    for k in range(LAG):
        mine = late[k * len(late) // LAG : (k + 1) * len(late) // LAG]

        @pl.when(step == k)
        def _(mine=mine):
            for tick in mine:
                tick()

    @pl.when(step == images + LAG - 1)
    def _():
        pack_two()
        two_ticks[0]()

    for k in range(LAG):

        @pl.when(step == images + LAG + k)
        def _(k=k):
            two_ticks[2 * k + 1]()
            pull(images - LAG + k, two_ticks[2 * k + 2])

    @pl.when(step == images + 2 * LAG - 1)
    def _():
        pack_one()
        rest = two_ticks[2 * LAG + 1 :]
        for i in range(max(len(rest), len(one_ticks))):
            for ticks in (one_ticks, rest):
                if i < len(ticks):
                    ticks[i]()
        for image in range(images):
            for kind in range(2, 4):
                halo(kind, image).wait()
        stores = [
            pltpu.make_async_copy(source, target, local_sems.at[i])
            for i, (source, target) in enumerate(
                ((wire_one, gone_any), (wire_two, gtwo_any), (back_in.at[0], gxh_any), (back_in.at[1], outh_any))
            )
        ]
        for copy in stores:
            copy.start()
        for copy in stores:
            copy.wait()


SMEM_SPEC = pl.BlockSpec(memory_space=pltpu.SMEM)
HBM_SPEC = pl.BlockSpec(memory_space=pl.ANY)


def whole(shape):
    return pl.BlockSpec(shape, lambda i: (0,) * len(shape))


def run_block(cols, keep, x, dy, owners, master, one_rows, two_rows, strips, buckets):
    samples, rows, columns, _ = x.shape
    wide = columns // WIN
    tokens = wide * CELLS
    own = rows - SHIFT
    halo = (samples, SHIFT, columns, C)
    plan_one = reduce_plan(strips, buckets, one_rows, ORDERS[:2])
    plan_two = reduce_plan(strips, buckets, two_rows, ORDERS)
    top = samples - 1

    def attended(i):
        return (jnp.minimum(i, top), 0, 0, 0)

    def fed(i):
        return (jnp.minimum(jnp.maximum(i - LAG, 0), top), 0, 0, 0)

    def pulled(i):
        early = jnp.minimum(jnp.maximum(i - LAG, 0), top - LAG)
        return (early + jnp.maximum(i - (samples + LAG) + 1, 0), 0, 0, 0)

    vectors = [3 * C, C, FF, C, C, C, C, C]
    sums = (GROUPS, CELLS, GROUP_HEADS * LANES)

    def struct(shape, dtype=F32):
        return jax.ShapeDtypeStruct(shape, dtype)

    token = pltpu.VMEM((tokens, C), F32)
    low = pltpu.VMEM((tokens, C), BF16)
    turned = pltpu.VMEM((C, tokens), BF16)
    scratch = [pltpu.VMEM(s, BF16) for s in ((C, 3 * C), (C, C), (C, FF), (FF, C))]
    scratch += [pltpu.VMEM((1, size), F32) for size in vectors]
    scratch += [pltpu.VMEM(s, F32) for s in ((C, 3 * C), (C, C), (C, FF), (C, FF))]
    scratch += [pltpu.VMEM((1, size), F32) for size in vectors]
    scratch += [
        pltpu.VMEM((2,) + sums, F32), pltpu.VMEM(sums, F32),
        pltpu.VMEM((16, 256), F32), pltpu.VMEM((SPAN * 8, 128), F32),
        pltpu.VMEM((LAG, tokens, C), F32), pltpu.VMEM((LAG, tokens, C), BF16),
        pltpu.VMEM((LAG, wide, LANES, 3 * C), BF16), pltpu.VMEM((LAG, wide) + sums, BF16),
        pltpu.VMEM((LAG, tokens, C), BF16), pltpu.VMEM((LAG, wide, LANES, C), BF16),
        pltpu.VMEM((LAG, tokens, C), F32),
        pltpu.VMEM((C // 128, WIN, columns + 16, 128), F32),
        token, token, token, low, low, token, token, token, turned, turned,
        pltpu.VMEM((wide,) + sums, F32), pltpu.VMEM((tokens, 3 * C), F32),
        pltpu.VMEM((2,) + halo[1:], F32),
        pltpu.VMEM((2,) + halo, BF16), pltpu.VMEM((2,) + halo, BF16), pltpu.VMEM((2,) + halo, BF16),
        pltpu.VMEM((one_rows, 128), BF16), pltpu.VMEM((two_rows, 128), BF16),
        pltpu.VMEM((-(-(master.shape[0] + 128) // 8) * 8, 128), F32), pltpu.VMEM((C * FF // 128, 128), F32),
        pltpu.SMEM(owners.shape, jnp.int32),
        pltpu.SemaphoreType.DMA((4,)), pltpu.SemaphoreType.DMA((4, samples)), pltpu.SemaphoreType.DMA((4, samples)),
    ]
    block = (1, rows, columns, C)
    part = (1, own, columns, C)
    return pl.pallas_call(
        lambda *refs: block_kernel(strips, buckets, samples, plan_one, plan_two, *refs),
        grid=(samples + 2 * LAG,),
        in_specs=[SMEM_SPEC, SMEM_SPEC, pl.BlockSpec(block, attended), pl.BlockSpec(block, fed)] + [HBM_SPEC] * 2
        + [whole(owners.shape), whole(master.shape)],
        out_specs=[pl.BlockSpec(part, fed), pl.BlockSpec(part, pulled)] + [whole(owners.shape)] * 2 + [HBM_SPEC] * 4,
        out_shape=[struct((samples, own, columns, C)), struct((samples, own, columns, C)), struct(owners.shape),
                   struct(owners.shape, jnp.int32), struct(halo, BF16), struct(halo, BF16), struct((one_rows, 128), BF16),
                   struct((two_rows, 128), BF16)],
        scratch_shapes=scratch + reduce_scratch(plan_one) + reduce_scratch(plan_two),
        compiler_params=pltpu.CompilerParams(
            vmem_limit_bytes=62 * 1024 * 1024, collective_id=1, has_side_effects=True
        ),
        name="block",
    )(cols, keep, x, dy, x, dy, owners, master)


def collect_kernel(
    start_ref, rank_ref, one_any, two_any, master_ref, first_ref, second_ref, outh_any, gxh_any, out_any, gx_any,
    first_out, second_out, master_out, out_final, gx_final, packed, total, wide, one, two, halos, sems,
):
    own = out_any.shape[1]
    pairs = [(one_any, one), (two_any, two), (outh_any, halos.at[0]), (gxh_any, halos.at[1])]
    pairs += [(main, wide.at[i, :, pl.ds(SHIFT, own)]) for i, main in enumerate((out_any, gx_any))]
    loads = [pltpu.make_async_copy(source, target, sems.at[i]) for i, (source, target) in enumerate(pairs)]
    stores = [pltpu.make_async_copy(wide.at[i], final, sems.at[6 + i]) for i, final in enumerate((out_final, gx_final))]
    for load in loads:
        load.start()
    capacity = master_ref.shape[0]
    total[...] = jnp.zeros_like(total)
    slot = lax.broadcasted_iota(jnp.int32, (128, 128), 0).astype(F32)

    def block(b, _):
        hot = (slot == rank_ref[pl.ds(b, 1), :]).astype(F32).astype(BF16)
        part = nn(hot, packed[pl.ds(pl.multiple_of(b * 128, 128), 128), :].astype(BF16))
        where = pl.ds(start_ref[b, 0], 128)
        total[where, :] = total[where, :] + part
        return 0

    def unpack(plan, source, offset):
        first, slabs, rows = plan
        for j in range(slabs):
            packed[pl.ds(first + j, rows, stride=slabs), :] = source[
                first - offset + j * rows : first - offset + (j + 1) * rows, :
            ].astype(F32)

    plans = slab_plan()
    small = SMALL_START // 128
    loads[0].wait()
    unpack(plans[0], one, 0)
    packed[SMALL_START : SMALL_START + SMALL_SPAN, :] = one[FIRST_ROWS : FIRST_ROWS + SMALL_SPAN, :].astype(F32)
    packed[SMALL_START + SMALL_SPAN : SMALL_START + 128, :] = jnp.zeros((128 - SMALL_SPAN, 128), F32)
    lax.fori_loop(0, FIRST_ROWS // 128, block, 0, unroll=9)
    for i in range(2):
        loads[2 + i].wait()
        wide[i, :, 0:SHIFT] = halos[i].astype(F32)
        loads[4 + i].wait()
        stores[i].start()
    loads[1].wait()
    for plan in plans[1:]:
        unpack(plan, two, FIRST_ROWS)
    lax.fori_loop(FIRST_ROWS // 128, small, block, 0, unroll=9)
    block(small, 0)
    slots = lax.broadcasted_iota(jnp.int32, (capacity, 1), 0)
    edges = [edge // 128 for edge in row_edges()[:4]] + [SMALL_START // 128 + 1]
    rates = [2.0 / math.sqrt(C), 2.0 / math.sqrt(C // 8), 2.0 / math.sqrt(C), 2.0 / math.sqrt(FF), 1.0, 0.0]
    rate = jnp.full((capacity, 1), rates[0], F32)
    for edge, amount in zip(edges, rates[1:]):
        rate = jnp.where(slots >= start_ref[edge, 0], amount, rate)
    decay = jnp.where(slots < start_ref[edges[3], 0], DECAY, 0.0)
    grads = total[0:capacity, :]
    weights = master_ref[...]
    first = BETA_ONE * first_ref[...] + (1.0 - BETA_ONE) * grads
    second = BETA_TWO * second_ref[...] + (1.0 - BETA_TWO) * grads * grads
    first_out[...] = first
    second_out[...] = second
    first_hat = first / (1.0 - BETA_ONE**STEP)
    second_hat = second / (1.0 - BETA_TWO**STEP)
    master_out[...] = weights - rate * (first_hat / (jnp.sqrt(second_hat) + ADAM_EPS) + decay * weights)
    for store in stores:
        store.wait()


def run_collect(starts, ranks, one, two, master, first, second, outh, gxh, out, gx):
    vmem = pl.BlockSpec(memory_space=pltpu.VMEM)
    samples, own, columns, channels = out.shape
    final = jax.ShapeDtypeStruct((samples, own + SHIFT, columns, channels), F32)
    return pl.pallas_call(
        collect_kernel,
        in_specs=[SMEM_SPEC, vmem, HBM_SPEC, HBM_SPEC] + [vmem] * 3 + [HBM_SPEC] * 4,
        out_specs=[vmem] * 3 + [HBM_SPEC] * 2,
        out_shape=[jax.ShapeDtypeStruct(master.shape, F32)] * 3 + [final, final],
        scratch_shapes=[
            pltpu.VMEM((SMALL_START + 128, 128), F32),
            pltpu.VMEM((-(-(master.shape[0] + 128) // 8) * 8, 128), F32),
            pltpu.VMEM((2,) + final.shape, F32),
            pltpu.VMEM(one.shape, BF16),
            pltpu.VMEM(two.shape, BF16),
            pltpu.VMEM((2,) + outh.shape, BF16),
            pltpu.SemaphoreType.DMA((8,)),
        ],
        compiler_params=pltpu.CompilerParams(vmem_limit_bytes=62 * 1024 * 1024),
        name="collect",
    )(starts, ranks, one, two, master, first, second, outh, gxh, out, gx)


def shards(
    block_input, cotangent, window_cols, keep_mask, owner_list, master, first_moment, second_moment
):
    strips = lax.axis_size("strip")
    buckets = lax.axis_size("bucket")
    blocks = -(-(SMALL_START // 128 + 2) // 8) * 8
    owners = jnp.pad(owner_list, (0, blocks * 128 - owner_list.shape[0]), constant_values=-1).reshape(blocks, 128)
    one_rows = wire_rows(FIRST_ROWS + 3 * SMALL_SPAN, strips, buckets)
    two_rows = wire_rows(SMALL_START - FIRST_ROWS, strips, buckets)
    output, grad_input, ranks, starts, output_halo, grad_halo, gone, gtwo = run_block(
        window_cols, keep_mask, block_input, cotangent, owners, master, one_rows, two_rows, strips, buckets
    )
    first, second_new, new_weights, output, grad_input = run_collect(
        starts, ranks, gone, gtwo, master, first_moment, second_moment, output_halo, grad_halo, output, grad_input
    )
    return (output, grad_input, first, second_new, new_weights)


def solution(mesh):
    in_specs = (
        P("bucket", "strip", None, None),
        P("bucket", "strip", None, None),
        P("bucket"),
        P("bucket", None),
        P(),
        P(("strip", "bucket"), None),
        P(("strip", "bucket"), None),
        P(("strip", "bucket"), None),
    )
    out_specs = (
        P("bucket", "strip", None, None),
        P("bucket", "strip", None, None),
        P(("strip", "bucket"), None),
        P(("strip", "bucket"), None),
        P(("strip", "bucket"), None),
    )
    return jax.shard_map(shards, mesh=mesh, in_specs=in_specs, out_specs=out_specs, check_vma=False)
```

```python
import functools
import math

import jax
import jax.numpy as jnp
from jax import lax
from jax.experimental import pallas as pl
from jax.experimental.pallas import tpu as pltpu
from jax.sharding import PartitionSpec as P

C = 384
HEADS = 12
HD = 32
FF = 1536
WIN = 7
SHIFT = 3
STEP = 10
SMALL_ROWS = 39
TABLE_ROWS = 16


PRECISE = lax.Precision.HIGHEST
NORM_EPS = 1e-05
KEEP_PROB = 0.8
MASK_FILL = -100.0
BETA_ONE = 0.5
BETA_TWO = 0.5
ADAM_EPS = 1e-08
DECAY = 0.05


def row_edges():
    first = 3 * C * C // 128
    second = first + C * C // 128
    third = second + C * FF // 128
    fourth = third + FF * C // 128
    fifth = fourth + SMALL_ROWS
    return [first, second, third, fourth, fifth]


GROUPS = 3
GROUP_HEADS = HEADS // GROUPS
CELLS = WIN * 8
LANES = 64
LOG2E = math.log2(math.e)
F32 = jnp.float32
BF16 = jnp.bfloat16


def nn(left, right):
    return lax.dot_general(left, right, (((1,), (0,)), ((), ())), preferred_element_type=F32)


def nt(left, right):
    return lax.dot_general(left, right, (((1,), (1,)), ((), ())), preferred_element_type=F32)


def tn(left, right):
    return lax.dot_general(left, right, (((0,), (0,)), ((), ())), preferred_element_type=F32)


def gelu_pair(u):
    normal = 0.5 + 0.5 * lax.erf(u * math.sqrt(0.5))
    gauss = jnp.exp2(u * u * (-0.5 * LOG2E))
    return u * normal, normal + u * gauss * (1.0 / math.sqrt(2.0 * math.pi))


def row_norm(values):
    center = values - jnp.mean(values, axis=-1, keepdims=True)
    scale = lax.rsqrt(jnp.mean(center * center, axis=-1, keepdims=True) + NORM_EPS)
    return center * scale, scale


def norm_pull(grad, normal, scale):
    first = jnp.mean(grad, axis=-1, keepdims=True)
    second = jnp.mean(grad * normal, axis=-1, keepdims=True)
    return scale * (grad - first - normal * second)


def column_sum(values):
    return jnp.sum(values, axis=0, keepdims=True)


SMALL_START = 3 * C * C // 128 + C * C // 128 + 2 * C * FF // 128
SMALL_SPAN = 64


def slab_plan():
    return [
        (0, 3 * C // 128, C),
        (3 * C * C // 128, C // 128, C),
        (4 * C * C // 128, FF // 128, C),
        (4 * C * C // 128 + C * FF // 128, C // 128, FF),
    ]


ORDERS = (("x", "y", "z"), ("y", "x", "z"), ("x", "y", "z"), ("z", "x", "y"))
LAG = 2
FIRST_ROWS = 3 * C * C // 128


def split_three(values):
    high = values.astype(BF16)
    rest = values - high.astype(F32)
    middle = rest.astype(BF16)
    return high, middle, (rest - middle.astype(F32)).astype(BF16)


def wire_rows(rows, strips, buckets):
    unit = 16 * strips * buckets
    return -(-rows // unit) * unit


def reduce_plan(strips, buckets, rows, orders):
    sizes = {"z": strips // 2, "y": 2, "x": buckets // 2}
    unit = 8 * strips * buckets
    units = rows // 2 // unit
    orders = orders[:units]
    parts, first = [], 0
    for p, order in enumerate(orders):
        length = (units // len(orders) + (p < units % len(orders))) * unit
        levels, share = [], length
        for axis in order:
            share = share // sizes[axis]
            levels.append((axis, sizes[axis], share))
        parts.append((first, length, levels))
        first += length
    return parts


def reduce_scratch(plan):
    shapes, copies = [], 0
    for _, length, levels in plan:
        shapes += [(length, 128), (length, 128)]
        for _, size, share in levels:
            shapes += [((size - 1) * share, 128), (share, 128)]
        copies += 2 + 2 * sum(size - 1 for _, size, _ in levels)
    return [pltpu.VMEM(shape, BF16) for shape in shapes] + [
        pltpu.SemaphoreType.DMA((copies,)), pltpu.SemaphoreType.DMA((copies,))
    ]


class Place:
    def __init__(self, strips, buckets):
        strip, bucket = lax.axis_index("strip"), lax.axis_index("bucket")
        self.sizes = {"z": strips // 2, "y": 2, "x": buckets // 2, "core": 2}
        self.mine = {"z": strip // 2, "y": strip % 2, "x": bucket // 2, "core": bucket % 2}
        self.above = (lax.rem(strip + strips - 1, strips), bucket)
        self.below = (lax.rem(strip + 1, strips), bucket)

    def peer(self, axis, offset):
        return lax.rem(self.mine[axis] + offset, self.sizes[axis])

    def device(self, axis, offset):
        place = dict(self.mine)
        place[axis] = self.peer(axis, offset)
        return (place["z"] * 2 + place["y"], place["x"] * 2 + place["core"])

    def greet(self, halos):
        barrier = pltpu.get_barrier_semaphore()
        partners = [self.device(axis, offset) for axis, size in self.sizes.items() for offset in range(1, size)]
        partners += [self.above, self.below] if halos else []
        for partner in partners:
            pl.semaphore_signal(barrier, inc=1, device_id=partner, device_id_type=pl.DeviceIdType.MESH)
        pl.semaphore_wait(barrier, len(partners))


def reduce_stages(place, plan, wire, scratch):
    buffers, send_sems, recv_sems = list(scratch[:-2]), scratch[-2], scratch[-1]
    half = wire.shape[0] // 2
    counter = [0]

    def span(start, length):
        return pl.ds(pl.multiple_of(start, 16), length)

    def copies_of(count):
        first = counter[0]
        counter[0] += count
        return first

    def copy(at, source, target, axis, offset):
        return pltpu.make_async_remote_copy(
            src_ref=source, dst_ref=target, send_sem=send_sems.at[at], recv_sem=recv_sems.at[at],
            device_id=place.device(axis, offset), device_id_type=pl.DeviceIdType.MESH,
        )

    def part_stages(first, length, levels):
        core_in, core_sum = buffers.pop(0), buffers.pop(0)
        boxes = [(buffers.pop(0), buffers.pop(0)) for _ in levels]
        held = [core_sum] + [total for _, total in boxes]

        def own():
            return place.mine["core"] * half + first

        def start_of(level):
            start = own()
            for axis, _, share in levels[:level]:
                start = start + place.mine[axis] * share
            return start

        core_at, back_at = copies_of(1), copies_of(1)
        down_at = [copies_of(size - 1) for _, size, _ in levels]
        up_at = [copies_of(size - 1) for _, size, _ in levels]

        def core_out():
            other = (1 - place.mine["core"]) * half + first
            return [copy(core_at, wire.at[span(other, length)], core_in, "core", 1)]

        def down(level):
            axis, size, share = levels[level]
            inbox = boxes[level][0]
            return [
                copy(down_at[level] + offset - 1, held[level].at[span(place.peer(axis, offset) * share, share)],
                     inbox.at[pl.ds((offset - 1) * share, share)], axis, offset)
                for offset in range(1, size)
            ]

        def up(level):
            axis, size, share = levels[level]
            region = wire.at[span(start_of(level + 1), share)]
            return [copy(up_at[level] + offset - 1, region, region, axis, offset) for offset in range(1, size)]

        def core_back():
            region = wire.at[span(own(), length)]
            return [copy(back_at, region, region, "core", 1)]

        def add_core():
            core_sum[...] = wire[span(own(), length), :] + core_in[...]

        def add(level):
            axis, size, share = levels[level]
            inbox, total = boxes[level]
            value = held[level][span(place.mine[axis] * share, share), :].astype(F32)
            for offset in range(1, size):
                value = value + inbox[(offset - 1) * share : offset * share, :].astype(F32)
            if level + 1 < len(levels):
                total[...] = value.astype(BF16)
            else:
                wire[span(start_of(len(levels)), share), :] = value.astype(BF16)

        count = len(levels)
        moves = [core_out] + [functools.partial(down, level) for level in range(count)]
        moves += [functools.partial(up, level) for level in reversed(range(count))] + [core_back]
        work = {1: add_core}
        for level in range(count):
            work[level + 2] = functools.partial(add, level)

        def stage(index):
            if index > 0:
                for one in moves[index - 1]():
                    one.wait()
            if index in work:
                work[index]()
            if index < len(moves):
                for one in moves[index]():
                    one.start()

        return [functools.partial(stage, index) for index in range(len(moves) + 1)]

    return [part_stages(*part) for part in plan]


def reduce_ticks(parts):
    ticks = []
    for p, stages in enumerate(parts):
        for index, stage in enumerate(stages):
            at = index + p // 2
            while len(ticks) <= at:
                ticks.append([])
            ticks[at].append(stage)

    def run(tick):
        for stage in tick:
            stage()

    return [functools.partial(run, tick) for tick in ticks]


def tick_slots(ticks, slots):
    return [[tick for i, tick in enumerate(ticks) if i * slots // len(ticks) == slot] for slot in range(slots)]


def head_bits():
    lane_head = lax.broadcasted_iota(jnp.int32, (1, 128), 1) // HD
    return [(lane_head == h).astype(F32).astype(BF16) for h in range(GROUP_HEADS)]


def stack_of(part, bits):
    return jnp.concatenate([part * bit for bit in bits], axis=0)


def unstack(part):
    lane_head = lax.broadcasted_iota(jnp.int32, (1, 128), 1) // HD
    total = None
    for h in range(GROUP_HEADS):
        piece = jnp.where(lane_head == h, part[h * LANES : h * LANES + CELLS], 0.0)
        total = piece if total is None else total + piece
    return total


def load_matrix(target, wire, first, rows):
    for j in range(target.shape[1] // 128):
        target[:, j * 128 : j * 128 + 128] = wire[first + j * rows : first + (j + 1) * rows, :]


def load_vectors(refs, wire, first):
    small = jnp.zeros((SMALL_SPAN, 128), F32)
    for i in range(3):
        small = small + wire[FIRST_ROWS + i * SMALL_SPAN : FIRST_ROWS + (i + 1) * SMALL_SPAN, :].astype(F32)
    for ref, row in zip(refs, first):
        for j in range(ref.shape[1] // 128):
            ref[:, j * 128 : j * 128 + 128] = small[row + j : row + j + 1]


def to_windows(line, last, main, halo, step, target):
    slabs, columns = C // 128, main.shape[2]
    wide, own = columns // WIN, WIN - SHIFT
    wrapped_row = lax.broadcasted_iota(jnp.int32, (8, 128), 0) >= own
    for a in range(WIN):
        row = main[0, SHIFT + a] if a < own else halo[step, a - own].astype(F32)
        for s in range(slabs):
            line[s, a, 8 : 8 + columns, :] = row[:, s * 128 : s * 128 + 128]
    for a in range(WIN):
        for s in range(slabs):
            front = line[s, a, 8 - own : 16 - own, :]
            for w in range(wide):
                first = 8 + w * WIN + SHIFT
                tile = jnp.where(wrapped_row & (w == last), front, line[s, a, first : first + 8, :])
                target[w * CELLS + a * 8 : w * CELLS + a * 8 + 8, s * 128 : s * 128 + 128] = tile


def from_windows(line, width, source, main, halo, step):
    slabs, columns = C // 128, main.shape[2]
    wide, own = columns // WIN, WIN - SHIFT
    for w in range(wide):
        for a in range(WIN):
            for s in range(slabs):
                first = 8 + w * WIN + SHIFT
                line[s, a, first : first + 8, :] = source[
                    w * CELLS + a * 8 : w * CELLS + a * 8 + 8, s * 128 : s * 128 + 128
                ]
    kept = lax.broadcasted_iota(jnp.int32, (columns, 128), 0) < width
    front = lax.broadcasted_iota(jnp.int32, (8, 128), 0) < SHIFT
    for a in range(WIN):
        for s in range(slabs):
            wrapped = line[s, a, pl.ds(width + 8, 8), :]
            line[s, a, 8:16, :] = jnp.where(front, wrapped, line[s, a, 8:16, :])
            row = jnp.where(kept, line[s, a, 8 : 8 + columns, :], 0.0)
            if a < own:
                main[0, a, :, s * 128 : s * 128 + 128] = row
            else:
                halo[step, a - own, :, s * 128 : s * 128 + 128] = row.astype(BF16)


def place_onehot(row):
    shape = (128, HEADS * LANES)
    source = lax.broadcasted_iota(jnp.int32, shape, 0)
    lane = lax.broadcasted_iota(jnp.int32, shape, 1)
    return (lane == source // 8 * LANES + row * 8 + source % 8).astype(F32).astype(BF16)


def offset_onehot(column):
    shape = (256, 128)
    source = lax.broadcasted_iota(jnp.int32, shape, 0)
    lane = lax.broadcasted_iota(jnp.int32, shape, 1)
    wanted = (lane % 8 - column + WIN - 1) * HEADS + lane // 8
    return ((source == wanted) & (lane < HEADS * 8)).astype(F32).astype(BF16)


SPAN = 2 * WIN - 1


def build_bias(raw, last_strip, offsets, spread, bias):
    flat = jnp.concatenate([raw[r : r + 1] for r in range(TABLE_ROWS)], axis=1)
    offsets[...] = jnp.zeros_like(offsets)
    spread[...] = jnp.zeros_like(spread)
    for d in range(SPAN):
        offsets[SPAN - 1 - d : SPAN - d, 0 : SPAN * HEADS] = flat[:, d * SPAN * HEADS : (d + 1) * SPAN * HEADS]
    terms = split_three(offsets[...])
    for column in range(WIN):
        pick = offset_onehot(column)
        part = nn(terms[0], pick) + nn(terms[1], pick) + nn(terms[2], pick)
        spread[pl.ds(column, SPAN, stride=8), :] = part[0:SPAN]
    terms = split_three(spread[...])
    total = jnp.zeros((CELLS, HEADS * LANES), F32)
    for row in range(WIN):
        pick = place_onehot(row)
        for term in terms:
            total = total + nn(term[8 * (WIN - 1 - row) : 8 * (WIN - 1 - row) + CELLS], pick)
    shape = (CELLS, HEADS * LANES)
    key = lax.broadcasted_iota(jnp.int32, shape, 0)
    query = lax.broadcasted_iota(jnp.int32, shape, 1) % LANES
    edge = WIN - SHIFT
    by_row = ((key // 8 >= edge) != (query // 8 >= edge)) & last_strip
    by_col = (key % 8 >= edge) != (query % 8 >= edge)
    for variant, masked in enumerate((by_row, by_row | by_col)):
        value = (total + jnp.where(masked, MASK_FILL, 0.0)) * LOG2E
        value = jnp.where(key % 8 < WIN, value, -1e30)
        for g in range(GROUPS):
            bias[variant, g] = value[:, g * GROUP_HEADS * LANES : (g + 1) * GROUP_HEADS * LANES]


def pull_bias(sums, spread):
    grads = jnp.concatenate([sums[g] for g in range(GROUPS)], axis=1)
    high, middle, _ = split_three(grads)
    spread[...] = jnp.zeros_like(spread)
    for row in range(WIN):
        pick = place_onehot(row)
        first = 8 * (WIN - 1 - row)
        spread[first : first + CELLS, :] += nt(high, pick) + nt(middle, pick)
    total = jnp.zeros((SPAN, 256), F32)
    for column in range(WIN):
        pick = offset_onehot(column)
        high, middle, _ = split_three(spread[pl.ds(column, SPAN, stride=8), :])
        total = total + nt(high, pick) + nt(middle, pick)
    flat = [total[SPAN - 1 - d : SPAN - d, 0 : SPAN * HEADS] for d in range(SPAN)]
    flat.append(jnp.zeros((1, TABLE_ROWS * 128 - SPAN * SPAN * HEADS), F32))
    flat = jnp.concatenate(flat, axis=1)
    return jnp.concatenate([flat[:, r * 128 : r * 128 + 128] for r in range(TABLE_ROWS)], axis=0)


def rank_rows(me, owner_ref, rank_ref, start_ref):
    blocks = owner_ref.shape[0]
    mine = (owner_ref[...] == me).astype(F32)
    low = mine.astype(BF16)
    row = lax.broadcasted_iota(jnp.int32, (128, 128), 0)
    col = lax.broadcasted_iota(jnp.int32, (128, 128), 1)
    within = nn(low, (row <= col).astype(F32).astype(BF16))
    sums = nn(low, jnp.ones((128, 128), BF16))
    below = lax.broadcasted_iota(jnp.int32, (blocks, blocks), 1) < lax.broadcasted_iota(jnp.int32, (blocks, blocks), 0)
    start = nn(below.astype(F32).astype(BF16), sums.astype(BF16))
    rank_ref[...] = jnp.where(mine > 0, within - 1.0, -1.0)
    start_ref[...] = start.astype(jnp.int32)


def spread_rows(first, slabs, rows, target, offset, rank_ref, start_s, padded, packed):
    slot = lax.broadcasted_iota(jnp.int32, (128, 128), 0).astype(F32)

    def block(b, _):
        at = first // 128 + b
        hot = (slot == rank_ref[pl.ds(at, 1), :]).astype(F32).astype(BF16)
        begin = jnp.clip(start_s[at, 0], 0, padded.shape[0] - 128)
        held = padded[pl.ds(begin, 128), :].astype(BF16)
        packed[pl.ds(pl.multiple_of(b * 128, 128), 128), :] = tn(hot, held)
        return 0

    count = slabs * rows // 128
    lax.fori_loop(0, count, block, 0, unroll=3 if count % 3 == 0 else 1)
    for j in range(slabs):
        target[offset + j * rows : offset + (j + 1) * rows, :] = packed[pl.ds(j, rows, stride=slabs), :].astype(BF16)


def spread_small(target, rank_ref, start_s, padded):
    slot = lax.broadcasted_iota(jnp.int32, (128, 128), 0).astype(F32)
    small = SMALL_START // 128
    hot = (slot == rank_ref[small : small + 1, :]).astype(F32).astype(BF16)
    begin = jnp.clip(start_s[small, 0], 0, padded.shape[0] - 128)
    for i, piece in enumerate(split_three(padded[pl.ds(begin, 128), :])):
        first = FIRST_ROWS + i * SMALL_SPAN
        target[first : first + SMALL_SPAN, :] = tn(hot, piece)[0:SMALL_SPAN].astype(BF16)
    used = FIRST_ROWS + 3 * SMALL_SPAN
    target[used:, :] = jnp.zeros((target.shape[0] - used, 128), BF16)


def block_kernel(
    strips, buckets, images, plan_one, plan_two,
    cols_ref, keep_ref, x_ref, dy_ref, x_any, dy_any, owner_ref, master_ref,
    out_ref, gx_ref, rank_ref, start_ref, outh_any, gxh_any, gone_any, gtwo_any,
    wq_ref, wp_ref, wu_ref, wd_ref, bq_ref, bp_ref, bu_ref, bd_ref, g1_ref, b1_ref, g2_ref, b2_ref,
    gwq_ref, gwp_ref, gwu_ref, gwdt_ref, gbq_ref, gbp_ref, gbu_ref, gbd_ref, gg1_ref, gb1_ref, gg2_ref, gb2_ref,
    bias, gs_ref, offsets, spread,
    xw, zs, qkv, prob, ctx, gctx, gx1s,
    line, dyw, x1s, n2s, h2s, gfs, ys, gh2s, resw, htr, gtr, gscores, gqkv,
    fetched, halo_out, halo_in, back_in, wire_one, wire_two, padded, packed, start_s,
    local_sems, send_sems, recv_sems, *scratch,
):
    step = pl.program_id(0)
    tokens = dyw.shape[0]
    wide = tokens // CELLS
    place = Place(strips, buckets)
    last = cols_ref[0] - 1
    width = cols_ref[0] * WIN
    count_one = len(reduce_scratch(plan_one))
    parts_one = reduce_stages(place, plan_one, wire_one, scratch[:count_one])
    parts_two = reduce_stages(place, plan_two, wire_two, scratch[count_one:])
    gather_ticks = reduce_ticks(parts_one + [[]] * (4 - len(parts_one)) + parts_two)
    early = len(parts_one[0])
    one_ticks, two_ticks = reduce_ticks(parts_one), reduce_ticks(parts_two)

    def halo(kind, image):
        return pltpu.make_async_remote_copy(
            src_ref=halo_out.at[kind % 2, image], dst_ref=(halo_in if kind < 2 else back_in).at[kind % 2, image],
            send_sem=send_sems.at[kind, image], recv_sem=recv_sems.at[kind, image],
            device_id=place.above if kind < 2 else place.below, device_id_type=pl.DeviceIdType.MESH,
        )

    def fetch(array, image, kind):
        return pltpu.make_async_copy(array.at[image, pl.ds(0, SHIFT)], fetched.at[kind], local_sems.at[kind])

    def send_rows(kind, image, held):
        halo_out[kind, image] = fetched[held].astype(BF16)
        halo(kind, image).start()

    @pl.when(step == 0)
    def _():
        first = [fetch(x_any, image, image) for image in range(2)]
        for copy in first:
            copy.start()
        me = lax.axis_index("strip") * buckets + lax.axis_index("bucket")
        rank_rows(me, owner_ref, rank_ref, start_ref)
        starts = pltpu.make_async_copy(start_ref, start_s, local_sems.at[2])
        starts.start()
        capacity = master_ref.shape[0]
        padded[0:capacity, :] = master_ref[...]
        padded[capacity:, :] = jnp.zeros((padded.shape[0] - capacity, 128), F32)
        starts.wait()
        plans = slab_plan()
        spread_rows(*plans[0], wire_one, 0, rank_ref, start_s, padded, packed)
        spread_small(wire_one, rank_ref, start_s, padded)
        place.greet(True)
        gather_ticks[0]()
        for image in range(2):
            first[image].wait()
            send_rows(0, image, image)
        fetch(x_any, 2, 0).start()
        fetch(dy_any, 0, 1).start()
        for plan in plans[1:3]:
            spread_rows(*plan, wire_two, plan[0] - FIRST_ROWS, rank_ref, start_s, padded, packed)
        gather_ticks[1]()
        spread_rows(*plans[3], wire_two, plans[3][0] - FIRST_ROWS, rank_ref, start_s, padded, packed)
        used = SMALL_START - FIRST_ROWS
        wire_two[used:, :] = jnp.zeros((wire_two.shape[0] - used, 128), BF16)
        gather_ticks[2]()
        line[...] = jnp.zeros_like(line)
        for ref in (gwq_ref, gwp_ref, gwu_ref, gwdt_ref, gbq_ref, gbp_ref, gbu_ref, gbd_ref,
                    gg1_ref, gb1_ref, gg2_ref, gb2_ref, gs_ref, qkv, gctx):
            ref[...] = jnp.zeros_like(ref)
        for tick in gather_ticks[3:early]:
            tick()
        load_matrix(wq_ref, wire_one, 0, C)
        load_vectors((bq_ref, bp_ref, bu_ref, bd_ref, g1_ref, b1_ref, g2_ref, b2_ref), wire_one,
                     (0, 9, 12, 24, 27, 30, 33, 36))
        raw = jnp.zeros((SMALL_SPAN, 128), F32)
        for i in range(3):
            raw = raw + wire_one[FIRST_ROWS + i * SMALL_SPAN : FIRST_ROWS + (i + 1) * SMALL_SPAN, :].astype(F32)
        build_bias(raw[SMALL_ROWS : SMALL_ROWS + TABLE_ROWS], lax.axis_index("strip") == strips - 1, offsets, spread, bias)

    @pl.when((step > 0) & (step + 1 < images))
    def _():
        fetch(x_any, step + 1, 0).wait()
        send_rows(0, step + 1, 0)

    @pl.when((step > 0) & (step + 2 < images))
    def _():
        fetch(x_any, step + 2, 0).start()

    @pl.when((step > 0) & (step - 1 < images))
    def _():
        fetch(dy_any, step - 1, 1).wait()
        send_rows(1, step - 1, 1)

    @pl.when((step > 0) & (step < images))
    def _():
        fetch(dy_any, step, 1).start()

    bits = head_bits()

    def attend(image):
        at = lax.rem(image, LAG)
        halo(0, image).wait_recv()
        to_windows(line, last, x_ref, halo_in.at[0], image, xw.at[at])
        normal, _ = row_norm(xw[at])
        zs[at] = (normal * g1_ref[...] + b1_ref[...]).astype(BF16)
        triple = nn(zs[at], wq_ref[...]) + bq_ref[...]
        for w in range(wide):
            qkv[at, w, 0:CELLS, :] = triple[w * CELLS : w * CELLS + CELLS].astype(BF16)
        for w in range(wide):
            variant = (w == last).astype(jnp.int32)
            for g in range(GROUPS):
                q = qkv[at, w, :, g * 128 : g * 128 + 128]
                k = qkv[at, w, 0:CELLS, C + g * 128 : C + g * 128 + 128]
                v = qkv[at, w, 0:CELLS, 2 * C + g * 128 : 2 * C + g * 128 + 128]
                s = nt(k, stack_of(q, bits)) * (HD ** (-0.5) * LOG2E) + bias[variant, g]
                e = jnp.exp2(s - jnp.max(s, axis=0, keepdims=True))
                a = (e * (1.0 / jnp.sum(e, axis=0, keepdims=True))).astype(BF16)
                prob[at, w, g] = a
                resw[w * CELLS : w * CELLS + CELLS, g * 128 : g * 128 + 128] = unstack(tn(a, v))
        ctx[at] = resw[...].astype(BF16)

    def feed(image):
        at = lax.rem(image, LAG)
        keep_one = keep_ref[image, 0].astype(F32) * (1.0 / KEEP_PROB)
        keep_two = keep_ref[image, 1].astype(F32) * (1.0 / KEEP_PROB)
        x1 = xw[at] + keep_one * (nn(ctx[at], wp_ref[...]) + bp_ref[...])
        x1s[...] = x1
        normal, scale_two = row_norm(x1)
        n2s[...] = normal
        h2 = (normal * g2_ref[...] + b2_ref[...]).astype(BF16)
        h2s[...] = h2
        htr[...] = h2.astype(F32).T.astype(BF16)

        halo(1, image).wait_recv()
        to_windows(line, last, dy_ref, halo_in.at[1], image, dyw)
        token = lax.broadcasted_iota(jnp.int32, (tokens, 1), 0)
        valid = ((token % 8 < WIN) & (token < cols_ref[0] * CELLS)).astype(F32)
        gy = dyw[...] * valid
        gf = (gy * keep_two).astype(BF16)
        gfs[...] = gf
        gbd_ref[...] += column_sum(gf.astype(F32))
        gtr[...] = gf.astype(F32).T.astype(BF16)
        ys[...] = jnp.zeros_like(ys)
        gh2s[...] = jnp.zeros_like(gh2s)
        chunk = 512
        for j in range(FF // chunk):
            part = slice(j * chunk, (j + 1) * chunk)
            u = nn(h2s[...], wu_ref[:, part]) + bu_ref[:, part]
            gm = nt(gfs[...], wd_ref[part, :])
            m, slope = gelu_pair(u)
            m = m.astype(BF16)
            gu = (gm * slope).astype(BF16)
            ys[...] += nn(m, wd_ref[part, :])
            gwdt_ref[:, part] += nn(gtr[...], m)
            gwu_ref[:, part] += nn(htr[...], gu)
            gbu_ref[:, part] += column_sum(gu.astype(F32))
            gh2s[...] += nt(gu, wu_ref[:, part])

        resw[...] = (x1s[...] + keep_two * (ys[...] + bd_ref[...])) * valid
        halo(1, image).wait_send()
        from_windows(line, width, resw, out_ref, halo_out.at[1], image)
        halo(3, image).start()

        gh2 = gh2s[...]
        gg2_ref[...] += column_sum(gh2 * n2s[...])
        gb2_ref[...] += column_sum(gh2)
        gx1 = dyw[...] * valid + norm_pull(gh2 * g2_ref[...], n2s[...], scale_two)
        gx1s[at] = gx1
        ga = (keep_one * gx1).astype(BF16)
        gbp_ref[...] += column_sum(ga.astype(F32))
        gwp_ref[...] += nn(ctx[at].astype(F32).T.astype(BF16), ga)
        gc = nt(ga, wp_ref[...])
        for w in range(wide):
            gctx[at, w, 0:CELLS, :] = gc[w * CELLS : w * CELLS + CELLS].astype(BF16)

    def pull(image):
        at = lax.rem(image, LAG)
        scale = HD ** (-0.5)
        for w in range(wide):
            rows = slice(w * CELLS, w * CELLS + CELLS)
            for g in range(GROUPS):
                v = qkv[at, w, 0:CELLS, 2 * C + g * 128 : 2 * C + g * 128 + 128]
                gstack = stack_of(gctx[at, w, :, g * 128 : g * 128 + 128], bits)
                low = prob[at, w, g]
                a = low.astype(F32)
                grad = nt(v, gstack)
                inner = jnp.sum(grad * a, axis=0, keepdims=True)
                gscores[w, g] = a * (grad - inner)
                gqkv[rows, 2 * C + g * 128 : 2 * C + g * 128 + 128] = nn(low, gstack)
        for w in range(wide):
            rows = slice(w * CELLS, w * CELLS + CELLS)
            for g in range(GROUPS):
                q = qkv[at, w, :, g * 128 : g * 128 + 128]
                k = qkv[at, w, 0:CELLS, C + g * 128 : C + g * 128 + 128]
                gs = gscores[w, g].astype(BF16)
                gqkv[rows, g * 128 : g * 128 + 128] = unstack(tn(gs, k)) * scale
                gqkv[rows, C + g * 128 : C + g * 128 + 128] = nn(gs, stack_of(q, bits)) * scale
        gs_ref[...] += jnp.sum(gscores[...], axis=0)

        gtriple = gqkv[...].astype(BF16)
        gbq_ref[...] += column_sum(gtriple.astype(F32))
        gwq_ref[...] += nn(zs[at].astype(F32).T.astype(BF16), gtriple)
        gz = nt(gtriple, wq_ref[...]).astype(BF16).astype(F32)
        normal, scale_one = row_norm(xw[at])
        gg1_ref[...] += column_sum(gz * normal)
        gb1_ref[...] += column_sum(gz)
        resw[...] = gx1s[at] + norm_pull(gz * g1_ref[...], normal, scale_one)
        halo(0, image).wait_send()
        from_windows(line, width, resw, gx_ref, halo_out.at[0], image)
        halo(2, image).start()

    def pack_two():
        first = 0
        for grad in (gwp_ref, gwu_ref):
            for j in range(grad.shape[1] // 128):
                wire_two[first : first + C, :] = grad[:, j * 128 : j * 128 + 128].astype(BF16)
                first += C
        for j in range(C // 128):
            wire_two[first : first + FF, :] = gwdt_ref[j * 128 : j * 128 + 128, :].T.astype(BF16)
            first += FF
        wire_two[first:, :] = jnp.zeros((wire_two.shape[0] - first, 128), BF16)

    def pack_one():
        for j in range(3 * C // 128):
            wire_one[j * C : (j + 1) * C, :] = gwq_ref[:, j * 128 : j * 128 + 128].astype(BF16)
        vectors = (gbq_ref, gbp_ref, gbu_ref, gbd_ref, gg1_ref, gb1_ref, gg2_ref, gb2_ref)
        pieces = [ref[:, j * 128 : j * 128 + 128] for ref in vectors for j in range(ref.shape[1] // 128)]
        pieces.append(pull_bias(gs_ref, spread))
        pieces.append(jnp.zeros((wire_one.shape[0] - FIRST_ROWS - SMALL_ROWS - TABLE_ROWS, 128), F32))
        wire_one[FIRST_ROWS:, :] = jnp.concatenate(pieces, axis=0).astype(BF16)

    @pl.when(step == LAG)
    def _():
        first = 0
        for ref, rows in ((wp_ref, C), (wu_ref, C), (wd_ref, FF)):
            load_matrix(ref, wire_two, first, rows)
            first += ref.shape[1] // 128 * rows

    @pl.when((step >= LAG) & (step < images + LAG))
    def _():
        feed(step - LAG)

    @pl.when((step >= LAG) & (step < images))
    def _():
        pull(step - LAG)

    @pl.when(step < images)
    def _():
        attend(step)

    late = gather_ticks[early:]
    for k in range(LAG):
        mine = late[k * len(late) // LAG : (k + 1) * len(late) // LAG]

        @pl.when(step == k)
        def _(mine=mine):
            for tick in mine:
                tick()

    @pl.when(step == images + LAG - 1)
    def _():
        pack_two()
        two_ticks[0]()

    for k in range(LAG):

        @pl.when(step == images + LAG + k)
        def _(k=k):
            two_ticks[k + 1]()
            pull(images - LAG + k)

    @pl.when(step == images + 2 * LAG - 1)
    def _():
        pack_one()
        rest = two_ticks[LAG + 1 :]
        for i in range(max(len(rest), len(one_ticks))):
            for ticks in (one_ticks, rest):
                if i < len(ticks):
                    ticks[i]()
        for image in range(images):
            for kind in range(2, 4):
                halo(kind, image).wait()
        stores = [
            pltpu.make_async_copy(source, target, local_sems.at[i])
            for i, (source, target) in enumerate(
                ((wire_one, gone_any), (wire_two, gtwo_any), (back_in.at[0], gxh_any), (back_in.at[1], outh_any))
            )
        ]
        for copy in stores:
            copy.start()
        for copy in stores:
            copy.wait()


SMEM_SPEC = pl.BlockSpec(memory_space=pltpu.SMEM)
HBM_SPEC = pl.BlockSpec(memory_space=pl.ANY)


def whole(shape):
    return pl.BlockSpec(shape, lambda i: (0,) * len(shape))


def run_block(cols, keep, x, dy, owners, master, one_rows, two_rows, strips, buckets):
    samples, rows, columns, _ = x.shape
    wide = columns // WIN
    tokens = wide * CELLS
    own = rows - SHIFT
    halo = (samples, SHIFT, columns, C)
    plan_one = reduce_plan(strips, buckets, one_rows, ORDERS[:2])
    plan_two = reduce_plan(strips, buckets, two_rows, ORDERS)
    top = samples - 1

    def attended(i):
        return (jnp.minimum(i, top), 0, 0, 0)

    def fed(i):
        return (jnp.minimum(jnp.maximum(i - LAG, 0), top), 0, 0, 0)

    def pulled(i):
        early = jnp.minimum(jnp.maximum(i - LAG, 0), top - LAG)
        return (early + jnp.maximum(i - (samples + LAG) + 1, 0), 0, 0, 0)

    vectors = [3 * C, C, FF, C, C, C, C, C]
    sums = (GROUPS, CELLS, GROUP_HEADS * LANES)

    def struct(shape, dtype=F32):
        return jax.ShapeDtypeStruct(shape, dtype)

    token = pltpu.VMEM((tokens, C), F32)
    low = pltpu.VMEM((tokens, C), BF16)
    turned = pltpu.VMEM((C, tokens), BF16)
    scratch = [pltpu.VMEM(s, BF16) for s in ((C, 3 * C), (C, C), (C, FF), (FF, C))]
    scratch += [pltpu.VMEM((1, size), F32) for size in vectors]
    scratch += [pltpu.VMEM(s, F32) for s in ((C, 3 * C), (C, C), (C, FF), (C, FF))]
    scratch += [pltpu.VMEM((1, size), F32) for size in vectors]
    scratch += [
        pltpu.VMEM((2,) + sums, F32), pltpu.VMEM(sums, F32),
        pltpu.VMEM((16, 256), F32), pltpu.VMEM((SPAN * 8, 128), F32),
        pltpu.VMEM((LAG, tokens, C), F32), pltpu.VMEM((LAG, tokens, C), BF16),
        pltpu.VMEM((LAG, wide, LANES, 3 * C), BF16), pltpu.VMEM((LAG, wide) + sums, BF16),
        pltpu.VMEM((LAG, tokens, C), BF16), pltpu.VMEM((LAG, wide, LANES, C), BF16),
        pltpu.VMEM((LAG, tokens, C), F32),
        pltpu.VMEM((C // 128, WIN, columns + 16, 128), F32),
        token, token, token, low, low, token, token, token, turned, turned,
        pltpu.VMEM((wide,) + sums, F32), pltpu.VMEM((tokens, 3 * C), F32),
        pltpu.VMEM((2,) + halo[1:], F32),
        pltpu.VMEM((2,) + halo, BF16), pltpu.VMEM((2,) + halo, BF16), pltpu.VMEM((2,) + halo, BF16),
        pltpu.VMEM((one_rows, 128), BF16), pltpu.VMEM((two_rows, 128), BF16),
        pltpu.VMEM((-(-(master.shape[0] + 128) // 8) * 8, 128), F32), pltpu.VMEM((C * FF // 128, 128), F32),
        pltpu.SMEM(owners.shape, jnp.int32),
        pltpu.SemaphoreType.DMA((4,)), pltpu.SemaphoreType.DMA((4, samples)), pltpu.SemaphoreType.DMA((4, samples)),
    ]
    block = (1, rows, columns, C)
    part = (1, own, columns, C)
    return pl.pallas_call(
        lambda *refs: block_kernel(strips, buckets, samples, plan_one, plan_two, *refs),
        grid=(samples + 2 * LAG,),
        in_specs=[SMEM_SPEC, SMEM_SPEC, pl.BlockSpec(block, attended), pl.BlockSpec(block, fed)] + [HBM_SPEC] * 2
        + [whole(owners.shape), whole(master.shape)],
        out_specs=[pl.BlockSpec(part, fed), pl.BlockSpec(part, pulled)] + [whole(owners.shape)] * 2 + [HBM_SPEC] * 4,
        out_shape=[struct((samples, own, columns, C)), struct((samples, own, columns, C)), struct(owners.shape),
                   struct(owners.shape, jnp.int32), struct(halo, BF16), struct(halo, BF16), struct((one_rows, 128), BF16),
                   struct((two_rows, 128), BF16)],
        scratch_shapes=scratch + reduce_scratch(plan_one) + reduce_scratch(plan_two),
        compiler_params=pltpu.CompilerParams(
            vmem_limit_bytes=62 * 1024 * 1024, collective_id=1, has_side_effects=True
        ),
        name="block",
    )(cols, keep, x, dy, x, dy, owners, master)


def collect_kernel(
    start_ref, rank_ref, one_any, two_any, master_ref, first_ref, second_ref, outh_any, gxh_any, out_any, gx_any,
    first_out, second_out, master_out, out_final, gx_final, packed, total, wide, one, two, halos, sems,
):
    own = out_any.shape[1]
    pairs = [(one_any, one), (two_any, two), (outh_any, halos.at[0]), (gxh_any, halos.at[1])]
    pairs += [(main, wide.at[i, :, pl.ds(SHIFT, own)]) for i, main in enumerate((out_any, gx_any))]
    loads = [pltpu.make_async_copy(source, target, sems.at[i]) for i, (source, target) in enumerate(pairs)]
    stores = [pltpu.make_async_copy(wide.at[i], final, sems.at[6 + i]) for i, final in enumerate((out_final, gx_final))]
    for load in loads:
        load.start()
    capacity = master_ref.shape[0]
    total[...] = jnp.zeros_like(total)
    slot = lax.broadcasted_iota(jnp.int32, (128, 128), 0).astype(F32)

    def block(b, _):
        hot = (slot == rank_ref[pl.ds(b, 1), :]).astype(F32).astype(BF16)
        part = nn(hot, packed[pl.ds(pl.multiple_of(b * 128, 128), 128), :].astype(BF16))
        where = pl.ds(start_ref[b, 0], 128)
        total[where, :] = total[where, :] + part
        return 0

    def unpack(plan, source, offset):
        first, slabs, rows = plan
        for j in range(slabs):
            packed[pl.ds(first + j, rows, stride=slabs), :] = source[
                first - offset + j * rows : first - offset + (j + 1) * rows, :
            ].astype(F32)

    plans = slab_plan()
    small = SMALL_START // 128
    loads[0].wait()
    unpack(plans[0], one, 0)
    packed[SMALL_START : SMALL_START + SMALL_SPAN, :] = one[FIRST_ROWS : FIRST_ROWS + SMALL_SPAN, :].astype(F32)
    packed[SMALL_START + SMALL_SPAN : SMALL_START + 128, :] = jnp.zeros((128 - SMALL_SPAN, 128), F32)
    lax.fori_loop(0, FIRST_ROWS // 128, block, 0, unroll=9)
    for i in range(2):
        loads[2 + i].wait()
        wide[i, :, 0:SHIFT] = halos[i].astype(F32)
        loads[4 + i].wait()
        stores[i].start()
    loads[1].wait()
    for plan in plans[1:]:
        unpack(plan, two, FIRST_ROWS)
    lax.fori_loop(FIRST_ROWS // 128, small, block, 0, unroll=9)
    block(small, 0)
    slots = lax.broadcasted_iota(jnp.int32, (capacity, 1), 0)
    edges = [edge // 128 for edge in row_edges()[:4]] + [SMALL_START // 128 + 1]
    rates = [2.0 / math.sqrt(C), 2.0 / math.sqrt(C // 8), 2.0 / math.sqrt(C), 2.0 / math.sqrt(FF), 1.0, 0.0]
    rate = jnp.full((capacity, 1), rates[0], F32)
    for edge, amount in zip(edges, rates[1:]):
        rate = jnp.where(slots >= start_ref[edge, 0], amount, rate)
    decay = jnp.where(slots < start_ref[edges[3], 0], DECAY, 0.0)
    grads = total[0:capacity, :]
    weights = master_ref[...]
    first = BETA_ONE * first_ref[...] + (1.0 - BETA_ONE) * grads
    second = BETA_TWO * second_ref[...] + (1.0 - BETA_TWO) * grads * grads
    first_out[...] = first
    second_out[...] = second
    first_hat = first / (1.0 - BETA_ONE**STEP)
    second_hat = second / (1.0 - BETA_TWO**STEP)
    master_out[...] = weights - rate * (first_hat / (jnp.sqrt(second_hat) + ADAM_EPS) + decay * weights)
    for store in stores:
        store.wait()


def run_collect(starts, ranks, one, two, master, first, second, outh, gxh, out, gx):
    vmem = pl.BlockSpec(memory_space=pltpu.VMEM)
    samples, own, columns, channels = out.shape
    final = jax.ShapeDtypeStruct((samples, own + SHIFT, columns, channels), F32)
    return pl.pallas_call(
        collect_kernel,
        in_specs=[SMEM_SPEC, vmem, HBM_SPEC, HBM_SPEC] + [vmem] * 3 + [HBM_SPEC] * 4,
        out_specs=[vmem] * 3 + [HBM_SPEC] * 2,
        out_shape=[jax.ShapeDtypeStruct(master.shape, F32)] * 3 + [final, final],
        scratch_shapes=[
            pltpu.VMEM((SMALL_START + 128, 128), F32),
            pltpu.VMEM((-(-(master.shape[0] + 128) // 8) * 8, 128), F32),
            pltpu.VMEM((2,) + final.shape, F32),
            pltpu.VMEM(one.shape, BF16),
            pltpu.VMEM(two.shape, BF16),
            pltpu.VMEM((2,) + outh.shape, BF16),
            pltpu.SemaphoreType.DMA((8,)),
        ],
        compiler_params=pltpu.CompilerParams(vmem_limit_bytes=62 * 1024 * 1024),
        name="collect",
    )(starts, ranks, one, two, master, first, second, outh, gxh, out, gx)


def shards(
    block_input, cotangent, window_cols, keep_mask, owner_list, master, first_moment, second_moment
):
    strips = lax.axis_size("strip")
    buckets = lax.axis_size("bucket")
    blocks = -(-(SMALL_START // 128 + 2) // 8) * 8
    owners = jnp.pad(owner_list, (0, blocks * 128 - owner_list.shape[0]), constant_values=-1).reshape(blocks, 128)
    one_rows = wire_rows(FIRST_ROWS + 3 * SMALL_SPAN, strips, buckets)
    two_rows = wire_rows(SMALL_START - FIRST_ROWS, strips, buckets)
    output, grad_input, ranks, starts, output_halo, grad_halo, gone, gtwo = run_block(
        window_cols, keep_mask, block_input, cotangent, owners, master, one_rows, two_rows, strips, buckets
    )
    first, second_new, new_weights, output, grad_input = run_collect(
        starts, ranks, gone, gtwo, master, first_moment, second_moment, output_halo, grad_halo, output, grad_input
    )
    return (output, grad_input, first, second_new, new_weights)


def solution(mesh):
    in_specs = (
        P("bucket", "strip", None, None),
        P("bucket", "strip", None, None),
        P("bucket"),
        P("bucket", None),
        P(),
        P(("strip", "bucket"), None),
        P(("strip", "bucket"), None),
        P(("strip", "bucket"), None),
    )
    out_specs = (
        P("bucket", "strip", None, None),
        P("bucket", "strip", None, None),
        P(("strip", "bucket"), None),
        P(("strip", "bucket"), None),
        P(("strip", "bucket"), None),
    )
    return jax.shard_map(shards, mesh=mesh, in_specs=in_specs, out_specs=out_specs, check_vma=False)
```

```python
import functools
import math

import jax
import jax.numpy as jnp
from jax import lax
from jax.experimental import pallas as pl
from jax.experimental.pallas import tpu as pltpu
from jax.sharding import PartitionSpec as P

C = 384
HEADS = 12
HD = 32
FF = 1536
WIN = 7
SHIFT = 3
STEP = 10
SMALL_ROWS = 39
TABLE_ROWS = 16


PRECISE = lax.Precision.HIGHEST
NORM_EPS = 1e-05
KEEP_PROB = 0.8
MASK_FILL = -100.0
BETA_ONE = 0.5
BETA_TWO = 0.5
ADAM_EPS = 1e-08
DECAY = 0.05


def row_edges():
    first = 3 * C * C // 128
    second = first + C * C // 128
    third = second + C * FF // 128
    fourth = third + FF * C // 128
    fifth = fourth + SMALL_ROWS
    return [first, second, third, fourth, fifth]


GROUPS = 3
GROUP_HEADS = HEADS // GROUPS
CELLS = WIN * 8
LANES = 64
LOG2E = math.log2(math.e)
F32 = jnp.float32
BF16 = jnp.bfloat16


def nn(left, right):
    return lax.dot_general(left, right, (((1,), (0,)), ((), ())), preferred_element_type=F32)


def nt(left, right):
    return lax.dot_general(left, right, (((1,), (1,)), ((), ())), preferred_element_type=F32)


def tn(left, right):
    return lax.dot_general(left, right, (((0,), (0,)), ((), ())), preferred_element_type=F32)


def gelu_pair(u):
    normal = 0.5 + 0.5 * lax.erf(u * math.sqrt(0.5))
    gauss = jnp.exp2(u * u * (-0.5 * LOG2E))
    return u * normal, normal + u * gauss * (1.0 / math.sqrt(2.0 * math.pi))


def row_norm(values):
    center = values - jnp.mean(values, axis=-1, keepdims=True)
    scale = lax.rsqrt(jnp.mean(center * center, axis=-1, keepdims=True) + NORM_EPS)
    return center * scale, scale


def norm_pull(grad, normal, scale):
    first = jnp.mean(grad, axis=-1, keepdims=True)
    second = jnp.mean(grad * normal, axis=-1, keepdims=True)
    return scale * (grad - first - normal * second)


def column_sum(values):
    return jnp.sum(values, axis=0, keepdims=True)


SMALL_START = 3 * C * C // 128 + C * C // 128 + 2 * C * FF // 128
SMALL_SPAN = 64


def slab_plan():
    return [
        (0, 3 * C // 128, C),
        (3 * C * C // 128, C // 128, C),
        (4 * C * C // 128, FF // 128, C),
        (4 * C * C // 128 + C * FF // 128, C // 128, FF),
    ]


ORDERS = (("x", "y", "z"), ("y", "x", "z"), ("x", "y", "z"), ("z", "x", "y"))
LAG = 2
FIRST_ROWS = 3 * C * C // 128


def split_three(values):
    high = values.astype(BF16)
    rest = values - high.astype(F32)
    middle = rest.astype(BF16)
    return high, middle, (rest - middle.astype(F32)).astype(BF16)


def wire_rows(rows, strips, buckets):
    unit = 16 * strips * buckets
    return -(-rows // unit) * unit


def reduce_plan(strips, buckets, rows, orders):
    sizes = {"z": strips // 2, "y": 2, "x": buckets // 2}
    unit = 8 * strips * buckets
    units = rows // 2 // unit
    orders = orders[:units]
    parts, first = [], 0
    for p, order in enumerate(orders):
        length = (units // len(orders) + (p < units % len(orders))) * unit
        levels, share = [], length
        for axis in order:
            share = share // sizes[axis]
            levels.append((axis, sizes[axis], share))
        parts.append((first, length, levels))
        first += length
    return parts


def reduce_scratch(plan):
    shapes, copies = [], 0
    for _, length, levels in plan:
        shapes += [(length, 128), (length, 128)]
        for _, size, share in levels:
            shapes += [((size - 1) * share, 128), (share, 128)]
        copies += 2 + 2 * sum(size - 1 for _, size, _ in levels)
    return [pltpu.VMEM(shape, BF16) for shape in shapes] + [
        pltpu.SemaphoreType.DMA((copies,)), pltpu.SemaphoreType.DMA((copies,))
    ]


class Place:
    def __init__(self, strips, buckets):
        strip, bucket = lax.axis_index("strip"), lax.axis_index("bucket")
        self.sizes = {"z": strips // 2, "y": 2, "x": buckets // 2, "core": 2}
        self.mine = {"z": strip // 2, "y": strip % 2, "x": bucket // 2, "core": bucket % 2}
        self.above = (lax.rem(strip + strips - 1, strips), bucket)
        self.below = (lax.rem(strip + 1, strips), bucket)

    def peer(self, axis, offset):
        return lax.rem(self.mine[axis] + offset, self.sizes[axis])

    def device(self, axis, offset):
        place = dict(self.mine)
        place[axis] = self.peer(axis, offset)
        return (place["z"] * 2 + place["y"], place["x"] * 2 + place["core"])

    def greet(self, halos):
        barrier = pltpu.get_barrier_semaphore()
        partners = [self.device(axis, offset) for axis, size in self.sizes.items() for offset in range(1, size)]
        partners += [self.above, self.below] if halos else []
        for partner in partners:
            pl.semaphore_signal(barrier, inc=1, device_id=partner, device_id_type=pl.DeviceIdType.MESH)
        pl.semaphore_wait(barrier, len(partners))


def reduce_stages(place, plan, wire, scratch):
    buffers, send_sems, recv_sems = list(scratch[:-2]), scratch[-2], scratch[-1]
    half = wire.shape[0] // 2
    counter = [0]

    def span(start, length):
        return pl.ds(pl.multiple_of(start, 16), length)

    def copies_of(count):
        first = counter[0]
        counter[0] += count
        return first

    def copy(at, source, target, axis, offset):
        return pltpu.make_async_remote_copy(
            src_ref=source, dst_ref=target, send_sem=send_sems.at[at], recv_sem=recv_sems.at[at],
            device_id=place.device(axis, offset), device_id_type=pl.DeviceIdType.MESH,
        )

    def part_stages(first, length, levels):
        core_in, core_sum = buffers.pop(0), buffers.pop(0)
        boxes = [(buffers.pop(0), buffers.pop(0)) for _ in levels]
        held = [core_sum] + [total for _, total in boxes]

        def own():
            return place.mine["core"] * half + first

        def start_of(level):
            start = own()
            for axis, _, share in levels[:level]:
                start = start + place.mine[axis] * share
            return start

        core_at, back_at = copies_of(1), copies_of(1)
        down_at = [copies_of(size - 1) for _, size, _ in levels]
        up_at = [copies_of(size - 1) for _, size, _ in levels]

        def core_out():
            other = (1 - place.mine["core"]) * half + first
            return [copy(core_at, wire.at[span(other, length)], core_in, "core", 1)]

        def down(level):
            axis, size, share = levels[level]
            inbox = boxes[level][0]
            return [
                copy(down_at[level] + offset - 1, held[level].at[span(place.peer(axis, offset) * share, share)],
                     inbox.at[pl.ds((offset - 1) * share, share)], axis, offset)
                for offset in range(1, size)
            ]

        def up(level):
            axis, size, share = levels[level]
            region = wire.at[span(start_of(level + 1), share)]
            return [copy(up_at[level] + offset - 1, region, region, axis, offset) for offset in range(1, size)]

        def core_back():
            region = wire.at[span(own(), length)]
            return [copy(back_at, region, region, "core", 1)]

        def add_core():
            core_sum[...] = wire[span(own(), length), :] + core_in[...]

        def add(level):
            axis, size, share = levels[level]
            inbox, total = boxes[level]
            value = held[level][span(place.mine[axis] * share, share), :].astype(F32)
            for offset in range(1, size):
                value = value + inbox[(offset - 1) * share : offset * share, :].astype(F32)
            if level + 1 < len(levels):
                total[...] = value.astype(BF16)
            else:
                wire[span(start_of(len(levels)), share), :] = value.astype(BF16)

        count = len(levels)
        moves = [core_out] + [functools.partial(down, level) for level in range(count)]
        moves += [functools.partial(up, level) for level in reversed(range(count))] + [core_back]
        work = {1: add_core}
        for level in range(count):
            work[level + 2] = functools.partial(add, level)

        def stage(index):
            if index > 0:
                for one in moves[index - 1]():
                    one.wait()
            if index in work:
                work[index]()
            if index < len(moves):
                for one in moves[index]():
                    one.start()

        return [functools.partial(stage, index) for index in range(len(moves) + 1)]

    return [part_stages(*part) for part in plan]


def reduce_ticks(parts):
    ticks = []
    for p, stages in enumerate(parts):
        for index, stage in enumerate(stages):
            at = index + p // 2
            while len(ticks) <= at:
                ticks.append([])
            ticks[at].append(stage)

    def run(tick):
        for stage in tick:
            stage()

    return [functools.partial(run, tick) for tick in ticks]


def tick_slots(ticks, slots):
    return [[tick for i, tick in enumerate(ticks) if i * slots // len(ticks) == slot] for slot in range(slots)]


def head_bits():
    lane_head = lax.broadcasted_iota(jnp.int32, (1, 128), 1) // HD
    return [(lane_head == h).astype(F32).astype(BF16) for h in range(GROUP_HEADS)]


def stack_of(part, bits):
    return jnp.concatenate([part * bit for bit in bits], axis=0)


def unstack(part):
    lane_head = lax.broadcasted_iota(jnp.int32, (1, 128), 1) // HD
    total = None
    for h in range(GROUP_HEADS):
        piece = jnp.where(lane_head == h, part[h * LANES : h * LANES + CELLS], 0.0)
        total = piece if total is None else total + piece
    return total


def load_matrix(target, wire, first, rows):
    for j in range(target.shape[1] // 128):
        target[:, j * 128 : j * 128 + 128] = wire[first + j * rows : first + (j + 1) * rows, :]


def load_vectors(refs, wire, first):
    small = jnp.zeros((SMALL_SPAN, 128), F32)
    for i in range(3):
        small = small + wire[FIRST_ROWS + i * SMALL_SPAN : FIRST_ROWS + (i + 1) * SMALL_SPAN, :].astype(F32)
    for ref, row in zip(refs, first):
        for j in range(ref.shape[1] // 128):
            ref[:, j * 128 : j * 128 + 128] = small[row + j : row + j + 1]


def to_windows(line, last, main, halo, step, target):
    slabs, columns = C // 128, main.shape[2]
    wide, own = columns // WIN, WIN - SHIFT
    wrapped_row = lax.broadcasted_iota(jnp.int32, (8, 128), 0) >= own
    for a in range(WIN):
        row = main[0, SHIFT + a] if a < own else halo[step, a - own].astype(F32)
        for s in range(slabs):
            line[s, a, 8 : 8 + columns, :] = row[:, s * 128 : s * 128 + 128]
    for a in range(WIN):
        for s in range(slabs):
            front = line[s, a, 8 - own : 16 - own, :]
            for w in range(wide):
                first = 8 + w * WIN + SHIFT
                tile = jnp.where(wrapped_row & (w == last), front, line[s, a, first : first + 8, :])
                target[w * CELLS + a * 8 : w * CELLS + a * 8 + 8, s * 128 : s * 128 + 128] = tile


def from_windows(line, width, source, main, halo, step):
    slabs, columns = C // 128, main.shape[2]
    wide, own = columns // WIN, WIN - SHIFT
    for w in range(wide):
        for a in range(WIN):
            for s in range(slabs):
                first = 8 + w * WIN + SHIFT
                line[s, a, first : first + 8, :] = source[
                    w * CELLS + a * 8 : w * CELLS + a * 8 + 8, s * 128 : s * 128 + 128
                ]
    kept = lax.broadcasted_iota(jnp.int32, (columns, 128), 0) < width
    front = lax.broadcasted_iota(jnp.int32, (8, 128), 0) < SHIFT
    for a in range(WIN):
        for s in range(slabs):
            wrapped = line[s, a, pl.ds(width + 8, 8), :]
            line[s, a, 8:16, :] = jnp.where(front, wrapped, line[s, a, 8:16, :])
            row = jnp.where(kept, line[s, a, 8 : 8 + columns, :], 0.0)
            if a < own:
                main[0, a, :, s * 128 : s * 128 + 128] = row
            else:
                halo[step, a - own, :, s * 128 : s * 128 + 128] = row.astype(BF16)


def place_onehot(row):
    shape = (128, HEADS * LANES)
    source = lax.broadcasted_iota(jnp.int32, shape, 0)
    lane = lax.broadcasted_iota(jnp.int32, shape, 1)
    return (lane == source // 8 * LANES + row * 8 + source % 8).astype(F32).astype(BF16)


def offset_onehot(column):
    shape = (256, 128)
    source = lax.broadcasted_iota(jnp.int32, shape, 0)
    lane = lax.broadcasted_iota(jnp.int32, shape, 1)
    wanted = (lane % 8 - column + WIN - 1) * HEADS + lane // 8
    return ((source == wanted) & (lane < HEADS * 8)).astype(F32).astype(BF16)


SPAN = 2 * WIN - 1


def build_bias(raw, last_strip, offsets, spread, bias):
    flat = jnp.concatenate([raw[r : r + 1] for r in range(TABLE_ROWS)], axis=1)
    offsets[...] = jnp.zeros_like(offsets)
    spread[...] = jnp.zeros_like(spread)
    for d in range(SPAN):
        offsets[SPAN - 1 - d : SPAN - d, 0 : SPAN * HEADS] = flat[:, d * SPAN * HEADS : (d + 1) * SPAN * HEADS]
    terms = split_three(offsets[...])
    for column in range(WIN):
        pick = offset_onehot(column)
        part = nn(terms[0], pick) + nn(terms[1], pick) + nn(terms[2], pick)
        spread[pl.ds(column, SPAN, stride=8), :] = part[0:SPAN]
    terms = split_three(spread[...])
    total = jnp.zeros((CELLS, HEADS * LANES), F32)
    for row in range(WIN):
        pick = place_onehot(row)
        for term in terms:
            total = total + nn(term[8 * (WIN - 1 - row) : 8 * (WIN - 1 - row) + CELLS], pick)
    shape = (CELLS, HEADS * LANES)
    key = lax.broadcasted_iota(jnp.int32, shape, 0)
    query = lax.broadcasted_iota(jnp.int32, shape, 1) % LANES
    edge = WIN - SHIFT
    by_row = ((key // 8 >= edge) != (query // 8 >= edge)) & last_strip
    by_col = (key % 8 >= edge) != (query % 8 >= edge)
    for variant, masked in enumerate((by_row, by_row | by_col)):
        value = (total + jnp.where(masked, MASK_FILL, 0.0)) * LOG2E
        value = jnp.where(key % 8 < WIN, value, -1e30)
        for g in range(GROUPS):
            bias[variant, g] = value[:, g * GROUP_HEADS * LANES : (g + 1) * GROUP_HEADS * LANES]


def pull_bias(sums, spread):
    grads = jnp.concatenate([sums[g] for g in range(GROUPS)], axis=1)
    high, middle, _ = split_three(grads)
    spread[...] = jnp.zeros_like(spread)
    for row in range(WIN):
        pick = place_onehot(row)
        first = 8 * (WIN - 1 - row)
        spread[first : first + CELLS, :] += nt(high, pick) + nt(middle, pick)
    total = jnp.zeros((SPAN, 256), F32)
    for column in range(WIN):
        pick = offset_onehot(column)
        high, middle, _ = split_three(spread[pl.ds(column, SPAN, stride=8), :])
        total = total + nt(high, pick) + nt(middle, pick)
    flat = [total[SPAN - 1 - d : SPAN - d, 0 : SPAN * HEADS] for d in range(SPAN)]
    flat.append(jnp.zeros((1, TABLE_ROWS * 128 - SPAN * SPAN * HEADS), F32))
    flat = jnp.concatenate(flat, axis=1)
    return jnp.concatenate([flat[:, r * 128 : r * 128 + 128] for r in range(TABLE_ROWS)], axis=0)


def rank_rows(me, owner_ref, rank_ref, start_ref):
    blocks = owner_ref.shape[0]
    mine = (owner_ref[...] == me).astype(F32)
    low = mine.astype(BF16)
    row = lax.broadcasted_iota(jnp.int32, (128, 128), 0)
    col = lax.broadcasted_iota(jnp.int32, (128, 128), 1)
    within = nn(low, (row <= col).astype(F32).astype(BF16))
    sums = nn(low, jnp.ones((128, 128), BF16))
    below = lax.broadcasted_iota(jnp.int32, (blocks, blocks), 1) < lax.broadcasted_iota(jnp.int32, (blocks, blocks), 0)
    start = nn(below.astype(F32).astype(BF16), sums.astype(BF16))
    rank_ref[...] = jnp.where(mine > 0, within - 1.0, -1.0)
    start_ref[...] = start.astype(jnp.int32)


def spread_rows(first, slabs, rows, target, offset, rank_ref, start_s, padded, packed):
    slot = lax.broadcasted_iota(jnp.int32, (128, 128), 0).astype(F32)

    def block(b, _):
        at = first // 128 + b
        hot = (slot == rank_ref[pl.ds(at, 1), :]).astype(F32).astype(BF16)
        begin = jnp.clip(start_s[at, 0], 0, padded.shape[0] - 128)
        held = padded[pl.ds(begin, 128), :].astype(BF16)
        packed[pl.ds(pl.multiple_of(b * 128, 128), 128), :] = tn(hot, held)
        return 0

    count = slabs * rows // 128
    lax.fori_loop(0, count, block, 0, unroll=3 if count % 3 == 0 else 1)
    for j in range(slabs):
        target[offset + j * rows : offset + (j + 1) * rows, :] = packed[pl.ds(j, rows, stride=slabs), :].astype(BF16)


def spread_small(target, rank_ref, start_s, padded):
    slot = lax.broadcasted_iota(jnp.int32, (128, 128), 0).astype(F32)
    small = SMALL_START // 128
    hot = (slot == rank_ref[small : small + 1, :]).astype(F32).astype(BF16)
    begin = jnp.clip(start_s[small, 0], 0, padded.shape[0] - 128)
    for i, piece in enumerate(split_three(padded[pl.ds(begin, 128), :])):
        first = FIRST_ROWS + i * SMALL_SPAN
        target[first : first + SMALL_SPAN, :] = tn(hot, piece)[0:SMALL_SPAN].astype(BF16)
    used = FIRST_ROWS + 3 * SMALL_SPAN
    target[used:, :] = jnp.zeros((target.shape[0] - used, 128), BF16)


def block_kernel(
    strips, buckets, images, plan_one, plan_two,
    cols_ref, keep_ref, x_ref, dy_ref, x_any, dy_any, owner_ref, master_ref,
    out_ref, gx_ref, rank_ref, start_ref, outh_any, gxh_any, gone_any, gtwo_any,
    wq_ref, wp_ref, wu_ref, wd_ref, bq_ref, bp_ref, bu_ref, bd_ref, g1_ref, b1_ref, g2_ref, b2_ref,
    gwq_ref, gwp_ref, gwu_ref, gwdt_ref, gbq_ref, gbp_ref, gbu_ref, gbd_ref, gg1_ref, gb1_ref, gg2_ref, gb2_ref,
    bias, gs_ref, offsets, spread,
    xw, zs, qkv, prob, ctx, gctx, gx1s,
    line, dyw, x1s, n2s, h2s, gfs, ys, gh2s, resw, htr, gtr, gscores, gqkv,
    fetched, halo_out, halo_in, back_in, wire_one, wire_two, padded, packed, start_s,
    local_sems, send_sems, recv_sems, *scratch,
):
    step = pl.program_id(0)
    tokens = dyw.shape[0]
    wide = tokens // CELLS
    place = Place(strips, buckets)
    last = cols_ref[0] - 1
    width = cols_ref[0] * WIN
    count_one = len(reduce_scratch(plan_one))
    parts_one = reduce_stages(place, plan_one, wire_one, scratch[:count_one])
    parts_two = reduce_stages(place, plan_two, wire_two, scratch[count_one:])
    gather_ticks = reduce_ticks(parts_one + [[]] * (4 - len(parts_one)) + parts_two)
    early = len(parts_one[0])
    one_ticks, two_ticks = reduce_ticks(parts_one), reduce_ticks(parts_two)

    def halo(kind, image):
        return pltpu.make_async_remote_copy(
            src_ref=halo_out.at[kind % 2, image], dst_ref=(halo_in if kind < 2 else back_in).at[kind % 2, image],
            send_sem=send_sems.at[kind, image], recv_sem=recv_sems.at[kind, image],
            device_id=place.above if kind < 2 else place.below, device_id_type=pl.DeviceIdType.MESH,
        )

    def fetch(array, image, kind):
        return pltpu.make_async_copy(array.at[image, pl.ds(0, SHIFT)], fetched.at[kind], local_sems.at[kind])

    def send_rows(kind, image, held):
        halo_out[kind, image] = fetched[held].astype(BF16)
        halo(kind, image).start()

    @pl.when(step == 0)
    def _():
        first = [fetch(x_any, image, image) for image in range(2)]
        for copy in first:
            copy.start()
        me = lax.axis_index("strip") * buckets + lax.axis_index("bucket")
        rank_rows(me, owner_ref, rank_ref, start_ref)
        starts = pltpu.make_async_copy(start_ref, start_s, local_sems.at[2])
        starts.start()
        capacity = master_ref.shape[0]
        padded[0:capacity, :] = master_ref[...]
        padded[capacity:, :] = jnp.zeros((padded.shape[0] - capacity, 128), F32)
        starts.wait()
        plans = slab_plan()
        spread_rows(*plans[0], wire_one, 0, rank_ref, start_s, padded, packed)
        spread_small(wire_one, rank_ref, start_s, padded)
        place.greet(True)
        gather_ticks[0]()
        for image in range(2):
            first[image].wait()
            send_rows(0, image, image)
        fetch(x_any, 2, 0).start()
        fetch(dy_any, 0, 1).start()
        for plan in plans[1:3]:
            spread_rows(*plan, wire_two, plan[0] - FIRST_ROWS, rank_ref, start_s, padded, packed)
        gather_ticks[1]()
        spread_rows(*plans[3], wire_two, plans[3][0] - FIRST_ROWS, rank_ref, start_s, padded, packed)
        used = SMALL_START - FIRST_ROWS
        wire_two[used:, :] = jnp.zeros((wire_two.shape[0] - used, 128), BF16)
        gather_ticks[2]()
        line[...] = jnp.zeros_like(line)
        for ref in (gwq_ref, gwp_ref, gwu_ref, gwdt_ref, gbq_ref, gbp_ref, gbu_ref, gbd_ref,
                    gg1_ref, gb1_ref, gg2_ref, gb2_ref, gs_ref, qkv, gctx):
            ref[...] = jnp.zeros_like(ref)
        for tick in gather_ticks[3:early]:
            tick()
        load_matrix(wq_ref, wire_one, 0, C)
        load_vectors((bq_ref, bp_ref, bu_ref, bd_ref, g1_ref, b1_ref, g2_ref, b2_ref), wire_one,
                     (0, 9, 12, 24, 27, 30, 33, 36))
        raw = jnp.zeros((SMALL_SPAN, 128), F32)
        for i in range(3):
            raw = raw + wire_one[FIRST_ROWS + i * SMALL_SPAN : FIRST_ROWS + (i + 1) * SMALL_SPAN, :].astype(F32)
        build_bias(raw[SMALL_ROWS : SMALL_ROWS + TABLE_ROWS], lax.axis_index("strip") == strips - 1, offsets, spread, bias)

    @pl.when((step > 0) & (step + 1 < images))
    def _():
        fetch(x_any, step + 1, 0).wait()
        send_rows(0, step + 1, 0)

    @pl.when((step > 0) & (step + 2 < images))
    def _():
        fetch(x_any, step + 2, 0).start()

    @pl.when((step > 0) & (step - 1 < images))
    def _():
        fetch(dy_any, step - 1, 1).wait()
        send_rows(1, step - 1, 1)

    @pl.when((step > 0) & (step < images))
    def _():
        fetch(dy_any, step, 1).start()

    bits = head_bits()

    def attend(image):
        at = lax.rem(image, LAG)
        halo(0, image).wait_recv()
        to_windows(line, last, x_ref, halo_in.at[0], image, xw.at[at])
        normal, _ = row_norm(xw[at])
        zs[at] = (normal * g1_ref[...] + b1_ref[...]).astype(BF16)
        triple = nn(zs[at], wq_ref[...]) + bq_ref[...]
        for w in range(wide):
            qkv[at, w, 0:CELLS, :] = triple[w * CELLS : w * CELLS + CELLS].astype(BF16)
        for w in range(wide):
            variant = (w == last).astype(jnp.int32)
            for g in range(GROUPS):
                q = qkv[at, w, :, g * 128 : g * 128 + 128]
                k = qkv[at, w, 0:CELLS, C + g * 128 : C + g * 128 + 128]
                v = qkv[at, w, 0:CELLS, 2 * C + g * 128 : 2 * C + g * 128 + 128]
                s = nt(k, stack_of(q, bits)) * (HD ** (-0.5) * LOG2E) + bias[variant, g]
                e = jnp.exp2(s - jnp.max(s, axis=0, keepdims=True))
                a = (e * (1.0 / jnp.sum(e, axis=0, keepdims=True))).astype(BF16)
                prob[at, w, g] = a
                resw[w * CELLS : w * CELLS + CELLS, g * 128 : g * 128 + 128] = unstack(tn(a, v))
        ctx[at] = resw[...].astype(BF16)

    def feed(image):
        at = lax.rem(image, LAG)
        keep = keep_ref[pl.ds(image, 1), :].astype(F32) * (1.0 / KEEP_PROB)
        keep_one = keep[:, 0:1]
        keep_two = keep[:, 1:2]
        x1 = xw[at] + keep_one * (nn(ctx[at], wp_ref[...]) + bp_ref[...])
        x1s[...] = x1
        normal, scale_two = row_norm(x1)
        n2s[...] = normal
        h2 = (normal * g2_ref[...] + b2_ref[...]).astype(BF16)
        h2s[...] = h2
        htr[...] = h2.astype(F32).T.astype(BF16)

        halo(1, image).wait_recv()
        to_windows(line, last, dy_ref, halo_in.at[1], image, dyw)
        token = lax.broadcasted_iota(jnp.int32, (tokens, 1), 0)
        valid = ((token % 8 < WIN) & (token < cols_ref[0] * CELLS)).astype(F32)
        gy = dyw[...] * valid
        gf = (gy * keep_two).astype(BF16)
        gfs[...] = gf
        gbd_ref[...] += column_sum(gf.astype(F32))
        gtr[...] = gf.astype(F32).T.astype(BF16)
        ys[...] = jnp.zeros_like(ys)
        gh2s[...] = jnp.zeros_like(gh2s)
        chunk = 512
        for j in range(FF // chunk):
            part = slice(j * chunk, (j + 1) * chunk)
            u = nn(h2s[...], wu_ref[:, part]) + bu_ref[:, part]
            gm = nt(gfs[...], wd_ref[part, :])
            m, slope = gelu_pair(u)
            m = m.astype(BF16)
            gu = (gm * slope).astype(BF16)
            ys[...] += nn(m, wd_ref[part, :])
            gwdt_ref[:, part] += nn(gtr[...], m)
            gwu_ref[:, part] += nn(htr[...], gu)
            gbu_ref[:, part] += column_sum(gu.astype(F32))
            gh2s[...] += nt(gu, wu_ref[:, part])

        resw[...] = (x1s[...] + keep_two * (ys[...] + bd_ref[...])) * valid
        halo(1, image).wait_send()
        from_windows(line, width, resw, out_ref, halo_out.at[1], image)
        halo(3, image).start()

        gh2 = gh2s[...]
        gg2_ref[...] += column_sum(gh2 * n2s[...])
        gb2_ref[...] += column_sum(gh2)
        gx1 = dyw[...] * valid + norm_pull(gh2 * g2_ref[...], n2s[...], scale_two)
        gx1s[at] = gx1
        ga = (keep_one * gx1).astype(BF16)
        gbp_ref[...] += column_sum(ga.astype(F32))
        gwp_ref[...] += nn(ctx[at].astype(F32).T.astype(BF16), ga)
        gc = nt(ga, wp_ref[...])
        for w in range(wide):
            gctx[at, w, 0:CELLS, :] = gc[w * CELLS : w * CELLS + CELLS].astype(BF16)

    def pull(image):
        at = lax.rem(image, LAG)
        scale = HD ** (-0.5)
        for w in range(wide):
            rows = slice(w * CELLS, w * CELLS + CELLS)
            for g in range(GROUPS):
                v = qkv[at, w, 0:CELLS, 2 * C + g * 128 : 2 * C + g * 128 + 128]
                gstack = stack_of(gctx[at, w, :, g * 128 : g * 128 + 128], bits)
                low = prob[at, w, g]
                a = low.astype(F32)
                grad = nt(v, gstack)
                inner = jnp.sum(grad * a, axis=0, keepdims=True)
                gscores[w, g] = a * (grad - inner)
                gqkv[rows, 2 * C + g * 128 : 2 * C + g * 128 + 128] = nn(low, gstack)
        for w in range(wide):
            rows = slice(w * CELLS, w * CELLS + CELLS)
            for g in range(GROUPS):
                q = qkv[at, w, :, g * 128 : g * 128 + 128]
                k = qkv[at, w, 0:CELLS, C + g * 128 : C + g * 128 + 128]
                gs = gscores[w, g].astype(BF16)
                gqkv[rows, g * 128 : g * 128 + 128] = unstack(tn(gs, k)) * scale
                gqkv[rows, C + g * 128 : C + g * 128 + 128] = nn(gs, stack_of(q, bits)) * scale
        gs_ref[...] += jnp.sum(gscores[...], axis=0)

        gtriple = gqkv[...].astype(BF16)
        gbq_ref[...] += column_sum(gtriple.astype(F32))
        gwq_ref[...] += nn(zs[at].astype(F32).T.astype(BF16), gtriple)
        gz = nt(gtriple, wq_ref[...]).astype(BF16).astype(F32)
        normal, scale_one = row_norm(xw[at])
        gg1_ref[...] += column_sum(gz * normal)
        gb1_ref[...] += column_sum(gz)
        resw[...] = gx1s[at] + norm_pull(gz * g1_ref[...], normal, scale_one)
        halo(0, image).wait_send()
        from_windows(line, width, resw, gx_ref, halo_out.at[0], image)
        halo(2, image).start()

    def pack_two():
        first = 0
        for grad in (gwp_ref, gwu_ref):
            for j in range(grad.shape[1] // 128):
                wire_two[first : first + C, :] = grad[:, j * 128 : j * 128 + 128].astype(BF16)
                first += C
        for j in range(C // 128):
            wire_two[first : first + FF, :] = gwdt_ref[j * 128 : j * 128 + 128, :].T.astype(BF16)
            first += FF
        wire_two[first:, :] = jnp.zeros((wire_two.shape[0] - first, 128), BF16)

    def pack_one():
        for j in range(3 * C // 128):
            wire_one[j * C : (j + 1) * C, :] = gwq_ref[:, j * 128 : j * 128 + 128].astype(BF16)
        vectors = (gbq_ref, gbp_ref, gbu_ref, gbd_ref, gg1_ref, gb1_ref, gg2_ref, gb2_ref)
        pieces = [ref[:, j * 128 : j * 128 + 128] for ref in vectors for j in range(ref.shape[1] // 128)]
        pieces.append(pull_bias(gs_ref, spread))
        pieces.append(jnp.zeros((wire_one.shape[0] - FIRST_ROWS - SMALL_ROWS - TABLE_ROWS, 128), F32))
        wire_one[FIRST_ROWS:, :] = jnp.concatenate(pieces, axis=0).astype(BF16)

    @pl.when(step == LAG)
    def _():
        first = 0
        for ref, rows in ((wp_ref, C), (wu_ref, C), (wd_ref, FF)):
            load_matrix(ref, wire_two, first, rows)
            first += ref.shape[1] // 128 * rows

    @pl.when((step >= LAG) & (step < images + LAG))
    def _():
        feed(step - LAG)

    @pl.when((step >= LAG) & (step < images))
    def _():
        pull(step - LAG)

    @pl.when(step < images)
    def _():
        attend(step)

    late = gather_ticks[early:]
    for k in range(LAG):
        mine = late[k * len(late) // LAG : (k + 1) * len(late) // LAG]

        @pl.when(step == k)
        def _(mine=mine):
            for tick in mine:
                tick()

    @pl.when(step == images + LAG - 1)
    def _():
        pack_two()
        two_ticks[0]()

    for k in range(LAG):

        @pl.when(step == images + LAG + k)
        def _(k=k):
            two_ticks[k + 1]()
            pull(images - LAG + k)

    @pl.when(step == images + 2 * LAG - 1)
    def _():
        pack_one()
        rest = two_ticks[LAG + 1 :]
        for i in range(max(len(rest), len(one_ticks))):
            for ticks in (one_ticks, rest):
                if i < len(ticks):
                    ticks[i]()
        for image in range(images):
            for kind in range(2, 4):
                halo(kind, image).wait()
        stores = [
            pltpu.make_async_copy(source, target, local_sems.at[i])
            for i, (source, target) in enumerate(
                ((wire_one, gone_any), (wire_two, gtwo_any), (back_in.at[0], gxh_any), (back_in.at[1], outh_any))
            )
        ]
        for copy in stores:
            copy.start()
        for copy in stores:
            copy.wait()


SMEM_SPEC = pl.BlockSpec(memory_space=pltpu.SMEM)
HBM_SPEC = pl.BlockSpec(memory_space=pl.ANY)


def whole(shape):
    return pl.BlockSpec(shape, lambda i: (0,) * len(shape))


def run_block(cols, keep, x, dy, owners, master, one_rows, two_rows, strips, buckets):
    samples, rows, columns, _ = x.shape
    wide = columns // WIN
    tokens = wide * CELLS
    own = rows - SHIFT
    halo = (samples, SHIFT, columns, C)
    plan_one = reduce_plan(strips, buckets, one_rows, ORDERS[:2])
    plan_two = reduce_plan(strips, buckets, two_rows, ORDERS)
    top = samples - 1

    def attended(i):
        return (jnp.minimum(i, top), 0, 0, 0)

    def fed(i):
        return (jnp.minimum(jnp.maximum(i - LAG, 0), top), 0, 0, 0)

    def pulled(i):
        early = jnp.minimum(jnp.maximum(i - LAG, 0), top - LAG)
        return (early + jnp.maximum(i - (samples + LAG) + 1, 0), 0, 0, 0)

    vectors = [3 * C, C, FF, C, C, C, C, C]
    sums = (GROUPS, CELLS, GROUP_HEADS * LANES)

    def struct(shape, dtype=F32):
        return jax.ShapeDtypeStruct(shape, dtype)

    token = pltpu.VMEM((tokens, C), F32)
    low = pltpu.VMEM((tokens, C), BF16)
    turned = pltpu.VMEM((C, tokens), BF16)
    scratch = [pltpu.VMEM(s, BF16) for s in ((C, 3 * C), (C, C), (C, FF), (FF, C))]
    scratch += [pltpu.VMEM((1, size), F32) for size in vectors]
    scratch += [pltpu.VMEM(s, F32) for s in ((C, 3 * C), (C, C), (C, FF), (C, FF))]
    scratch += [pltpu.VMEM((1, size), F32) for size in vectors]
    scratch += [
        pltpu.VMEM((2,) + sums, F32), pltpu.VMEM(sums, F32),
        pltpu.VMEM((16, 256), F32), pltpu.VMEM((SPAN * 8, 128), F32),
        pltpu.VMEM((LAG, tokens, C), F32), pltpu.VMEM((LAG, tokens, C), BF16),
        pltpu.VMEM((LAG, wide, LANES, 3 * C), BF16), pltpu.VMEM((LAG, wide) + sums, BF16),
        pltpu.VMEM((LAG, tokens, C), BF16), pltpu.VMEM((LAG, wide, LANES, C), BF16),
        pltpu.VMEM((LAG, tokens, C), F32),
        pltpu.VMEM((C // 128, WIN, columns + 16, 128), F32),
        token, token, token, low, low, token, token, token, turned, turned,
        pltpu.VMEM((wide,) + sums, F32), pltpu.VMEM((tokens, 3 * C), F32),
        pltpu.VMEM((2,) + halo[1:], F32),
        pltpu.VMEM((2,) + halo, BF16), pltpu.VMEM((2,) + halo, BF16), pltpu.VMEM((2,) + halo, BF16),
        pltpu.VMEM((one_rows, 128), BF16), pltpu.VMEM((two_rows, 128), BF16),
        pltpu.VMEM((-(-(master.shape[0] + 128) // 8) * 8, 128), F32), pltpu.VMEM((C * FF // 128, 128), F32),
        pltpu.SMEM(owners.shape, jnp.int32),
        pltpu.SemaphoreType.DMA((4,)), pltpu.SemaphoreType.DMA((4, samples)), pltpu.SemaphoreType.DMA((4, samples)),
    ]
    block = (1, rows, columns, C)
    part = (1, own, columns, C)
    return pl.pallas_call(
        lambda *refs: block_kernel(strips, buckets, samples, plan_one, plan_two, *refs),
        grid=(samples + 2 * LAG,),
        in_specs=[SMEM_SPEC, whole(keep.shape), pl.BlockSpec(block, attended), pl.BlockSpec(block, fed)] + [HBM_SPEC] * 2
        + [whole(owners.shape), whole(master.shape)],
        out_specs=[pl.BlockSpec(part, fed), pl.BlockSpec(part, pulled)] + [whole(owners.shape)] * 2 + [HBM_SPEC] * 4,
        out_shape=[struct((samples, own, columns, C)), struct((samples, own, columns, C)), struct(owners.shape),
                   struct(owners.shape, jnp.int32), struct(halo, BF16), struct(halo, BF16), struct((one_rows, 128), BF16),
                   struct((two_rows, 128), BF16)],
        scratch_shapes=scratch + reduce_scratch(plan_one) + reduce_scratch(plan_two),
        compiler_params=pltpu.CompilerParams(
            vmem_limit_bytes=62 * 1024 * 1024, collective_id=1, has_side_effects=True
        ),
        name="block",
    )(cols, keep, x, dy, x, dy, owners, master)


def collect_kernel(
    start_ref, rank_ref, one_any, two_any, master_ref, first_ref, second_ref, outh_any, gxh_any, out_any, gx_any,
    first_out, second_out, master_out, out_final, gx_final, packed, total, wide, one, two, halos, sems,
):
    own = out_any.shape[1]
    pairs = [(one_any, one), (two_any, two), (outh_any, halos.at[0]), (gxh_any, halos.at[1])]
    pairs += [(main, wide.at[i, :, pl.ds(SHIFT, own)]) for i, main in enumerate((out_any, gx_any))]
    loads = [pltpu.make_async_copy(source, target, sems.at[i]) for i, (source, target) in enumerate(pairs)]
    stores = [pltpu.make_async_copy(wide.at[i], final, sems.at[6 + i]) for i, final in enumerate((out_final, gx_final))]
    for load in loads:
        load.start()
    capacity = master_ref.shape[0]
    total[...] = jnp.zeros_like(total)
    slot = lax.broadcasted_iota(jnp.int32, (128, 128), 0).astype(F32)

    def block(b, _):
        hot = (slot == rank_ref[pl.ds(b, 1), :]).astype(F32).astype(BF16)
        part = nn(hot, packed[pl.ds(pl.multiple_of(b * 128, 128), 128), :].astype(BF16))
        where = pl.ds(start_ref[b, 0], 128)
        total[where, :] = total[where, :] + part
        return 0

    def unpack(plan, source, offset):
        first, slabs, rows = plan
        for j in range(slabs):
            packed[pl.ds(first + j, rows, stride=slabs), :] = source[
                first - offset + j * rows : first - offset + (j + 1) * rows, :
            ].astype(F32)

    plans = slab_plan()
    small = SMALL_START // 128
    loads[0].wait()
    unpack(plans[0], one, 0)
    packed[SMALL_START : SMALL_START + SMALL_SPAN, :] = one[FIRST_ROWS : FIRST_ROWS + SMALL_SPAN, :].astype(F32)
    packed[SMALL_START + SMALL_SPAN : SMALL_START + 128, :] = jnp.zeros((128 - SMALL_SPAN, 128), F32)
    lax.fori_loop(0, FIRST_ROWS // 128, block, 0, unroll=9)
    for i in range(2):
        loads[2 + i].wait()
        wide[i, :, 0:SHIFT] = halos[i].astype(F32)
        loads[4 + i].wait()
        stores[i].start()
    loads[1].wait()
    for plan in plans[1:]:
        unpack(plan, two, FIRST_ROWS)
    lax.fori_loop(FIRST_ROWS // 128, small, block, 0, unroll=9)
    block(small, 0)
    slots = lax.broadcasted_iota(jnp.int32, (capacity, 1), 0)
    edges = [edge // 128 for edge in row_edges()[:4]] + [SMALL_START // 128 + 1]
    rates = [2.0 / math.sqrt(C), 2.0 / math.sqrt(C // 8), 2.0 / math.sqrt(C), 2.0 / math.sqrt(FF), 1.0, 0.0]
    rate = jnp.full((capacity, 1), rates[0], F32)
    for edge, amount in zip(edges, rates[1:]):
        rate = jnp.where(slots >= start_ref[edge, 0], amount, rate)
    decay = jnp.where(slots < start_ref[edges[3], 0], DECAY, 0.0)
    grads = total[0:capacity, :]
    weights = master_ref[...]
    first = BETA_ONE * first_ref[...] + (1.0 - BETA_ONE) * grads
    second = BETA_TWO * second_ref[...] + (1.0 - BETA_TWO) * grads * grads
    first_out[...] = first
    second_out[...] = second
    first_hat = first / (1.0 - BETA_ONE**STEP)
    second_hat = second / (1.0 - BETA_TWO**STEP)
    master_out[...] = weights - rate * (first_hat / (jnp.sqrt(second_hat) + ADAM_EPS) + decay * weights)
    for store in stores:
        store.wait()


def run_collect(starts, ranks, one, two, master, first, second, outh, gxh, out, gx):
    vmem = pl.BlockSpec(memory_space=pltpu.VMEM)
    samples, own, columns, channels = out.shape
    final = jax.ShapeDtypeStruct((samples, own + SHIFT, columns, channels), F32)
    return pl.pallas_call(
        collect_kernel,
        in_specs=[SMEM_SPEC, vmem, HBM_SPEC, HBM_SPEC] + [vmem] * 3 + [HBM_SPEC] * 4,
        out_specs=[vmem] * 3 + [HBM_SPEC] * 2,
        out_shape=[jax.ShapeDtypeStruct(master.shape, F32)] * 3 + [final, final],
        scratch_shapes=[
            pltpu.VMEM((SMALL_START + 128, 128), F32),
            pltpu.VMEM((-(-(master.shape[0] + 128) // 8) * 8, 128), F32),
            pltpu.VMEM((2,) + final.shape, F32),
            pltpu.VMEM(one.shape, BF16),
            pltpu.VMEM(two.shape, BF16),
            pltpu.VMEM((2,) + outh.shape, BF16),
            pltpu.SemaphoreType.DMA((8,)),
        ],
        compiler_params=pltpu.CompilerParams(vmem_limit_bytes=62 * 1024 * 1024),
        name="collect",
    )(starts, ranks, one, two, master, first, second, outh, gxh, out, gx)


def shards(
    block_input, cotangent, window_cols, keep_mask, owner_list, master, first_moment, second_moment
):
    strips = lax.axis_size("strip")
    buckets = lax.axis_size("bucket")
    blocks = -(-(SMALL_START // 128 + 2) // 8) * 8
    owners = jnp.pad(owner_list, (0, blocks * 128 - owner_list.shape[0]), constant_values=-1).reshape(blocks, 128)
    one_rows = wire_rows(FIRST_ROWS + 3 * SMALL_SPAN, strips, buckets)
    two_rows = wire_rows(SMALL_START - FIRST_ROWS, strips, buckets)
    output, grad_input, ranks, starts, output_halo, grad_halo, gone, gtwo = run_block(
        window_cols, keep_mask, block_input, cotangent, owners, master, one_rows, two_rows, strips, buckets
    )
    first, second_new, new_weights, output, grad_input = run_collect(
        starts, ranks, gone, gtwo, master, first_moment, second_moment, output_halo, grad_halo, output, grad_input
    )
    return (output, grad_input, first, second_new, new_weights)


def solution(mesh):
    in_specs = (
        P("bucket", "strip", None, None),
        P("bucket", "strip", None, None),
        P("bucket"),
        P("bucket", None),
        P(),
        P(("strip", "bucket"), None),
        P(("strip", "bucket"), None),
        P(("strip", "bucket"), None),
    )
    out_specs = (
        P("bucket", "strip", None, None),
        P("bucket", "strip", None, None),
        P(("strip", "bucket"), None),
        P(("strip", "bucket"), None),
        P(("strip", "bucket"), None),
    )
    return jax.shard_map(shards, mesh=mesh, in_specs=in_specs, out_specs=out_specs, check_vma=False)
```
